128 devices in a mesh: expert: 8 (over x, core), ctx: 8 (over z_hi, y), dp: 2 (over z_lo).
Axes of the slice: x: 4, y: 4, z: 4 (z_hi: 2, z_lo: 2; z = z_hi * 2 + z_lo), core: 2. Of those that a mesh axis runs over, the one named last changes fastest.
Arguments:
- tokens: bfloat16 [16384, 1024], P(('expert', 'ctx', 'dp')), may hold values from -6 to 6
- norm_in: bfloat16 [1024], P('expert'), may hold values from 0.25 to 1.75
- w_query: bfloat16 [1024, 1024], P('expert'), may hold values from -0.1875 to 0.1875
- w_key: bfloat16 [1024, 512], P('expert'), may hold values from -0.1875 to 0.1875
- w_value: bfloat16 [1024, 512], P('expert'), may hold values from -0.1875 to 0.1875
- query_gain: bfloat16 [1024], P('expert'), may hold values from 0.25 to 1.75
- key_gain: bfloat16 [512], P('expert'), may hold values from 0.25 to 1.75
- w_out: bfloat16 [1024, 1024], P('expert'), may hold values from -4 to 4
- norm_mid: bfloat16 [1024], P('expert'), may hold values from 0.25 to 1.75
- w_router: bfloat16 [1024, 32], P('expert'), may hold values from -0.09375 to 0.09375
- expert_gate: bfloat16 [1024, 32, 512], P(('ctx', 'dp'), 'expert'), may hold values from -0.1875 to 0.1875
- expert_up: bfloat16 [1024, 32, 512], P(('ctx', 'dp'), 'expert'), may hold values from -0.1875 to 0.1875
- expert_down: bfloat16 [1024, 32, 512], P(('ctx', 'dp'), 'expert'), may hold values from -4 to 4
- routes: int32 [16384, 8], P(('expert', 'ctx', 'dp')), may hold values from 0 to 31, all different within a row; in each aligned block of 128 rows (0 to 127, 128 to 255, ...) at most 64 rows name the same one
- valid: int32 [16384], P(('expert', 'ctx', 'dp')), may hold values 0 or 1
- teacher: float32 [16384, 1024], P(('expert', 'ctx', 'dp')), may hold values from -18 to 18
Outputs:
- mixed: bfloat16 [16384, 1024], P(('expert', 'ctx', 'dp'))
- loss: float32 [], replicated
- grad_tokens: float32 [16384, 1024], P(('expert', 'ctx', 'dp'))
- grad_norm_in: float32 [1024], P('expert')
- grad_query: float32 [1024, 1024], P('expert')
- grad_key: float32 [1024, 512], P('expert')
- grad_value: float32 [1024, 512], P('expert')
- grad_query_gain: float32 [1024], P('expert')
- grad_key_gain: float32 [512], P('expert')
- grad_out: float32 [1024, 1024], P('expert')
- grad_norm_mid: float32 [1024], P('expert')
- grad_router: float32 [1024, 32], P('expert')
- grad_gate: float32 [1024, 32, 512], P(('ctx', 'dp'), 'expert')
- grad_up: float32 [1024, 32, 512], P(('ctx', 'dp'), 'expert')
- grad_down: float32 [1024, 32, 512], P(('ctx', 'dp'), 'expert')
The draws below stay inside these ranges and needn't reach their ends.
Inputs may be any that keep to these rules, and one draw needn't show every extreme that they name: `routes`: in each aligned block of 128 rows (the rows of one device) no expert is named by more than 64 rows, a bound that some block reaches; each row names 8 different experts.
All inputs are finite; a program needn't handle non-finite values. No bound on the sum of `valid` on one device may be relied on, other than what follows from the above.
Results may differ from the reference program's by a relative error of at most 0.023.
Values may be sent and summed in bfloat16 or wider, within the bound.
A program may use at most 128 MiB of HBM per device.

```python
import math
import jax
import jax.numpy as jnp
import numpy as np
from jax import lax

D = 1024
HEADS = 16
HEAD = 64
KV_HEADS = 8
FF = 512
TOP = 8
BLOCK = 256
TOK_DEV = 128
EXPERTS = 32
QW = 1024
KVW = 512
SEQ = 2048
TOKENS = 16384
CAP = 64
N_EXPERT = 8


def draw_teacher(key, part):
    key = jax.random.fold_in(key, 7)
    place = jnp.arange(TOKENS, dtype=jnp.float32) / float(max(TOKENS - 1, 1))
    values = jnp.clip(jax.random.normal(key, (TOKENS, D), jnp.float32), -6.0, 6.0)
    scale = 1.0 + 2.0 * place
    return (values * scale[:, None]).astype(jnp.float32)


def set_ends(array, own_key, least, largest):
    shape = array.shape
    index_at = [jax.random.randint(jax.random.fold_in(own_key, axis), (), 0, shape[axis]) for axis in range(len(shape))]
    array = array.at[tuple(index_at)].set(least)
    longest = shape.index(max(shape))
    index_at[longest] = (index_at[longest] + 1) % shape[longest]
    return array.at[tuple(index_at)].set(largest)


def steps_of(key, shape, shards, smallest, high):
    gain, own = 1.0, jax.random.fold_in(key, 6)
    for axis_at, blocks in shards:
        draws = jnp.exp(jax.random.uniform(jax.random.fold_in(own, axis_at), (blocks,), jnp.float32, smallest / len(shards), high / len(shards)))
        gain = gain * jnp.repeat(draws, shape[axis_at] // blocks).reshape([-1 if axis == axis_at else 1 for axis in range(len(shape))])
    return gain


def routed_block(stream_key, own, number, rows, amount, top, limit, skew):
    sequence = jax.random.permutation(stream_key, amount)
    heavy_load, common = shares(amount, rows * top, limit, skew, True), shares(amount, rows * top, limit, skew, False)
    places = jnp.arange(amount)

    def named(tallies, offset_by):
        used = int((tallies > 0).sum())
        fixed = max(1, used // 4)
        shifted = fixed + (places - fixed + offset_by * (used - fixed)) % max(1, amount - fixed)
        return jnp.zeros((amount,), jnp.int32).at[sequence[jnp.where(places < fixed, places, shifted)]].set(jnp.asarray(tallies, jnp.int32))

    tallies = jnp.where(number % 4 == 0, named(heavy_load, number // 4), named(common, number - number // 4 - 1))
    mixed = jax.random.permutation(jax.random.fold_in(own, 3), amount)
    donor, receiver = mixed[0:amount // 2 * 2:2], mixed[1:amount // 2 * 2:2]
    room = jnp.minimum(tallies[donor] - 1, limit - tallies[receiver]) // 2
    room = jnp.where((donor == sequence[0]) | (receiver == sequence[0]) | (tallies[receiver] == 0), 0, jnp.maximum(room, 0))
    shifted = jax.random.randint(jax.random.fold_in(own, 4), (amount // 2,), 0, 1 << 20) % (room + 1)
    tallies = tallies.at[donor].add(-shifted).at[receiver].add(shifted)
    members = jnp.searchsorted(jnp.cumsum(tallies), jnp.arange(rows * top), side="right").astype(jnp.int32)
    listing = members.reshape(top, rows).T
    listing = listing[jax.random.permutation(jax.random.fold_in(own, 1), rows)]
    offset_by = jax.random.randint(jax.random.fold_in(own, 2), (rows, 1), 0, top)
    return jnp.take_along_axis(listing, (jnp.arange(top)[None, :] + offset_by) % top, axis=1)


def shares(amount, total, limit, slope, full):
    portions = [(1 << 20) // math.isqrt(grade ** slope) + 1 for grade in range(1, amount + 1)]
    largest = limit if full else min(limit, max(-(-total // amount), total * portions[0] // sum(portions)))
    least = 1 if total - largest >= amount - 1 else 0
    given, spare = [largest] + [least] * (amount - 1), total - largest - least * (amount - 1)
    while spare > 0:
        movable = [i for i in range(1, amount) if given[i] < largest] or [i for i in range(1, amount) if given[i] < limit]
        whole, budget = sum([portions[i] for i in movable]), spare
        for i in movable:
            extra = min(limit - given[i], max(1, budget * portions[i] // whole), spare)
            given[i] = given[i] + extra
            spare = spare - extra
    return np.array(given)


def scatter_about(rng, shape, width, most, split=(), kind=jnp.bfloat16):
    values = jax.random.normal(rng, shape, jnp.float32) * width
    if len(split) > 0:
        values = steps_of(rng, shape, split, -0.22, 0.18) * values
    return jnp.clip(values, min=-most, max=most).astype(kind)


def setup_inputs(seed: int = 0) -> dict:
    seeds = jax.random.split(jax.random.key(seed), 17)
    tokens = scatter_about(seeds[0], (TOKENS, D), 1.0, 6.0, ((0, 128),))
    norm_in = jnp.clip(1.0 + 0.15 * jax.random.normal(seeds[1], (D,), jnp.float32), 0.25, 1.75).astype(jnp.bfloat16)
    w_query = scatter_about(seeds[2], (D, QW), D ** -0.5, 0.1875, ((0, 8),))
    w_key = scatter_about(seeds[3], (D, KVW), D ** -0.5, 0.1875, ((0, 8),))
    w_value = scatter_about(seeds[4], (D, KVW), D ** -0.5, 0.1875, ((0, 8),))
    query_gain = jnp.clip(1.0 + 0.15 * jax.random.normal(seeds[5], (QW,), jnp.float32), 0.25, 1.75).astype(jnp.bfloat16)
    key_gain = jnp.clip(1.0 + 0.15 * jax.random.normal(seeds[6], (KVW,), jnp.float32), 0.25, 1.75).astype(jnp.bfloat16)
    w_out = scatter_about(seeds[7], (QW, D), (max(1, 4 * QW // SEQ)) ** -0.5, 4.0, ((0, 8),))
    norm_mid = jnp.clip(1.0 + 0.15 * jax.random.normal(seeds[8], (D,), jnp.float32), 0.25, 1.75).astype(jnp.bfloat16)
    w_router = scatter_about(seeds[9], (D, EXPERTS), (4 * D) ** -0.5, 0.09375, ((0, 8),))
    expert_gate = scatter_about(seeds[10], (D, EXPERTS, FF), D ** -0.5, 0.1875, ((0, 16), (1, 8)))
    expert_up = scatter_about(seeds[11], (D, EXPERTS, FF), D ** -0.5, 0.1875, ((0, 16), (1, 8)))
    expert_down = scatter_about(seeds[12], (D, EXPERTS, FF), (max(1, FF // 256)) ** -0.5, 4.0, ((0, 16), (1, 8)))
    routes_keys = jax.random.split(jax.random.fold_in(seeds[13], 1), TOKENS // TOK_DEV)
    routes_turns = jax.random.permutation(jax.random.fold_in(seeds[13], 3), TOKENS // TOK_DEV)
    routes = jax.vmap(lambda own, number: routed_block(jax.random.fold_in(seeds[13], 2), own, number, TOK_DEV, EXPERTS, TOP, CAP, 1))(routes_keys, routes_turns).reshape((TOKENS, TOP))
    valid = set_ends((jax.random.randint(seeds[14], (TOKENS,), 0, 4) < 3).astype(jnp.int32), jax.random.fold_in(seeds[14], 1), 0, 1)
    teacher = draw_teacher(jax.random.fold_in(seeds[16], 71), 0)
    return {"tokens": tokens, "norm_in": norm_in, "w_query": w_query, "w_key": w_key, "w_value": w_value, "query_gain": query_gain, "key_gain": key_gain, "w_out": w_out, "norm_mid": norm_mid, "w_router": w_router, "expert_gate": expert_gate, "expert_up": expert_up, "expert_down": expert_down, "routes": routes, "valid": valid, "teacher": teacher}


EPS = 1e-06
THETA = 10000.0
NEG = -1e+30
HIGH = lax.Precision.HIGHEST

@jax.custom_vjp
def low(v):
    return lax.optimization_barrier(v.astype(jnp.bfloat16)).astype(jnp.float32)

@jax.custom_vjp
def low_back(v):
    return v

def low_keep(v):
    return (low(v), None)

def low_pass(kept, grad):
    return (grad,)

def back_keep(v):
    return (v, None)

def back_low(kept, grad):
    return (low(grad),)
low.defvjp(low_keep, low_pass)
low_back.defvjp(back_keep, back_low)

def rms_norm(values):
    return values * lax.rsqrt(lax.optimization_barrier(jnp.mean(values * values, axis=-1, keepdims=True)) + EPS)

def rope_tables(positions):
    half_head = HEAD // 2
    frequency = THETA ** (-(jnp.arange(half_head).astype(jnp.float32) * (2.0 / HEAD)))
    angles = positions.astype(jnp.float32)[:, None] * frequency[None, :]
    return (jnp.cos(angles), jnp.sin(angles))

def rotate(values, cosine, sine, head_count):
    count_rows = values.shape[0]
    shaped = values.reshape(count_rows, head_count, HEAD)
    half_head = HEAD // 2
    first_half = shaped[..., :half_head]
    second_half = shaped[..., half_head:]
    cos_rows = cosine[:, None, :]
    sin_rows = sine[:, None, :]
    turned = jnp.concatenate([first_half * cos_rows - second_half * sin_rows, second_half * cos_rows + first_half * sin_rows], axis=-1)
    return turned.reshape(count_rows, head_count * HEAD)

def attend_sequence(query_seq, key_seq, value_seq, keep_seq):
    group_size = HEADS // KV_HEADS
    query_grouped = query_seq.reshape(SEQ, KV_HEADS, group_size, HEAD)
    key_heads = key_seq.reshape(SEQ, KV_HEADS, HEAD)
    value_heads = value_seq.reshape(SEQ, KV_HEADS, HEAD)
    key_pos = jnp.arange(SEQ, dtype=jnp.int32)
    query_rows = min(512, SEQ)

    def one_block(row_start):
        query_part = lax.dynamic_slice_in_dim(query_grouped, row_start, query_rows, 0)
        query_pos = row_start + jnp.arange(query_rows, dtype=jnp.int32)
        scores = jnp.einsum('tkgd,skd->kgts', query_part, key_heads, precision=HIGH) * HEAD ** (-0.5)
        scores = low_back(scores)
        allowed = (key_pos[None, :] // BLOCK <= query_pos[:, None] // BLOCK) & ((keep_seq[None, :] > 0) | (key_pos[None, :] == query_pos[:, None]))
        scores = jnp.where(allowed[None, None], scores, NEG)
        weights = low(jax.nn.softmax(scores, axis=-1))
        result = jnp.einsum('kgts,skd->tkgd', weights, value_heads, precision=HIGH)
        return result.reshape(query_rows, QW)
    starts = (jnp.arange(SEQ // query_rows) * query_rows).astype(jnp.int32)
    pieces = lax.map(jax.checkpoint(one_block), starts)
    return pieces.reshape(SEQ, QW)

def expert_table(routes):
    sources = TOKENS // TOK_DEV
    flat_routes = routes.reshape(sources, TOK_DEV * TOP)
    picks = (flat_routes[:, :, None] == jnp.arange(EXPERTS, dtype=jnp.int32)[None, None, :]).astype(jnp.int32)
    slot_index = lax.optimization_barrier(jnp.sum((jnp.cumsum(picks, axis=1) - 1) * picks, axis=2)).astype(jnp.int32)
    source_ids = jnp.arange(sources, dtype=jnp.int32)[:, None]
    places = (flat_routes * (sources * CAP) + source_ids * CAP + slot_index).reshape(-1).astype(jnp.int32)
    entry_ids = jnp.arange(TOKENS * TOP, dtype=jnp.int32)
    table = jnp.full((EXPERTS * sources * CAP,), -1, jnp.int32).at[places].set(entry_ids)
    return table.reshape(EXPERTS, sources * CAP)

def reference(tokens, norm_in, w_query, w_key, w_value, query_gain, key_gain, w_out, norm_mid, w_router, expert_gate, expert_up, expert_down, routes, valid, teacher):
    table = expert_table(routes)
    valid_float = valid.astype(jnp.float32)[:, None]
    cosine, sine = rope_tables(jnp.arange(SEQ, dtype=jnp.int32))
    cos_all = jnp.tile(cosine, (N_EXPERT, 1))
    sin_all = jnp.tile(sine, (N_EXPERT, 1))

    def half_loss(token_vals, gain_in, query_w, key_w, value_w, qgain, kgain, out_w, gain_mid, router_w, gate_w, up_w, down_w):
        normed = low(rms_norm(token_vals) * gain_in)
        query_pre = low_back(jnp.dot(normed, query_w, precision=HIGH))
        key_pre = low_back(jnp.dot(normed, key_w, precision=HIGH))
        value_low = low(low_back(jnp.dot(normed, value_w, precision=HIGH)))
        query_low = low(rotate(rms_norm(query_pre) * qgain, cos_all, sin_all, HEADS))
        key_low = low(rotate(rms_norm(key_pre) * kgain, cos_all, sin_all, KV_HEADS))

        def one_sequence(pieces):
            return attend_sequence(pieces[0], pieces[1], pieces[2], pieces[3])
        attended = lax.map(one_sequence, (query_low.reshape(N_EXPERT, SEQ, QW), key_low.reshape(N_EXPERT, SEQ, KVW), value_low.reshape(N_EXPERT, SEQ, KVW), valid.reshape(N_EXPERT, SEQ)))
        attended = low(low_back(attended.reshape(TOKENS, QW)))
        residual = token_vals + low_back(jnp.dot(attended, out_w, precision=HIGH))
        mid_low = low(rms_norm(residual) * gain_mid)
        probs = jax.nn.softmax(jnp.dot(mid_low, router_w, precision=HIGH), axis=-1)
        gate_flat = jnp.take_along_axis(probs, routes, axis=1).reshape(-1)

        def expert_part(entries, gate_e, up_e, down_e):
            used = entries >= 0
            safe = jnp.where(used, entries, 0)
            rows_in = low_back(jnp.where(used[:, None], mid_low[safe // TOP], 0.0))
            gate_pre = low_back(jnp.dot(rows_in, gate_e, precision=HIGH))
            up_pre = low_back(jnp.dot(rows_in, up_e, precision=HIGH))
            act_low = low(jax.nn.silu(gate_pre) * up_pre)
            out_rows = low_back(low(jnp.dot(act_low, down_e.T, precision=HIGH)))
            return jnp.where(used, gate_flat[safe], 0.0)[:, None] * out_rows

        def add_expert(running, inputs):
            entries = inputs[0]
            contrib = jax.checkpoint(expert_part)(entries, inputs[1], inputs[2], inputs[3])
            target = jnp.where(entries >= 0, entries, 0) // TOP
            return (running.at[target].add(contrib), None)
        stacked = (table, jnp.transpose(gate_w, (1, 0, 2)), jnp.transpose(up_w, (1, 0, 2)), jnp.transpose(down_w, (1, 0, 2)))
        moe_sum, _ = lax.scan(add_expert, jnp.zeros_like(residual), stacked)
        out_vals = residual + moe_sum
        err = (out_vals - teacher) * valid_float
        return (0.5 * jnp.sum(err * err), out_vals)
    floats = (tokens.astype(jnp.float32), norm_in.astype(jnp.float32), w_query.astype(jnp.float32), w_key.astype(jnp.float32), w_value.astype(jnp.float32), query_gain.astype(jnp.float32), key_gain.astype(jnp.float32), w_out.astype(jnp.float32), norm_mid.astype(jnp.float32), w_router.astype(jnp.float32), expert_gate.astype(jnp.float32), expert_up.astype(jnp.float32), expert_down.astype(jnp.float32))
    half_sq, pullback, out_vals = jax.vjp(half_loss, floats[0], floats[1], floats[2], floats[3], floats[4], floats[5], floats[6], floats[7], floats[8], floats[9], floats[10], floats[11], floats[12], has_aux=True)
    grads = pullback(jnp.ones((), jnp.float32))
    count = jnp.sum(valid).astype(jnp.float32)
    loss = 2.0 * half_sq / (count * D)
    return (out_vals.astype(jnp.bfloat16), loss, grads[0], grads[1], grads[2], grads[3], grads[4], grads[5], grads[6], grads[7], grads[8], grads[9], grads[10], grads[11], grads[12])
```

```python
import jax
import jax.numpy as jnp
from jax import lax
from jax.experimental import pallas as pl
from jax.experimental.pallas import tpu as pltpu
from jax.sharding import PartitionSpec as P

MESH = pl.DeviceIdType.MESH
F32 = jnp.float32
BF16 = jnp.bfloat16

HEAD = 64
TOP = 8
EPS = 1e-06
THETA = 10000.0
NEG = -1e30
HIGH = lax.Precision.HIGHEST


def mm(a, b):
    return lax.dot_general(a, b, (((1,), (0,)), ((), ())), preferred_element_type=F32)


def mm_nt(a, b):
    return lax.dot_general(a, b, (((1,), (1,)), ((), ())), preferred_element_type=F32)


def mm_tn(a, b):
    return lax.dot_general(a, b, (((0,), (0,)), ((), ())), preferred_element_type=F32)


def places():
    e, c, d = lax.axis_index("expert"), lax.axis_index("ctx"), lax.axis_index("dp")
    return e // 2, e % 2, c, d


def remote(src, dst, send, recv, device):
    return pltpu.make_async_remote_copy(
        src_ref=src, dst_ref=dst, send_sem=send, recv_sem=recv, device_id=device, device_id_type=MESH
    )


def line_device(x, core):
    return (lax.rem(x + 4, 4) * 2 + core, lax.axis_index("ctx"), lax.axis_index("dp"))


def greet_line():
    barrier = pltpu.get_barrier_semaphore()
    e, c, d = lax.axis_index("expert"), lax.axis_index("ctx"), lax.axis_index("dp")
    for o in range(1, 8):
        pl.semaphore_signal(barrier, inc=1, device_id=(lax.rem(e + o, 8), c, d), device_id_type=MESH)
    pl.semaphore_wait(barrier, 7)


def line_gather_start(own, buf, send, recv):
    x, core, _, _ = places()
    me = x * 2 + core
    copies = [remote(own, buf(me), send.at[o], recv.at[o], line_device(x + o, core)) for o in (2, 1, 3)]
    copies.append(remote(own, buf(me), send.at[0], recv.at[0], line_device(x, 1 - core)))
    for copy in copies:
        copy.start()
    return copies


def line_gather_finish(copies, buf, send, recv):
    x, core, _, _ = places()
    forwards = []
    for at, o in ((1, 1), (2, 3), (0, 2)):
        copies[at].wait_recv()
        block = buf(lax.rem(x - o + 4, 4) * 2 + core)
        copy = remote(block, block, send.at[4 + o], recv.at[4 + o], line_device(x, 1 - core))
        copy.start()
        forwards.append(copy)
    copies[3].wait_recv()
    for copy in forwards:
        copy.wait_recv()
    for copy in copies + forwards:
        copy.wait_send()


def line_scatter_send_pair(pair, sib, send, recv):
    x, core, _, _ = places()
    copy = remote(pair, sib, send.at[0], recv.at[0], line_device(x, 1 - core))
    copy.start()
    return copy


def line_scatter_send_x(mine, pair_copy, sib, inbox, send, recv):
    x, core, _, _ = places()
    pair_copy.wait_recv()
    copies = []
    for o in (2, 1, 3):
        to = lax.rem(x + o, 4)
        mine[to] = (mine[to].astype(F32) + sib[to].astype(F32)).astype(mine.dtype)
        copy = remote(mine.at[to], inbox.at[o - 1], send.at[o], recv.at[o], line_device(x + o, core))
        copy.start()
        copies.append(copy)
    return copies


def line_scatter_sum(mine, sib, inbox, copies):
    x, _, _, _ = places()
    total = mine[x].astype(F32) + sib[x].astype(F32)
    for at, o in ((1, 1), (2, 3), (0, 2)):
        copies[at].wait_recv()
        total = total + inbox[o - 1].astype(F32)
    return total


def moe_kernel(
    wg_hbm, xall, meta, residual, teacher, valid_row,
    mixed, err_out, stats, dw_hbm, dmid, dgates,
    wg, pcat, gslot, xc, oc, dc, gpre, upre, gact, dg, du,
    mine1, pair1, sib1, inbox1, dlow, dall, mine2, pair2, sib2, inbox2, dgsend, stage,
    load_sem, s1, r1, s2, r2, s3, r3, s4, r4, store_sem,
):
    x, core, _, _ = places()
    me = x * 2 + core
    loads = [pltpu.make_async_copy(wg_hbm.at[m], wg.at[m], load_sem.at[m]) for m in range(12)]
    for m in (0, 4, 8, 1, 5, 9, 2, 6, 10, 3, 7, 11):
        loads[m].start()
    greet_line()

    slot_ids = lax.broadcasted_iota(jnp.int32, (64, 128), 0).astype(F32)

    def compact(s, _):
        for e in range(4):
            hit = slot_ids == meta[s, 4 + e : 5 + e, :]
            pcat[s, e * 64 : (e + 1) * 64, :] = hit.astype(F32).astype(BF16)
            gate = jnp.sum(jnp.where(hit, meta[s, e : e + 1, :], 0.0), axis=1, keepdims=True)
            gslot[e, s] = jnp.broadcast_to(gate, (64, 128))
        rows = mm(pcat[s], xall[s]).astype(BF16)
        for e in range(4):
            xc[e, s] = rows[e * 64 : (e + 1) * 64]
        return 0

    lax.fori_loop(0, 8, compact, 0)
    for copy in loads:
        copy.wait()

    def forward(e, _):
        rows = xc[e].reshape(512, 1024)
        g = mm(rows, wg[e])
        u = mm(rows, wg[4 + e])
        gpre[e] = g
        upre[e] = u
        act = g * jax.nn.sigmoid(g) * u
        gate = gslot[e].reshape(512, 128)[:, :1]
        gact[e] = (act * gate).astype(BF16)
        back = mm_nt(act.astype(BF16), wg[8 + e]) * gate
        oc[e] = back.astype(BF16).reshape(8, 64, 1024)
        return 0

    lax.fori_loop(0, 4, forward, 0)

    def combine(mine, pair):
        def one(xs, _):
            for k in range(2):
                s = xs * 2 + (1 - core if k == 0 else core)
                rows = jnp.concatenate([oc[e, s] for e in range(4)], axis=0)
                part = mm_tn(pcat[s], rows).astype(BF16)
                if k == 0:
                    pair[xs] = part
                else:
                    mine[xs] = part
            return 0

        lax.fori_loop(0, 4, one, 0)

    combine(mine1, pair1)
    pair_copy = line_scatter_send_pair(pair1, sib1, s1, r1)
    x_copies = line_scatter_send_x(mine1, pair_copy, sib1, inbox1, s1, r1)
    out = residual[...] + line_scatter_sum(mine1, sib1, inbox1, x_copies)
    mixed[...] = out.astype(BF16)
    eye = lax.broadcasted_iota(jnp.int32, (128, 128), 0) == lax.broadcasted_iota(jnp.int32, (128, 128), 1)
    valid_col = jnp.sum(jnp.where(eye, valid_row[0:1, :], 0.0), axis=1, keepdims=True)
    err = (out - teacher[...]) * valid_col
    err_out[...] = err
    dlow[...] = err.astype(BF16)
    dall[me] = dlow[...]
    gather = line_gather_start(dlow, lambda i: dall.at[i], s2, r2)
    square = jnp.sum(jnp.sum(err * err, axis=1, keepdims=True), axis=0, keepdims=True)
    count = jnp.sum(valid_row[0:1, :], axis=1, keepdims=True)
    stats[0:1, :] = jnp.broadcast_to(square, (1, 128))
    stats[1:2, :] = jnp.broadcast_to(count, (1, 128))
    stats[2:8, :] = jnp.zeros((6, 128), F32)
    line_gather_finish(gather, lambda i: dall.at[i], s2, r2)

    def spread(s, _):
        rows = mm(pcat[s], dall[s]).astype(BF16)
        for e in range(4):
            dc[e, s] = rows[e * 64 : (e + 1) * 64]
        return 0

    lax.fori_loop(0, 8, spread, 0)

    def backward(e, _):
        g = gpre[e]
        u = upre[e]
        sigma = jax.nn.sigmoid(g)
        silu = g * sigma
        gate = gslot[e].reshape(512, 128)[:, :1]
        raw = mm(dc[e].reshape(512, 1024), wg[8 + e])
        act = (silu * u).astype(BF16).astype(F32)
        dgate = jnp.sum(raw * act, axis=1, keepdims=True)
        gslot[e] = jnp.broadcast_to(dgate, (512, 128)).reshape(8, 64, 128)
        da = raw * gate
        dg_e = (da * u * (sigma * (1.0 + g * (1.0 - sigma)))).astype(BF16)
        du_e = (da * silu).astype(BF16)
        dg[e] = dg_e
        du[e] = du_e
        dx = mm_nt(dg_e, wg[e]) + mm_nt(du_e, wg[4 + e])
        oc[e] = dx.astype(BF16).reshape(8, 64, 1024)
        return 0

    lax.fori_loop(0, 4, backward, 0)
    combine(mine2, pair2)
    pair_copy2 = line_scatter_send_pair(pair2, sib2, s3, r3)

    def gate_rows(s, _):
        rows = []
        for e in range(4):
            hit = pcat[s, e * 64 : (e + 1) * 64, :].astype(F32)
            rows.append(jnp.sum(hit * gslot[e, s], axis=0, keepdims=True))
        dgsend[s] = jnp.concatenate(rows + [jnp.zeros((4, 128), F32)], axis=0)
        return 0

    lax.fori_loop(0, 8, gate_rows, 0)
    gate_copies = []
    c, d = lax.axis_index("ctx"), lax.axis_index("dp")
    for o in range(1, 8):
        to = lax.rem(me + o, 8)
        copy = remote(dgsend.at[to], dgates.at[me], s4.at[o], r4.at[o], (to, c, d))
        copy.start()
        gate_copies.append(copy)
    dgates[me] = dgsend[me]
    x_copies2 = line_scatter_send_x(mine2, pair_copy2, sib2, inbox2, s3, r3)

    def weight_grads(e, _):
        rows = xc[e].reshape(512, 1024)
        drows = dc[e].reshape(512, 1024)
        for m, (a, b) in enumerate(((rows, dg[e]), (rows, du[e]), (drows, gact[e]))):
            copy = pltpu.make_async_copy(stage.at[m], dw_hbm.at[m * 4 + e], store_sem.at[m])

            @pl.when(e > 0)
            def _():
                copy.wait()

            stage[m] = mm_tn(a, b).astype(BF16)
            copy.start()
        return 0

    lax.fori_loop(0, 4, weight_grads, 0)
    dmid[...] = line_scatter_sum(mine2, sib2, inbox2, x_copies2)
    for copy in gate_copies:
        copy.wait()
    for m in range(3):
        pltpu.make_async_copy(stage.at[m], dw_hbm.at[m * 4], store_sem.at[m]).wait()
    for copy in [pair_copy, pair_copy2] + x_copies + x_copies2:
        copy.wait_send()


def moe(wg, xall, meta, residual, teacher, valid_row):
    vm = pl.BlockSpec(memory_space=pltpu.VMEM)
    hbm = pl.BlockSpec(memory_space=pl.ANY)
    sems = pltpu.SemaphoreType.DMA
    return pl.pallas_call(
        moe_kernel,
        out_shape=(
            jax.ShapeDtypeStruct((128, 1024), BF16),
            jax.ShapeDtypeStruct((128, 1024), F32),
            jax.ShapeDtypeStruct((8, 128), F32),
            jax.ShapeDtypeStruct((12, 1024, 512), BF16),
            jax.ShapeDtypeStruct((128, 1024), F32),
            jax.ShapeDtypeStruct((8, 8, 128), F32),
        ),
        in_specs=[hbm, vm, vm, vm, vm, vm],
        out_specs=(vm, vm, vm, hbm, vm, vm),
        scratch_shapes=[
            pltpu.VMEM((12, 1024, 512), BF16),
            pltpu.VMEM((8, 256, 128), BF16),
            pltpu.VMEM((4, 8, 64, 128), F32),
            pltpu.VMEM((4, 8, 64, 1024), BF16),
            pltpu.VMEM((4, 8, 64, 1024), BF16),
            pltpu.VMEM((4, 8, 64, 1024), BF16),
            pltpu.VMEM((4, 512, 512), F32),
            pltpu.VMEM((4, 512, 512), F32),
            pltpu.VMEM((4, 512, 512), BF16),
            pltpu.VMEM((4, 512, 512), BF16),
            pltpu.VMEM((4, 512, 512), BF16),
            pltpu.VMEM((4, 128, 1024), BF16),
            pltpu.VMEM((4, 128, 1024), BF16),
            pltpu.VMEM((4, 128, 1024), BF16),
            pltpu.VMEM((3, 128, 1024), BF16),
            pltpu.VMEM((128, 1024), BF16),
            pltpu.VMEM((8, 128, 1024), BF16),
            pltpu.VMEM((4, 128, 1024), BF16),
            pltpu.VMEM((4, 128, 1024), BF16),
            pltpu.VMEM((4, 128, 1024), BF16),
            pltpu.VMEM((3, 128, 1024), BF16),
            pltpu.VMEM((8, 8, 128), F32),
            pltpu.VMEM((3, 1024, 512), BF16),
            sems((12,)),
            sems((4,)),
            sems((4,)),
            sems((8,)),
            sems((8,)),
            sems((4,)),
            sems((4,)),
            sems((8,)),
            sems((8,)),
            sems((3,)),
        ],
        compiler_params=pltpu.CompilerParams(
            collective_id=1, has_side_effects=True, vmem_limit_bytes=63 << 20
        ),
        cost_estimate=pl.CostEstimate(flops=22 * 10**9, bytes_accessed=30 << 20, transcendentals=4 << 20),
        name="moe",
    )(wg, xall, meta, residual, teacher, valid_row)


def plane_device(y, z):
    return (lax.axis_index("expert"), lax.div(z, 2) * 4 + y, lax.rem(z, 2))


def yz():
    c, d = lax.axis_index("ctx"), lax.axis_index("dp")
    return lax.rem(c, 4), lax.div(c, 4) * 2 + d


def greet_all():
    barrier = pltpu.get_barrier_semaphore()
    e, c, d = lax.axis_index("expert"), lax.axis_index("ctx"), lax.axis_index("dp")
    p = c * 2 + d
    for o in range(1, 8):
        pl.semaphore_signal(barrier, inc=1, device_id=(lax.rem(e + o, 8), c, d), device_id_type=MESH)
    for o in range(1, 16):
        q = lax.rem(p + o, 16)
        pl.semaphore_signal(barrier, inc=1, device_id=(e, lax.div(q, 2), lax.rem(q, 2)), device_id_type=MESH)
    pl.semaphore_wait(barrier, 22)


def low_lanes():
    return lax.broadcasted_iota(jnp.int32, (128, 128), 1) < 64


def swap_halves(tile):
    lane = lax.rem(lax.broadcasted_iota(jnp.int32, (128, 128), 1), 64)
    return jnp.where(lane < 32, pltpu.roll(tile, 96, 1), pltpu.roll(tile, 32, 1))


def gain_row(small, row):
    return jnp.concatenate([small[i, row : row + 1, :] for i in range(8)], axis=1)


def key_gain_row(small):
    lane = lax.broadcasted_iota(jnp.int32, (1, 128), 1)
    return jnp.concatenate(
        [jnp.where(lane < 64, small[2 * t, 3:4, :], small[2 * t + 1, 3:4, :]) for t in range(4)], axis=1
    )


def router_rows(small):
    return jnp.concatenate([small[i, 16:48, :] for i in range(8)], axis=1)


def inverse_rms(values):
    return lax.rsqrt(jnp.mean(values * values, axis=1, keepdims=True) + EPS)


def key_bias(vbuf, c):
    row = jnp.concatenate([vbuf[2 * c, 0:1, :], vbuf[2 * c + 1, 0:1, :]], axis=1)
    return (row - 1.0) * 1e30


def diagonal(d):
    row = lax.rem(lax.broadcasted_iota(jnp.int32, (256, 256), 0), 128) + 128 * d
    return row == lax.broadcasted_iota(jnp.int32, (256, 256), 1)


def stack_heads(tile, upper):
    lo = low_lanes()
    turned = pltpu.roll(tile, 64, 1)
    first, second = (turned, tile) if upper else (tile, turned)
    keep = jnp.logical_not(lo) if upper else lo
    return jnp.concatenate([jnp.where(keep, first, 0.0), jnp.where(keep, second, 0.0)], axis=0)


def front_kernel(
    tokens, wq, wk, wv, wo, small, ew, valid, cosine, sine, routes,
    wg, wall_out, small_all, vbuf, kvbuf, qbuf, oheads, lse, att, residual, normed_t, qpre, kpre, xall, meta, probs_out, picks_out,
    wall, sendkv, sendq, osend, low, metasend,
    own_sem, ew_sem, wall_sem, ssm, rsm, sqkv, rqkv, swo, rwo, sv, rv, sa1, ra1, sb1, rb1, sa2, ra2, sb2, rb2,
    skv, rkv, sq, rq, so, ro, sx, rx, sm, rm,
):
    x, core, c, d = places()
    me = x * 2 + core
    p = c * 2 + d
    y, z = yz()
    zh, zl = lax.div(z, 2), lax.rem(z, 2)
    e = lax.axis_index("expert")
    own = [
        pltpu.make_async_copy(wq, wall.at[me, :, pl.ds(0, 1024)], own_sem.at[0]),
        pltpu.make_async_copy(wk, wall.at[me, :, pl.ds(1024, 512)], own_sem.at[1]),
        pltpu.make_async_copy(wv, wall.at[me, :, pl.ds(1536, 512)], own_sem.at[2]),
        pltpu.make_async_copy(wo, wall.at[me, :, pl.ds(2048, 1024)], own_sem.at[3]),
    ]
    for copy in own:
        copy.start()
    own_ew = pltpu.make_async_copy(ew, wg.at[:, zh, y, zl], ew_sem)
    own_ew.start()
    small_all[me] = small[...]
    vbuf[p] = valid[...]
    greet_all()

    small_gather = line_gather_start(small, lambda i: small_all.at[i], ssm, rsm)
    ew_a, ew_b = ew.at[pl.ds(0, 6)], ew.at[pl.ds(6, 6)]
    a1 = [
        remote(ew_a, wg.at[pl.ds(0, 6), zh, y, zl], sa1.at[o], ra1.at[o], plane_device(lax.rem(y + o, 4), z))
        for o in (2, 1, 3)
    ]
    b1 = [
        remote(ew_b, wg.at[pl.ds(6, 6), zh, y, zl], sb1.at[o], rb1.at[o], plane_device(y, lax.rem(z + o, 4)))
        for o in (2, 1, 3)
    ]
    for copy in a1 + b1:
        copy.start()
    for copy in own[:3]:
        copy.wait()
    qkv_gather = line_gather_start(
        wall.at[me, :, pl.ds(0, 2048)], lambda i: wall.at[i, :, pl.ds(0, 2048)], sqkv, rqkv
    )
    own[3].wait()
    out_gather = line_gather_start(
        wall.at[me, :, pl.ds(2048, 1024)], lambda i: wall.at[i, :, pl.ds(2048, 1024)], swo, rwo
    )
    valid_copies = []
    for o in range(1, 16):
        q = lax.rem(p + o, 16)
        copy = remote(valid, vbuf.at[p], sv.at[o], rv.at[o], (e, lax.div(q, 2), lax.rem(q, 2)))
        copy.start()
        valid_copies.append(copy)

    line_gather_finish(small_gather, lambda i: small_all.at[i], ssm, rsm)
    gains = small_all[...].astype(F32)
    values = tokens[...].astype(F32)
    normed = (values * inverse_rms(values) * gain_row(gains, 0)).astype(BF16)
    for t in range(8):
        normed_t[t] = normed[:, 128 * t : 128 * t + 128]

    own_ew.wait()
    for copy in a1 + b1:
        copy.wait_recv()
    a2, b2 = [], []
    for o in (2, 1, 3):
        view = wg.at[pl.ds(0, 6), zh, :, zl]
        a2.append(remote(view, view, sa2.at[o], ra2.at[o], plane_device(y, lax.rem(z + o, 4))))
        view = wg.at[pl.ds(6, 6), :, y, :]
        b2.append(remote(view, view, sb2.at[o], rb2.at[o], plane_device(lax.rem(y + o, 4), z)))
    for copy in a2 + b2:
        copy.start()

    line_gather_finish(qkv_gather, lambda i: wall.at[i, :, pl.ds(0, 2048)], sqkv, rqkv)
    q_pre = mm(normed, wall[:, :, 0:1024].reshape(1024, 1024))
    k_pre = mm(normed, wall[:, :, 1024:1536].reshape(1024, 512))
    v_low = mm(normed, wall[:, :, 1536:2048].reshape(1024, 512)).astype(BF16).astype(F32)
    qpre[...] = q_pre
    kpre[...] = k_pre
    cos, sin = cosine[...], sine[...]
    lo = low_lanes()
    kn = k_pre * inverse_rms(k_pre) * key_gain_row(gains)
    for t in range(4):
        tile = kn[:, 128 * t : 128 * t + 128]
        k_rot = tile * cos + swap_halves(tile) * sin
        v_tile = v_low[:, 128 * t : 128 * t + 128]
        sendkv[2 * t] = jnp.where(lo, k_rot, pltpu.roll(v_tile, 64, 1)).astype(BF16)
        sendkv[2 * t + 1] = jnp.where(lo, pltpu.roll(k_rot, 64, 1), v_tile).astype(BF16)
    kvbuf[p] = sendkv[c]
    kv_copies = []
    for o in range(1, 16):
        q = lax.rem(p + o, 16)
        to = lax.div(q, 2)
        copy = remote(sendkv.at[to], kvbuf.at[p], skv.at[o], rkv.at[o], (e, to, lax.rem(q, 2)))
        copy.start()
        kv_copies.append(copy)
    qn = q_pre * inverse_rms(q_pre) * gain_row(gains, 1)
    for t in range(8):
        tile = qn[:, 128 * t : 128 * t + 128]
        sendq[t] = (tile * cos + swap_halves(tile) * sin).astype(BF16)
    qbuf[c] = sendq[c]
    q_copies = []
    for o in range(1, 8):
        to = lax.rem(c + o, 8)
        copy = remote(sendq.at[to], qbuf.at[c], sq.at[o], rq.at[o], (e, to, d))
        copy.start()
        q_copies.append(copy)
    for copy in valid_copies + kv_copies + q_copies:
        copy.wait_recv()

    def chunk(i, _):
        b = lax.rem(c + 1 + i, 8)
        queries = (stack_heads(qbuf[b].astype(F32), False) * (HEAD**-0.5)).astype(BF16)

        def update(carry, block, scores):
            top, total, acc = carry
            new_top = jnp.maximum(top, jnp.max(scores, axis=1, keepdims=True))
            weights = jnp.exp(scores - new_top)
            shrink = jnp.exp(top - new_top)
            total = total * shrink + jnp.sum(weights, axis=1, keepdims=True)
            acc = acc * shrink + mm(weights.astype(BF16), block)
            return (new_top, total, acc)

        def keys(k, carry):
            block = kvbuf[pl.ds(2 * k, 2)].reshape(256, 128)
            return update(carry, block, mm_nt(queries, block) + key_bias(vbuf, k))

        zero = jnp.zeros((256, 1), F32)
        carry = lax.fori_loop(0, b, keys, (zero + NEG, zero, jnp.zeros((256, 128), F32)))
        block = kvbuf[pl.ds(2 * b, 2)].reshape(256, 128)
        scores = mm_nt(queries, block)
        scores = jnp.where(diagonal(d), scores, scores + key_bias(vbuf, b))
        top, total, acc = update(carry, block, scores)
        acc = acc / total
        lse[b] = jnp.broadcast_to(top + jnp.log(total), (256, 128))
        merged = jnp.where(lo, pltpu.roll(acc[:128], 64, 1), acc[128:])
        oheads[b] = merged
        osend[b] = merged.astype(BF16)

        @pl.when(b != c)
        def _():
            remote(osend.at[b], att.at[c], so.at[b], ro.at[c], (e, b, d)).start()

        @pl.when(b == c)
        def _():
            att[c] = osend[c]

        return 0

    lax.fori_loop(0, 8, chunk, 0)
    line_gather_finish(out_gather, lambda i: wall.at[i, :, pl.ds(2048, 1024)], swo, rwo)
    store = pltpu.make_async_copy(wall, wall_out, wall_sem)
    store.start()

    def wait_rest(i, _):
        b = lax.rem(c + 1 + i, 8)
        copy = remote(osend.at[b], att.at[b], so.at[b], ro.at[b], (e, b, d))
        copy.wait_send()
        copy.wait_recv()
        return 0

    lax.fori_loop(0, 7, wait_rest, 0)
    attended = jnp.concatenate([att[t] for t in range(8)], axis=1)
    res = tokens[...].astype(F32) + mm(attended, wall[:, :, 2048:3072].reshape(1024, 1024))
    residual[...] = res
    mid = (res * inverse_rms(res) * gain_row(gains, 2)).astype(BF16)
    low[...] = mid
    xall[me] = mid
    mid_gather = line_gather_start(low, lambda i: xall.at[i], sx, rx)
    logits = mm_nt(router_rows(small_all[...]), mid)
    terms = jnp.exp(logits - jnp.max(logits, axis=0, keepdims=True))
    probs = terms / jnp.sum(terms, axis=0, keepdims=True)
    ids = lax.broadcasted_iota(jnp.int32, (32, 128), 0)
    picks = jnp.zeros((32, 128), F32)
    for k in range(TOP):
        picks = picks + (ids == routes[k : k + 1, :]).astype(F32)
    before = lax.broadcasted_iota(jnp.int32, (128, 128), 0) < lax.broadcasted_iota(jnp.int32, (128, 128), 1)
    slots = mm(picks.astype(BF16), before.astype(F32).astype(BF16))
    slots = jnp.where(picks > 0.0, slots, -1.0)
    probs_out[...] = probs
    picks_out[...] = picks
    gates = probs * picks
    for i in range(8):
        metasend[i, 0:4, :] = gates[4 * i : 4 * i + 4, :]
        metasend[i, 4:8, :] = slots[4 * i : 4 * i + 4, :]
    meta[me] = metasend[me]
    meta_copies = []
    for o in range(1, 8):
        to = lax.rem(me + o, 8)
        copy = remote(metasend.at[to], meta.at[me], sm.at[o], rm.at[o], (to, c, d))
        copy.start()
        meta_copies.append(copy)
    line_gather_finish(mid_gather, lambda i: xall.at[i], sx, rx)
    for copy in meta_copies:
        copy.wait()
    for copy in a2 + b2:
        copy.wait()
    for copy in a1 + b1 + valid_copies + kv_copies + q_copies:
        copy.wait_send()
    store.wait()


def front(tokens, wq, wk, wv, wo, small, ew, valid, cosine, sine, routes):
    vm = pl.BlockSpec(memory_space=pltpu.VMEM)
    hbm = pl.BlockSpec(memory_space=pl.ANY)
    sems = pltpu.SemaphoreType.DMA
    shape = jax.ShapeDtypeStruct
    return pl.pallas_call(
        front_kernel,
        out_shape=(
            shape((12, 2, 4, 2, 64, 512), BF16),
            shape((8, 128, 3072), BF16),
            shape((8, 48, 128), BF16),
            shape((16, 8, 128), F32),
            shape((16, 128, 128), BF16),
            shape((8, 128, 128), BF16),
            shape((8, 128, 128), F32),
            shape((8, 256, 128), F32),
            shape((8, 128, 128), BF16),
            shape((128, 1024), F32),
            shape((8, 128, 128), BF16),
            shape((128, 1024), F32),
            shape((128, 512), F32),
            shape((8, 128, 1024), BF16),
            shape((8, 8, 128), F32),
            shape((32, 128), F32),
            shape((32, 128), F32),
        ),
        in_specs=[vm, hbm, hbm, hbm, hbm, vm, hbm, vm, vm, vm, vm],
        out_specs=(hbm, hbm) + (vm,) * 15,
        scratch_shapes=[
            pltpu.VMEM((8, 128, 3072), BF16),
            pltpu.VMEM((8, 128, 128), BF16),
            pltpu.VMEM((8, 128, 128), BF16),
            pltpu.VMEM((8, 128, 128), BF16),
            pltpu.VMEM((128, 1024), BF16),
            pltpu.VMEM((8, 8, 128), F32),
            sems((4,)), sems(()), sems(()),
            sems((8,)), sems((8,)), sems((8,)), sems((8,)), sems((8,)), sems((8,)),
            sems((16,)), sems((16,)),
            sems((4,)), sems((4,)), sems((4,)), sems((4,)), sems((4,)), sems((4,)), sems((4,)), sems((4,)),
            sems((16,)), sems((16,)),
            sems((8,)), sems((8,)), sems((8,)), sems((8,)), sems((8,)), sems((8,)), sems((8,)), sems((8,)),
        ],
        compiler_params=pltpu.CompilerParams(
            collective_id=0, has_side_effects=True, vmem_limit_bytes=48 << 20
        ),
        cost_estimate=pl.CostEstimate(flops=3 * 10**9, bytes_accessed=30 << 20, transcendentals=3 << 20),
        name="front",
    )(tokens, wq, wk, wv, wo, small, ew, valid, cosine, sine, routes)


def line_scatter_begin(parts_of, pair, mine, sib, send, recv):
    x, core, _, _ = places()

    def one(k, _):
        pair[k] = parts_of(k * 2 + 1 - core)
        return 0

    def other(k, _):
        mine[k] = parts_of(k * 2 + core)
        return 0

    lax.fori_loop(0, 4, one, 0)
    copy = line_scatter_send_pair(pair, sib, send, recv)
    lax.fori_loop(0, 4, other, 0)
    return copy


def plane_peer(o):
    e, c, d = lax.axis_index("expert"), lax.axis_index("ctx"), lax.axis_index("dp")
    q = lax.rem(c * 2 + d + o, 16)
    return q, (e, lax.div(q, 2), lax.rem(q, 2))


def plane_sum_send(pieces, n, inbox, send, recv):
    copies = []
    for o in range(1, 16):
        q, device = plane_peer(o)
        copy = remote(pieces.at[pl.ds(q * n, n)], inbox.at[o], send.at[o], recv.at[o], device)
        copy.start()
        copies.append(copy)
    return copies


def plane_sum_share(copies, pieces, n, inbox, result, send, recv):
    p = lax.axis_index("ctx") * 2 + lax.axis_index("dp")
    total = pieces[pl.ds(p * n, n)].astype(F32)
    for at, copy in enumerate(copies):
        copy.wait_recv()
        total = total + inbox[at + 1].astype(F32)
    result[pl.ds(p * n, n)] = total.astype(BF16)
    shares = []
    view = result.at[pl.ds(p * n, n)]
    for o in range(1, 16):
        _, device = plane_peer(o)
        copy = remote(view, view, send.at[o], recv.at[o], device)
        copy.start()
        shares.append(copy)
    return shares


def rms_back(values, inverse, grad):
    hat = values * inverse
    return inverse * (grad - hat * jnp.mean(grad * hat, axis=1, keepdims=True))


def back_kernel(
    dw, wall_hbm, small_in, vbuf, kvbuf, qbuf, oheads, lse, att, residual, normed_t, qpre, kpre, xall,
    probs_in, picks_in, err, stats, dmid_in, dgates, tokens, cosine, sine,
    gw, gtok, gq, gk, gv, gout, gsmall,
    wall, own_a, own_b, in_a, in_b, sum_a, sum_b, in2_a, in2_b,
    dsend, dattbuf, qpad, dop, delta, dqacc, dkvsend, dqsend, dqbuf, dkvbuf, dqkv, dnorm, dlog,
    pair_o, mine_o, sib_o, inbox_o, pair_n, mine_n, sib_n, inbox_n, smsend, sminbox, smsum, small,
    pieces_o, pin_o, res_o, pieces_n, pin_n, res_n,
    wall_sem, own_sem, sa1, ra1, sb1, rb1, sa2, ra2, sb2, rb2, sd, rd, sdq, rdq, sdkv, rdkv,
    so, ro, sn, rn, ssm, rsm, sp1, rp1, sp2, rp2, sp3, rp3, sp4, rp4, sp5, rp5,
):
    x, core, c, d = places()
    me = x * 2 + core
    p = c * 2 + d
    y, z = yz()
    zh, zl = lax.div(z, 2), lax.rem(z, 2)
    e = lax.axis_index("expert")
    wall_load = pltpu.make_async_copy(wall_hbm, wall, wall_sem)
    wall_load.start()
    own = [
        pltpu.make_async_copy(dw.at[pl.ds(0, 6), zh, :, zl], own_a, own_sem.at[0]),
        pltpu.make_async_copy(dw.at[pl.ds(6, 6), :, y, :], own_b, own_sem.at[1]),
    ]
    for copy in own:
        copy.start()
    greet_all()
    a1, b1 = [], []
    for o in (2, 1, 3):
        to = lax.rem(z + o, 4)
        a1.append(remote(
            dw.at[pl.ds(0, 6), lax.div(to, 2), :, lax.rem(to, 2)], in_a.at[o - 1], sa1.at[o], ra1.at[o], plane_device(y, to)
        ))
        to = lax.rem(y + o, 4)
        b1.append(remote(dw.at[pl.ds(6, 6), :, to, :], in_b.at[o - 1], sb1.at[o], rb1.at[o], plane_device(to, z)))
    for copy in a1 + b1:
        copy.start()

    gains = small_in[...].astype(F32)
    lo = low_lanes()
    probs = probs_in[...]
    dprobs = jnp.concatenate([dgates[i, 0:4, :] for i in range(8)], axis=0) * picks_in[...]
    dlogits = probs * (dprobs - jnp.sum(probs * dprobs, axis=0, keepdims=True))
    high = dlogits.astype(BF16)
    rest = (dlogits - high.astype(F32)).astype(BF16)
    dlog[0:32, :] = high
    dlog[32:64, :] = rest

    def router_back(i, _):
        at = pl.ds(pl.multiple_of(128 * i, 128), 128)
        part = mm(dlog[...], xall[me, :, at])
        smsend[i, 16:48, :] = part[:32] + part[32:]
        router = small_in[i, 16:48, :]
        dnorm[i] = mm_tn(dlog[...], jnp.concatenate([router, router], axis=0))
        return 0

    lax.fori_loop(0, 8, router_back, 0)
    dmid = dmid_in[...] + jnp.concatenate([dnorm[i] for i in range(8)], axis=1)
    res = residual[...]
    res_inv = inverse_rms(res)
    dgain_mid = jnp.sum(dmid * (res * res_inv), axis=0, keepdims=True)
    dres = err[...] + rms_back(res, res_inv, dmid * gain_row(gains, 2))
    dbranch = dres.astype(BF16)
    gtok[...] = dres
    wall_load.wait()
    dqkv[:, 0:1024] = dbranch

    def attended_back(t, _):
        dsend[t] = mm_nt(dqkv[:, 0:1024], wall[t, :, 2048:3072]).astype(BF16)
        return 0

    lax.fori_loop(0, 8, attended_back, 0)
    dattbuf[c] = dsend[c]
    d_copies = []
    for o in range(1, 8):
        to = lax.rem(c + o, 8)
        copy = remote(dsend.at[to], dattbuf.at[c], sd.at[o], rd.at[o], (e, to, d))
        copy.start()
        d_copies.append(copy)
    pair_copy_o = line_scatter_begin(lambda i: mm_tn(att[i], dqkv[:, 0:1024]).astype(BF16), pair_o, mine_o, sib_o, so, ro)

    def prepare(b, _):
        qpad[b] = (stack_heads(qbuf[b].astype(F32), False) * (HEAD**-0.5)).astype(BF16)
        return 0

    lax.fori_loop(0, 8, prepare, 0)
    x_copies_o = line_scatter_send_x(mine_o, pair_copy_o, sib_o, inbox_o, so, ro)
    for copy in d_copies:
        copy.wait_recv()

    def prepare_back(b, _):
        tile = dattbuf[b].astype(F32)
        dop[b] = stack_heads(tile, True).astype(BF16)
        both = tile * oheads[b]
        first = jnp.sum(jnp.where(lo, both, 0.0), axis=1, keepdims=True)
        second = jnp.sum(jnp.where(lo, 0.0, both), axis=1, keepdims=True)
        delta[b] = jnp.broadcast_to(jnp.concatenate([first, second], axis=0), (256, 128))
        dqacc[b] = jnp.zeros((256, 128), F32)
        return 0

    lax.fori_loop(0, 8, prepare_back, 0)

    def key_block(k, _):
        block = kvbuf[pl.ds(2 * k, 2)].reshape(256, 128)
        bias = key_bias(vbuf, k)

        def one(b, acc, scores):
            weights = jnp.exp(scores - lse[b][:, 0:1])
            dweights = mm_nt(dop[b], block)
            dscores = (weights * (dweights - delta[b][:, 0:1])).astype(BF16)
            dqacc[b] = dqacc[b] + mm(dscores, block)
            return acc + mm_tn(weights.astype(BF16), dop[b]) + mm_tn(dscores, qpad[b])

        scores = mm_nt(qpad[k], block)
        acc = one(k, jnp.zeros((256, 128), F32), jnp.where(diagonal(d), scores, scores + bias))
        acc = lax.fori_loop(k + 1, 8, lambda b, acc: one(b, acc, mm_nt(qpad[b], block) + bias), acc)
        dkvsend[pl.ds(2 * k, 2)] = acc.astype(BF16).reshape(2, 128, 128)
        done = dqacc[k] * (HEAD**-0.5)
        dqsend[k] = jnp.where(lo, done[:128], pltpu.roll(done[128:], 64, 1)).astype(BF16)

        @pl.when(k != c)
        def _():
            remote(dqsend.at[k], dqbuf.at[c], sdq.at[k], rdq.at[c], (e, k, d)).start()
            remote(dkvsend.at[2 * k], dkvbuf.at[p], sdkv.at[2 * k], rdkv.at[p], (e, k, 0)).start()
            remote(dkvsend.at[2 * k + 1], dkvbuf.at[p], sdkv.at[2 * k + 1], rdkv.at[p], (e, k, 1)).start()

        @pl.when(k == c)
        def _():
            dqbuf[c] = dqsend[c]
            dkvbuf[p] = dkvsend[p]
            other = c * 2 + 1 - d
            remote(dkvsend.at[other], dkvbuf.at[p], sdkv.at[other], rdkv.at[p], (e, c, 1 - d)).start()

        return 0

    lax.fori_loop(0, 8, key_block, 0)

    sum_o = line_scatter_sum(mine_o, sib_o, inbox_o, x_copies_o).astype(BF16)
    for t in range(8):
        for h in range(2):
            pieces_o[2 * t + h] = sum_o[64 * h : 64 * h + 64, 128 * t : 128 * t + 128]
    p_copies_o = plane_sum_send(pieces_o, 1, pin_o, sp1, rp1)

    def wait_dq(i, _):
        b = lax.rem(c + 1 + i, 8)
        copy = remote(dqsend.at[b], dqbuf.at[b], sdq.at[b], rdq.at[b], (e, b, d))
        copy.wait_send()
        copy.wait_recv()
        return 0

    def wait_dkv(i, _):
        q = lax.rem(p + 1 + i, 16)
        copy = remote(dkvsend.at[q], dkvbuf.at[q], sdkv.at[q], rdkv.at[q], (e, lax.div(q, 2), lax.rem(q, 2)))
        copy.wait_send()
        copy.wait_recv()
        return 0

    lax.fori_loop(0, 7, wait_dq, 0)
    lax.fori_loop(0, 15, wait_dkv, 0)
    cos, sin = cosine[...], -sine[...]
    dq = jnp.concatenate([dqbuf[t] for t in range(8)], axis=1).astype(F32)
    dq = jnp.concatenate(
        [dq[:, 128 * t : 128 * t + 128] * cos + swap_halves(dq[:, 128 * t : 128 * t + 128]) * sin for t in range(8)], axis=1
    )
    q_pre = qpre[...]
    q_inv = inverse_rms(q_pre)
    dgain_q = jnp.sum(dq * (q_pre * q_inv), axis=0, keepdims=True)
    dqkv[:, 0:1024] = rms_back(q_pre, q_inv, dq * gain_row(gains, 1)).astype(BF16)
    dk_tiles, dv_tiles = [], []
    for t in range(4):
        even = dkvbuf[4 * t].astype(F32) + dkvbuf[4 * t + 1].astype(F32)
        odd = dkvbuf[4 * t + 2].astype(F32) + dkvbuf[4 * t + 3].astype(F32)
        tile = jnp.where(lo, even, pltpu.roll(odd, 64, 1))
        dk_tiles.append(tile * cos + swap_halves(tile) * sin)
        dv_tiles.append(jnp.where(lo, pltpu.roll(even, 64, 1), odd))
    dk = jnp.concatenate(dk_tiles, axis=1)
    k_pre = kpre[...]
    k_inv = inverse_rms(k_pre)
    dgain_k = jnp.sum(dk * (k_pre * k_inv), axis=0, keepdims=True)
    dqkv[:, 1024:1536] = rms_back(k_pre, k_inv, dk * key_gain_row(gains)).astype(BF16)
    dqkv[:, 1536:2048] = jnp.concatenate(dv_tiles, axis=1).astype(BF16)
    pair_copy_n = line_scatter_begin(lambda i: mm_tn(normed_t[i], dqkv[...]).astype(BF16), pair_n, mine_n, sib_n, sn, rn)

    shares_o = plane_sum_share(p_copies_o, pieces_o, 1, pin_o, res_o, sp2, rp2)

    def normed_back(t, _):
        dnorm[t] = mm_nt(dqkv[...], wall[t, :, 0:2048])
        return 0

    lax.fori_loop(0, 8, normed_back, 0)
    dnormed = jnp.concatenate([dnorm[t] for t in range(8)], axis=1)
    x_copies_n = line_scatter_send_x(mine_n, pair_copy_n, sib_n, inbox_n, sn, rn)
    values = tokens[...].astype(F32)
    inv = inverse_rms(values)
    dgain_in = jnp.sum(dnormed * (values * inv), axis=0, keepdims=True)
    gtok[...] = gtok[...] + rms_back(values, inv, dnormed * gain_row(gains, 0))
    for i in range(8):
        at = slice(128 * i, 128 * i + 128)
        smsend[i, 0:1, :] = dgain_in[:, at]
        smsend[i, 1:2, :] = dgain_q[:, at]
        smsend[i, 2:3, :] = dgain_mid[:, at]
        half = dgain_k[:, 128 * (i // 2) : 128 * (i // 2) + 128]
        smsend[i, 3:4, :] = half if i % 2 == 0 else pltpu.roll(jnp.broadcast_to(half, (8, 128)), 64, 1)[0:1]
        smsend[i, 4:6, :] = stats[0:2, :]
        smsend[i, 6:16, :] = jnp.zeros((10, 128), F32)
    sm_copies = []
    for o in range(1, 8):
        to = lax.rem(me + o, 8)
        copy = remote(smsend.at[to], sminbox.at[o], ssm.at[o], rsm.at[o], (to, c, d))
        copy.start()
        sm_copies.append(copy)

    for copy in own:
        copy.wait()
    for copy in a1 + b1:
        copy.wait_recv()

    def first_sums(m, _):
        sum_a[m] = (
            own_a[m].astype(F32) + in_a[0, m].astype(F32) + in_a[1, m].astype(F32) + in_a[2, m].astype(F32)
        ).astype(BF16)
        sum_b[m] = (
            own_b[m].astype(F32) + in_b[0, m].astype(F32) + in_b[1, m].astype(F32) + in_b[2, m].astype(F32)
        ).astype(BF16)
        return 0

    lax.fori_loop(0, 6, first_sums, 0)
    a2, b2 = [], []
    for o in (2, 1, 3):
        to = lax.rem(y + o, 4)
        a2.append(remote(sum_a.at[:, to], in2_a.at[o - 1], sa2.at[o], ra2.at[o], plane_device(to, z)))
        to = lax.rem(z + o, 4)
        b2.append(remote(
            sum_b.at[:, lax.div(to, 2), lax.rem(to, 2)], in2_b.at[o - 1], sb2.at[o], rb2.at[o], plane_device(y, to)
        ))
    for copy in a2 + b2:
        copy.start()

    total = smsend[me]
    for at, copy in enumerate(sm_copies):
        copy.wait_recv()
        total = total + sminbox[at + 1]
    smsum[...] = total
    small_copies = []
    for o in range(1, 16):
        _, device = plane_peer(o)
        copy = remote(smsum, small.at[o], sp5.at[o], rp5.at[o], device)
        copy.start()
        small_copies.append(copy)
    sum_n = line_scatter_sum(mine_n, sib_n, inbox_n, x_copies_n).astype(BF16)
    for t in range(16):
        for h in range(2):
            pieces_n[2 * t + h] = sum_n[64 * h : 64 * h + 64, 128 * t : 128 * t + 128]
    p_copies_n = plane_sum_send(pieces_n, 2, pin_n, sp3, rp3)
    for copy in shares_o:
        copy.wait_recv()
    for t in range(8):
        gout[:, 128 * t : 128 * t + 128] = jnp.concatenate([res_o[2 * t], res_o[2 * t + 1]], axis=0).astype(F32)
    shares_n = plane_sum_share(p_copies_n, pieces_n, 2, pin_n, res_n, sp4, rp4)
    for at, copy in enumerate(small_copies):
        copy.wait_recv()
        total = total + small[at + 1]
    gsmall[...] = total
    for copy in a2 + b2:
        copy.wait_recv()

    def second_sums(m, _):
        gw[m] = sum_a[m, y].astype(F32) + in2_a[0, m].astype(F32) + in2_a[1, m].astype(F32) + in2_a[2, m].astype(F32)
        gw[6 + m] = (
            sum_b[m, zh, zl].astype(F32) + in2_b[0, m].astype(F32) + in2_b[1, m].astype(F32) + in2_b[2, m].astype(F32)
        )
        return 0

    lax.fori_loop(0, 6, second_sums, 0)
    for copy in shares_n:
        copy.wait_recv()
    for t in range(16):
        tile = jnp.concatenate([res_n[2 * t], res_n[2 * t + 1]], axis=0).astype(F32)
        if t < 8:
            gq[:, 128 * t : 128 * t + 128] = tile
        elif t < 12:
            gk[:, 128 * (t - 8) : 128 * (t - 8) + 128] = tile
        else:
            gv[:, 128 * (t - 12) : 128 * (t - 12) + 128] = tile
    for copy in (
        a1 + b1 + a2 + b2 + d_copies + [pair_copy_o, pair_copy_n] + x_copies_o + x_copies_n + sm_copies
        + small_copies + p_copies_o + p_copies_n + shares_o + shares_n
    ):
        copy.wait_send()


def back(*args):
    vm = pl.BlockSpec(memory_space=pltpu.VMEM)
    hbm = pl.BlockSpec(memory_space=pl.ANY)
    sems = pltpu.SemaphoreType.DMA
    shape = jax.ShapeDtypeStruct
    return pl.pallas_call(
        back_kernel,
        out_shape=(
            shape((12, 64, 512), F32),
            shape((128, 1024), F32),
            shape((128, 1024), F32),
            shape((128, 512), F32),
            shape((128, 512), F32),
            shape((128, 1024), F32),
            shape((48, 128), F32),
        ),
        in_specs=[hbm, hbm] + [vm] * 21,
        out_specs=(vm,) * 7,
        scratch_shapes=[
            pltpu.VMEM((8, 128, 3072), BF16),
            pltpu.VMEM((6, 4, 64, 512), BF16),
            pltpu.VMEM((6, 2, 2, 64, 512), BF16),
            pltpu.VMEM((3, 6, 4, 64, 512), BF16),
            pltpu.VMEM((3, 6, 2, 2, 64, 512), BF16),
            pltpu.VMEM((6, 4, 64, 512), BF16),
            pltpu.VMEM((6, 2, 2, 64, 512), BF16),
            pltpu.VMEM((3, 6, 64, 512), BF16),
            pltpu.VMEM((3, 6, 64, 512), BF16),
            pltpu.VMEM((8, 128, 128), BF16),
            pltpu.VMEM((8, 128, 128), BF16),
            pltpu.VMEM((8, 256, 128), BF16),
            pltpu.VMEM((8, 256, 128), BF16),
            pltpu.VMEM((8, 256, 128), F32),
            pltpu.VMEM((8, 256, 128), F32),
            pltpu.VMEM((16, 128, 128), BF16),
            pltpu.VMEM((8, 128, 128), BF16),
            pltpu.VMEM((8, 128, 128), BF16),
            pltpu.VMEM((16, 128, 128), BF16),
            pltpu.VMEM((128, 2048), BF16),
            pltpu.VMEM((8, 128, 128), F32),
            pltpu.VMEM((64, 128), BF16),
            pltpu.VMEM((4, 128, 1024), BF16),
            pltpu.VMEM((4, 128, 1024), BF16),
            pltpu.VMEM((4, 128, 1024), BF16),
            pltpu.VMEM((3, 128, 1024), BF16),
            pltpu.VMEM((4, 128, 2048), BF16),
            pltpu.VMEM((4, 128, 2048), BF16),
            pltpu.VMEM((4, 128, 2048), BF16),
            pltpu.VMEM((3, 128, 2048), BF16),
            pltpu.VMEM((8, 48, 128), F32),
            pltpu.VMEM((8, 48, 128), F32),
            pltpu.VMEM((48, 128), F32),
            pltpu.VMEM((16, 48, 128), F32),
            pltpu.VMEM((16, 64, 128), BF16),
            pltpu.VMEM((16, 1, 64, 128), BF16),
            pltpu.VMEM((16, 64, 128), BF16),
            pltpu.VMEM((32, 64, 128), BF16),
            pltpu.VMEM((16, 2, 64, 128), BF16),
            pltpu.VMEM((32, 64, 128), BF16),
            sems(()), sems((2,)),
            sems((4,)), sems((4,)), sems((4,)), sems((4,)), sems((4,)), sems((4,)), sems((4,)), sems((4,)),
            sems((8,)), sems((8,)), sems((8,)), sems((8,)), sems((16,)), sems((16,)),
            sems((4,)), sems((4,)), sems((4,)), sems((4,)), sems((8,)), sems((8,)),
        ] + [sems((16,))] * 10,
        compiler_params=pltpu.CompilerParams(
            collective_id=2, has_side_effects=True, vmem_limit_bytes=60 << 20
        ),
        cost_estimate=pl.CostEstimate(flops=6 * 10**9, bytes_accessed=60 << 20, transcendentals=3 << 20),
        name="back",
    )(*args)


def per_device(
    tokens,
    norm_in,
    w_query,
    w_key,
    w_value,
    query_gain,
    key_gain,
    w_out,
    norm_mid,
    w_router,
    expert_gate,
    expert_up,
    expert_down,
    routes,
    valid,
    teacher,
):
    positions = (lax.axis_index("ctx") * 2 + lax.axis_index("dp")) * 128 + jnp.arange(128, dtype=jnp.int32)
    frequency = THETA ** (-(jnp.arange(HEAD // 2).astype(F32) * (2.0 / HEAD)))
    angles = positions.astype(F32)[:, None] * frequency[None, :]
    cos, sin = jnp.cos(angles), jnp.sin(angles)
    cosine = jnp.concatenate([cos, cos, cos, cos], axis=1)
    sine = jnp.concatenate([-sin, sin, -sin, sin], axis=1)
    rows = jnp.stack([norm_in, query_gain, norm_mid, jnp.concatenate([key_gain, key_gain])])
    small = jnp.concatenate([rows, jnp.zeros((12, 128), BF16), w_router.T], axis=0)
    ew = jnp.concatenate([jnp.transpose(w, (1, 0, 2)) for w in (expert_gate, expert_up, expert_down)], axis=0)
    valid_rows = jnp.broadcast_to(valid.astype(F32)[None, :], (8, 128))
    (
        wg, wall, small_all, vbuf, kvbuf, qbuf, oheads, lse, att, residual, normed_t, qpre, kpre, xall, meta, probs, picks
    ) = front(tokens, w_query, w_key, w_value, w_out, small, ew, valid_rows, cosine, sine, routes.T)
    mixed, err, stats, dw, dmid, dgates = moe(
        wg.reshape(12, 1024, 512), xall, meta, residual, teacher, valid_rows
    )
    gw, gtok, gq, gk, gv, gout, gsmall = back(
        dw.reshape(12, 2, 4, 2, 64, 512), wall, small_all, vbuf, kvbuf, qbuf, oheads, lse, att, residual, normed_t,
        qpre, kpre, xall, probs, picks, err, stats, dmid, dgates, tokens, cosine, sine,
    )
    loss = gsmall[4, 0] / (gsmall[5, 0] * 1024.0)
    grad_gate, grad_up, grad_down = [jnp.transpose(gw[4 * m : 4 * m + 4], (1, 0, 2)) for m in range(3)]
    return (
        mixed, loss, gtok, gsmall[0], gq, gk, gv, gsmall[1], gsmall[3, :64], gout, gsmall[2], gsmall[16:48].T,
        grad_gate, grad_up, grad_down,
    )


def solution(mesh):
    placed = (
        P(("expert", "ctx", "dp"), None),
        P("expert"),
        P("expert", None),
        P("expert", None),
        P("expert", None),
        P("expert"),
        P("expert"),
        P("expert", None),
        P("expert"),
        P("expert", None),
        P(("ctx", "dp"), "expert", None),
        P(("ctx", "dp"), "expert", None),
        P(("ctx", "dp"), "expert", None),
        P(("expert", "ctx", "dp"), None),
        P(("expert", "ctx", "dp")),
        P(("expert", "ctx", "dp"), None),
    )
    return jax.shard_map(
        per_device,
        mesh=mesh,
        in_specs=placed,
        out_specs=(
            P(("expert", "ctx", "dp"), None),
            P(),
            P(("expert", "ctx", "dp"), None),
            P("expert"),
            P("expert", None),
            P("expert", None),
            P("expert", None),
            P("expert"),
            P("expert"),
            P("expert", None),
            P("expert"),
            P("expert", None),
            P(("ctx", "dp"), "expert", None),
            P(("ctx", "dp"), "expert", None),
            P(("ctx", "dp"), "expert", None),
        ),
        check_vma=False,
    )
```

```python
import jax
import jax.numpy as jnp
from jax import lax
from jax.experimental import pallas as pl
from jax.experimental.pallas import tpu as pltpu
from jax.sharding import PartitionSpec as P

MESH = pl.DeviceIdType.MESH
F32 = jnp.float32
BF16 = jnp.bfloat16

HEAD = 64
TOP = 8
EPS = 1e-06
THETA = 10000.0
NEG = -1e30
HIGH = lax.Precision.HIGHEST


def mm(a, b):
    return lax.dot_general(a, b, (((1,), (0,)), ((), ())), preferred_element_type=F32)


def mm_nt(a, b):
    return lax.dot_general(a, b, (((1,), (1,)), ((), ())), preferred_element_type=F32)


def mm_tn(a, b):
    return lax.dot_general(a, b, (((0,), (0,)), ((), ())), preferred_element_type=F32)


def places():
    e, c, d = lax.axis_index("expert"), lax.axis_index("ctx"), lax.axis_index("dp")
    return e // 2, e % 2, c, d


def remote(src, dst, send, recv, device):
    return pltpu.make_async_remote_copy(
        src_ref=src, dst_ref=dst, send_sem=send, recv_sem=recv, device_id=device, device_id_type=MESH
    )


def line_device(x, core):
    return (lax.rem(x + 4, 4) * 2 + core, lax.axis_index("ctx"), lax.axis_index("dp"))


def greet_line():
    barrier = pltpu.get_barrier_semaphore()
    e, c, d = lax.axis_index("expert"), lax.axis_index("ctx"), lax.axis_index("dp")
    for o in range(1, 8):
        pl.semaphore_signal(barrier, inc=1, device_id=(lax.rem(e + o, 8), c, d), device_id_type=MESH)
    pl.semaphore_wait(barrier, 7)


def line_gather_start(own, buf, send, recv):
    x, core, _, _ = places()
    me = x * 2 + core
    copies = [remote(own, buf(me), send.at[o], recv.at[o], line_device(x + o, core)) for o in (2, 1, 3)]
    copies.append(remote(own, buf(me), send.at[0], recv.at[0], line_device(x, 1 - core)))
    for copy in copies:
        copy.start()
    return copies


def line_gather_finish(copies, buf, send, recv):
    x, core, _, _ = places()
    forwards = []
    for at, o in ((1, 1), (2, 3), (0, 2)):
        copies[at].wait_recv()
        block = buf(lax.rem(x - o + 4, 4) * 2 + core)
        copy = remote(block, block, send.at[4 + o], recv.at[4 + o], line_device(x, 1 - core))
        copy.start()
        forwards.append(copy)
    copies[3].wait_recv()
    for copy in forwards:
        copy.wait_recv()
    for copy in copies + forwards:
        copy.wait_send()


def line_scatter_send_pair(pair, sib, send, recv):
    x, core, _, _ = places()
    copy = remote(pair, sib, send.at[0], recv.at[0], line_device(x, 1 - core))
    copy.start()
    return copy


def line_scatter_send_x(mine, pair_copy, sib, inbox, send, recv):
    x, core, _, _ = places()
    pair_copy.wait_recv()
    copies = []
    for o in (2, 1, 3):
        to = lax.rem(x + o, 4)
        mine[to] = (mine[to].astype(F32) + sib[to].astype(F32)).astype(mine.dtype)
        copy = remote(mine.at[to], inbox.at[o - 1], send.at[o], recv.at[o], line_device(x + o, core))
        copy.start()
        copies.append(copy)
    return copies


def line_scatter_sum(mine, sib, inbox, copies):
    x, _, _, _ = places()
    total = mine[x].astype(F32) + sib[x].astype(F32)
    for at, o in ((1, 1), (2, 3), (0, 2)):
        copies[at].wait_recv()
        total = total + inbox[o - 1].astype(F32)
    return total


def moe_kernel(
    wg_hbm, xall, meta, residual, teacher, valid_row,
    mixed, err_out, stats, dw_hbm, dmid, dgates,
    wg, pcat, gslot, xc, oc, dc, gpre, upre, gact, dg, du,
    mine1, pair1, sib1, inbox1, dlow, dall, mine2, pair2, sib2, inbox2, dgsend, stage,
    load_sem, s1, r1, s2, r2, s3, r3, s4, r4, store_sem,
):
    x, core, _, _ = places()
    me = x * 2 + core
    loads = [pltpu.make_async_copy(wg_hbm.at[m], wg.at[m], load_sem.at[m]) for m in range(12)]
    for m in (0, 4, 8, 1, 5, 9, 2, 6, 10, 3, 7, 11):
        loads[m].start()

    greet_line()

    slot_ids = lax.broadcasted_iota(jnp.int32, (64, 128), 0).astype(F32)

    def compact(s, _):
        for e in range(4):
            hit = slot_ids == meta[s, 4 + e : 5 + e, :]
            pcat[s, e * 64 : (e + 1) * 64, :] = hit.astype(F32).astype(BF16)
            gate = jnp.sum(jnp.where(hit, meta[s, e : e + 1, :], 0.0), axis=1, keepdims=True)
            gslot[e, s] = jnp.broadcast_to(gate, (64, 128))
        rows = mm(pcat[s], xall[s]).astype(BF16)
        for e in range(4):
            xc[e, s] = rows[e * 64 : (e + 1) * 64]
        return 0

    lax.fori_loop(0, 8, compact, 0)

    for copy in loads:
        copy.wait()

    def forward(e, _):
        rows = xc[e].reshape(512, 1024)
        g = mm(rows, wg[e])
        u = mm(rows, wg[4 + e])
        gpre[e] = g
        upre[e] = u
        act = g * jax.nn.sigmoid(g) * u
        gate = gslot[e].reshape(512, 128)[:, :1]
        gact[e] = (act * gate).astype(BF16)
        back = mm_nt(act.astype(BF16), wg[8 + e]) * gate
        oc[e] = back.astype(BF16).reshape(8, 64, 1024)
        return 0

    lax.fori_loop(0, 4, forward, 0)

    def combine(mine, pair):
        def one(xs, _):
            for k in range(2):
                s = xs * 2 + (1 - core if k == 0 else core)
                rows = jnp.concatenate([oc[e, s] for e in range(4)], axis=0)
                part = mm_tn(pcat[s], rows).astype(BF16)
                if k == 0:
                    pair[xs] = part
                else:
                    mine[xs] = part
            return 0

        lax.fori_loop(0, 4, one, 0)

    combine(mine1, pair1)

    pair_copy = line_scatter_send_pair(pair1, sib1, s1, r1)
    x_copies = line_scatter_send_x(mine1, pair_copy, sib1, inbox1, s1, r1)
    out = residual[...] + line_scatter_sum(mine1, sib1, inbox1, x_copies)

    mixed[...] = out.astype(BF16)
    eye = lax.broadcasted_iota(jnp.int32, (128, 128), 0) == lax.broadcasted_iota(jnp.int32, (128, 128), 1)
    valid_col = jnp.sum(jnp.where(eye, valid_row[0:1, :], 0.0), axis=1, keepdims=True)
    err = (out - teacher[...]) * valid_col
    err_out[...] = err
    dlow[...] = err.astype(BF16)
    dall[me] = dlow[...]
    gather = line_gather_start(dlow, lambda i: dall.at[i], s2, r2)
    square = jnp.sum(jnp.sum(err * err, axis=1, keepdims=True), axis=0, keepdims=True)
    count = jnp.sum(valid_row[0:1, :], axis=1, keepdims=True)
    stats[0:1, :] = jnp.broadcast_to(square, (1, 128))
    stats[1:2, :] = jnp.broadcast_to(count, (1, 128))
    stats[2:8, :] = jnp.zeros((6, 128), F32)

    line_gather_finish(gather, lambda i: dall.at[i], s2, r2)

    def spread(s, _):
        rows = mm(pcat[s], dall[s]).astype(BF16)
        for e in range(4):
            dc[e, s] = rows[e * 64 : (e + 1) * 64]
        return 0

    lax.fori_loop(0, 8, spread, 0)

    def backward(e, _):
        g = gpre[e]
        u = upre[e]
        sigma = jax.nn.sigmoid(g)
        silu = g * sigma
        gate = gslot[e].reshape(512, 128)[:, :1]
        raw = mm(dc[e].reshape(512, 1024), wg[8 + e])
        act = (silu * u).astype(BF16).astype(F32)
        dgate = jnp.sum(raw * act, axis=1, keepdims=True)
        gslot[e] = jnp.broadcast_to(dgate, (512, 128)).reshape(8, 64, 128)
        da = raw * gate
        dg_e = (da * u * (sigma * (1.0 + g * (1.0 - sigma)))).astype(BF16)
        du_e = (da * silu).astype(BF16)
        dg[e] = dg_e
        du[e] = du_e
        dx = mm_nt(dg_e, wg[e]) + mm_nt(du_e, wg[4 + e])
        oc[e] = dx.astype(BF16).reshape(8, 64, 1024)
        return 0

    lax.fori_loop(0, 4, backward, 0)

    combine(mine2, pair2)
    pair_copy2 = line_scatter_send_pair(pair2, sib2, s3, r3)

    def gate_rows(s, _):
        rows = []
        for e in range(4):
            hit = pcat[s, e * 64 : (e + 1) * 64, :].astype(F32)
            rows.append(jnp.sum(hit * gslot[e, s], axis=0, keepdims=True))
        dgsend[s] = jnp.concatenate(rows + [jnp.zeros((4, 128), F32)], axis=0)
        return 0

    lax.fori_loop(0, 8, gate_rows, 0)
    gate_copies = []
    c, d = lax.axis_index("ctx"), lax.axis_index("dp")
    for o in range(1, 8):
        to = lax.rem(me + o, 8)
        copy = remote(dgsend.at[to], dgates.at[me], s4.at[o], r4.at[o], (to, c, d))
        copy.start()
        gate_copies.append(copy)
    dgates[me] = dgsend[me]
    x_copies2 = line_scatter_send_x(mine2, pair_copy2, sib2, inbox2, s3, r3)

    def weight_grads(e, _):
        rows = xc[e].reshape(512, 1024)
        drows = dc[e].reshape(512, 1024)
        for m, (a, b) in enumerate(((rows, dg[e]), (rows, du[e]), (drows, gact[e]))):
            copy = pltpu.make_async_copy(stage.at[m], dw_hbm.at[m * 4 + e], store_sem.at[m])

            @pl.when(e > 0)
            def _():
                copy.wait()

            stage[m] = mm_tn(a, b).astype(BF16)
            copy.start()
        return 0

    lax.fori_loop(0, 4, weight_grads, 0)

    dmid[...] = line_scatter_sum(mine2, sib2, inbox2, x_copies2)
    for copy in gate_copies:
        copy.wait()
    for m in range(3):
        pltpu.make_async_copy(stage.at[m], dw_hbm.at[m * 4], store_sem.at[m]).wait()
    for copy in [pair_copy, pair_copy2] + x_copies + x_copies2:
        copy.wait_send()


def moe(wg, xall, meta, residual, teacher, valid_row):
    vm = pl.BlockSpec(memory_space=pltpu.VMEM)
    hbm = pl.BlockSpec(memory_space=pl.ANY)
    sems = pltpu.SemaphoreType.DMA
    return pl.pallas_call(
        moe_kernel,
        out_shape=(
            jax.ShapeDtypeStruct((128, 1024), BF16),
            jax.ShapeDtypeStruct((128, 1024), F32),
            jax.ShapeDtypeStruct((8, 128), F32),
            jax.ShapeDtypeStruct((12, 1024, 512), BF16),
            jax.ShapeDtypeStruct((128, 1024), F32),
            jax.ShapeDtypeStruct((8, 8, 128), F32),
        ),
        in_specs=[hbm, vm, vm, vm, vm, vm],
        out_specs=(vm, vm, vm, hbm, vm, vm),
        scratch_shapes=[
            pltpu.VMEM((12, 1024, 512), BF16),
            pltpu.VMEM((8, 256, 128), BF16),
            pltpu.VMEM((4, 8, 64, 128), F32),
            pltpu.VMEM((4, 8, 64, 1024), BF16),
            pltpu.VMEM((4, 8, 64, 1024), BF16),
            pltpu.VMEM((4, 8, 64, 1024), BF16),
            pltpu.VMEM((4, 512, 512), F32),
            pltpu.VMEM((4, 512, 512), F32),
            pltpu.VMEM((4, 512, 512), BF16),
            pltpu.VMEM((4, 512, 512), BF16),
            pltpu.VMEM((4, 512, 512), BF16),
            pltpu.VMEM((4, 128, 1024), BF16),
            pltpu.VMEM((4, 128, 1024), BF16),
            pltpu.VMEM((4, 128, 1024), BF16),
            pltpu.VMEM((3, 128, 1024), BF16),
            pltpu.VMEM((128, 1024), BF16),
            pltpu.VMEM((8, 128, 1024), BF16),
            pltpu.VMEM((4, 128, 1024), BF16),
            pltpu.VMEM((4, 128, 1024), BF16),
            pltpu.VMEM((4, 128, 1024), BF16),
            pltpu.VMEM((3, 128, 1024), BF16),
            pltpu.VMEM((8, 8, 128), F32),
            pltpu.VMEM((3, 1024, 512), BF16),
            sems((12,)),
            sems((4,)),
            sems((4,)),
            sems((8,)),
            sems((8,)),
            sems((4,)),
            sems((4,)),
            sems((8,)),
            sems((8,)),
            sems((3,)),
        ],
        compiler_params=pltpu.CompilerParams(
            collective_id=1, has_side_effects=True, vmem_limit_bytes=63 << 20
        ),
        cost_estimate=pl.CostEstimate(flops=22 * 10**9, bytes_accessed=30 << 20, transcendentals=4 << 20),
        name="moe",
    )(wg, xall, meta, residual, teacher, valid_row)


def plane_device(y, z):
    return (lax.axis_index("expert"), lax.div(z, 2) * 4 + y, lax.rem(z, 2))


def yz():
    c, d = lax.axis_index("ctx"), lax.axis_index("dp")
    return lax.rem(c, 4), lax.div(c, 4) * 2 + d


def greet_all():
    barrier = pltpu.get_barrier_semaphore()
    e, c, d = lax.axis_index("expert"), lax.axis_index("ctx"), lax.axis_index("dp")
    p = c * 2 + d
    for o in range(1, 8):
        pl.semaphore_signal(barrier, inc=1, device_id=(lax.rem(e + o, 8), c, d), device_id_type=MESH)
    for o in range(1, 16):
        q = lax.rem(p + o, 16)
        pl.semaphore_signal(barrier, inc=1, device_id=(e, lax.div(q, 2), lax.rem(q, 2)), device_id_type=MESH)
    pl.semaphore_wait(barrier, 22)


def low_lanes():
    return lax.broadcasted_iota(jnp.int32, (128, 128), 1) < 64


def swap_halves(tile):
    lane = lax.rem(lax.broadcasted_iota(jnp.int32, (128, 128), 1), 64)
    return jnp.where(lane < 32, pltpu.roll(tile, 96, 1), pltpu.roll(tile, 32, 1))


def gain_row(small, row):
    return jnp.concatenate([small[i, row : row + 1, :] for i in range(8)], axis=1)


def key_gain_row(small):
    lane = lax.broadcasted_iota(jnp.int32, (1, 128), 1)
    return jnp.concatenate(
        [jnp.where(lane < 64, small[2 * t, 3:4, :], small[2 * t + 1, 3:4, :]) for t in range(4)], axis=1
    )


def router_rows(small):
    return jnp.concatenate([small[i, 16:48, :] for i in range(8)], axis=1)


def inverse_rms(values):
    return lax.rsqrt(jnp.mean(values * values, axis=1, keepdims=True) + EPS)


def key_bias(vbuf, c):
    row = jnp.concatenate([vbuf[2 * c, 0:1, :], vbuf[2 * c + 1, 0:1, :]], axis=1)
    return (row - 1.0) * 1e30


def diagonal(d):
    row = lax.rem(lax.broadcasted_iota(jnp.int32, (256, 256), 0), 128) + 128 * d
    return row == lax.broadcasted_iota(jnp.int32, (256, 256), 1)


def stack_heads(tile, upper):
    lo = low_lanes()
    turned = pltpu.roll(tile, 64, 1)
    first, second = (turned, tile) if upper else (tile, turned)
    keep = jnp.logical_not(lo) if upper else lo
    return jnp.concatenate([jnp.where(keep, first, 0.0), jnp.where(keep, second, 0.0)], axis=0)


class PlaneGather:
    def __init__(self, ew, wg, send, recv):
        self.ew, self.wg, self.send, self.recv = ew, wg, send, recv
        self.y, self.z = yz()
        self.copies = {}

    def go(self, n, src, dst, device):
        copy = remote(src, dst, self.send.at[n], self.recv.at[n], device)
        copy.start()
        self.copies[n] = copy

    def place(self, m, y, z):
        return self.wg.at[m, lax.div(z, 2), y, lax.rem(z, 2)]

    def shards(self):
        y, z = self.y, self.z
        a, b = pl.ds(0, 6), pl.ds(6, 6)
        for i, o in enumerate((1, 3)):
            self.go(i, self.ew.at[a], self.place(a, y, z), plane_device(lax.rem(y + o, 4), z))
            self.go(2 + i, self.ew.at[b], self.place(b, y, z), plane_device(y, lax.rem(z + o, 4)))

    def shards_on(self):
        y, z = self.y, self.z
        a, b = pl.ds(0, 6), pl.ds(6, 6)
        for i, o in enumerate((1, 3)):
            rows = pl.ds(32 * i, 32)
            self.copies[i].wait_recv()
            view = self.place(a, lax.rem(y - o + 4, 4), z).at[:, rows]
            self.go(4 + i, view, view, plane_device(lax.rem(y + o, 4), z))
            self.copies[2 + i].wait_recv()
            view = self.place(b, y, lax.rem(z - o + 4, 4)).at[:, rows]
            self.go(6 + i, view, view, plane_device(y, lax.rem(z + o, 4)))

    def shards_wait(self):
        for n in range(4, 8):
            self.copies[n].wait_recv()

    def lines(self, j):
        y, z = self.y, self.z
        for i, o in enumerate((1, 3)):
            view = self.wg.at[j, lax.div(z, 2), :, lax.rem(z, 2)]
            self.go(8 + 8 * j + i, view, view, plane_device(y, lax.rem(z + o, 4)))
            view = self.wg.at[6 + j, :, y]
            self.go(10 + 8 * j + i, view, view, plane_device(lax.rem(y + o, 4), z))

    def lines_on(self, j):
        y, z = self.y, self.z
        for i, o in enumerate((1, 3)):
            self.copies[8 + 8 * j + i].wait_recv()
            from_z = lax.rem(z - o + 4, 4)
            view = self.wg.at[j, lax.div(from_z, 2), pl.ds(2 * i, 2), lax.rem(from_z, 2)]
            self.go(12 + 8 * j + i, view, view, plane_device(y, lax.rem(z + o, 4)))
            self.copies[10 + 8 * j + i].wait_recv()
            view = self.wg.at[6 + j, i, lax.rem(y - o + 4, 4)]
            self.go(14 + 8 * j + i, view, view, plane_device(lax.rem(y + o, 4), z))

    def finish(self):
        for j in range(6):
            for n in range(12 + 8 * j, 16 + 8 * j):
                self.copies[n].wait_recv()
        for copy in self.copies.values():
            copy.wait_send()


def front_kernel(
    tokens, wq, wk, wv, wo, small, ew, valid, cosine, sine, routes,
    wg, wall_out, small_all, vbuf, kvbuf, qbuf, oheads, lse, att, residual, normed_t, qpre, kpre, xall, meta, probs_out, picks_out, nx, attx,
    wall, sendkv, sendq, osend, low, metasend,
    own_sem, ew_sem, wall_sem, ssm, rsm, sqkv, rqkv, swo, rwo, sv, rv, sew, rew, snx, rnx, sax, rax,
    skv, rkv, sq, rq, so, ro, sx, rx, sm, rm,
):
    x, core, c, d = places()
    me = x * 2 + core
    p = c * 2 + d
    y, z = yz()
    zh, zl = lax.div(z, 2), lax.rem(z, 2)
    e = lax.axis_index("expert")
    own = [
        pltpu.make_async_copy(wq, wall.at[me, :, pl.ds(0, 1024)], own_sem.at[0]),
        pltpu.make_async_copy(wk, wall.at[me, :, pl.ds(1024, 512)], own_sem.at[1]),
        pltpu.make_async_copy(wv, wall.at[me, :, pl.ds(1536, 512)], own_sem.at[2]),
        pltpu.make_async_copy(wo, wall.at[me, :, pl.ds(2048, 1024)], own_sem.at[3]),
    ]
    for copy in own:
        copy.start()
    own_ew = pltpu.make_async_copy(ew, wg.at[:, zh, y, zl], ew_sem)
    own_ew.start()
    small_all[me] = small[...]
    vbuf[p] = valid[...]
    greet_all()

    small_gather = line_gather_start(small, lambda i: small_all.at[i], ssm, rsm)
    bulk = PlaneGather(ew, wg, sew, rew)
    bulk.shards()
    for copy in own[:3]:
        copy.wait()
    qkv_gather = line_gather_start(
        wall.at[me, :, pl.ds(0, 2048)], lambda i: wall.at[i, :, pl.ds(0, 2048)], sqkv, rqkv
    )
    own[3].wait()
    out_gather = line_gather_start(
        wall.at[me, :, pl.ds(2048, 1024)], lambda i: wall.at[i, :, pl.ds(2048, 1024)], swo, rwo
    )
    valid_copies = []
    for o in range(1, 16):
        q = lax.rem(p + o, 16)
        copy = remote(valid, vbuf.at[p], sv.at[o], rv.at[o], (e, lax.div(q, 2), lax.rem(q, 2)))
        copy.start()
        valid_copies.append(copy)

    line_gather_finish(small_gather, lambda i: small_all.at[i], ssm, rsm)
    gains = small_all[...].astype(F32)
    values = tokens[...].astype(F32)
    normed = (values * inverse_rms(values) * gain_row(gains, 0)).astype(BF16)
    for t in range(8):
        normed_t[t] = normed[:, 128 * t : 128 * t + 128]

    nx[me] = normed_t[me]
    nx_copies = []
    for o in range(1, 8):
        to = lax.rem(me + o, 8)
        copy = remote(normed_t.at[to], nx.at[me], snx.at[o], rnx.at[o], (to, c, d))
        copy.start()
        nx_copies.append(copy)
    bulk.shards_on()
    own_ew.wait()
    bulk.shards_wait()
    for j in range(2):
        bulk.lines(j)
    line_gather_finish(qkv_gather, lambda i: wall.at[i, :, pl.ds(0, 2048)], sqkv, rqkv)
    for j in range(2):
        bulk.lines_on(j)
    q_pre = mm(normed, wall[:, :, 0:1024].reshape(1024, 1024))
    k_pre = mm(normed, wall[:, :, 1024:1536].reshape(1024, 512))
    v_low = mm(normed, wall[:, :, 1536:2048].reshape(1024, 512)).astype(BF16).astype(F32)
    qpre[...] = q_pre
    kpre[...] = k_pre
    cos, sin = cosine[...], sine[...]
    lo = low_lanes()
    kn = k_pre * inverse_rms(k_pre) * key_gain_row(gains)
    for t in range(4):
        tile = kn[:, 128 * t : 128 * t + 128]
        k_rot = tile * cos + swap_halves(tile) * sin
        v_tile = v_low[:, 128 * t : 128 * t + 128]
        sendkv[2 * t] = jnp.where(lo, k_rot, pltpu.roll(v_tile, 64, 1)).astype(BF16)
        sendkv[2 * t + 1] = jnp.where(lo, pltpu.roll(k_rot, 64, 1), v_tile).astype(BF16)
    kvbuf[p] = sendkv[c]
    kv_copies = []
    for o in range(1, 16):
        q = lax.rem(p + o, 16)
        to = lax.div(q, 2)
        copy = remote(sendkv.at[to], kvbuf.at[p], skv.at[o], rkv.at[o], (e, to, lax.rem(q, 2)))
        copy.start()
        kv_copies.append(copy)
    qn = q_pre * inverse_rms(q_pre) * gain_row(gains, 1)
    for t in range(8):
        tile = qn[:, 128 * t : 128 * t + 128]
        sendq[t] = (tile * cos + swap_halves(tile) * sin).astype(BF16)
    qbuf[c] = sendq[c]
    q_copies = []
    for o in range(1, 8):
        to = lax.rem(c + o, 8)
        copy = remote(sendq.at[to], qbuf.at[c], sq.at[o], rq.at[o], (e, to, d))
        copy.start()
        q_copies.append(copy)
    for copy in valid_copies + kv_copies + q_copies:
        copy.wait_recv()

    bulk.lines(2)

    def chunk(i, _):
        b = lax.rem(c + 1 + i, 8)
        queries = (stack_heads(qbuf[b].astype(F32), False) * (HEAD**-0.5)).astype(BF16)

        def update(carry, block, scores):
            top, total, acc = carry
            new_top = jnp.maximum(top, jnp.max(scores, axis=1, keepdims=True))
            weights = jnp.exp(scores - new_top)
            shrink = jnp.exp(top - new_top)
            total = total * shrink + jnp.sum(weights, axis=1, keepdims=True)
            acc = acc * shrink + mm(weights.astype(BF16), block)
            return (new_top, total, acc)

        def keys(k, carry):
            block = kvbuf[pl.ds(2 * k, 2)].reshape(256, 128)
            return update(carry, block, mm_nt(queries, block) + key_bias(vbuf, k))

        zero = jnp.zeros((256, 1), F32)
        carry = lax.fori_loop(0, b, keys, (zero + NEG, zero, jnp.zeros((256, 128), F32)))
        block = kvbuf[pl.ds(2 * b, 2)].reshape(256, 128)
        scores = mm_nt(queries, block)
        scores = jnp.where(diagonal(d), scores, scores + key_bias(vbuf, b))
        top, total, acc = update(carry, block, scores)
        acc = acc / total
        lse[b] = jnp.broadcast_to(top + jnp.log(total), (256, 128))
        merged = jnp.where(lo, pltpu.roll(acc[:128], 64, 1), acc[128:])
        oheads[b] = merged
        osend[b] = merged.astype(BF16)

        @pl.when(b != c)
        def _():
            remote(osend.at[b], att.at[c], so.at[b], ro.at[c], (e, b, d)).start()

        @pl.when(b == c)
        def _():
            att[c] = osend[c]

        return 0

    lax.fori_loop(0, 4, chunk, 0)
    bulk.lines_on(2)
    lax.fori_loop(4, 8, chunk, 0)
    line_gather_finish(out_gather, lambda i: wall.at[i, :, pl.ds(2048, 1024)], swo, rwo)
    store = pltpu.make_async_copy(wall, wall_out, wall_sem)
    store.start()

    def wait_rest(i, _):
        b = lax.rem(c + 1 + i, 8)
        copy = remote(osend.at[b], att.at[b], so.at[b], ro.at[b], (e, b, d))
        copy.wait_send()
        copy.wait_recv()
        return 0

    lax.fori_loop(0, 7, wait_rest, 0)
    for j in range(3, 6):
        bulk.lines(j)
    attx[me] = att[me]
    for o in range(1, 8):
        to = lax.rem(me + o, 8)
        copy = remote(att.at[to], attx.at[me], sax.at[o], rax.at[o], (to, c, d))
        copy.start()
        nx_copies.append(copy)
    attended = jnp.concatenate([att[t] for t in range(8)], axis=1)
    res = tokens[...].astype(F32) + mm(attended, wall[:, :, 2048:3072].reshape(1024, 1024))
    residual[...] = res
    mid = (res * inverse_rms(res) * gain_row(gains, 2)).astype(BF16)
    low[...] = mid
    xall[me] = mid
    mid_gather = line_gather_start(low, lambda i: xall.at[i], sx, rx)
    logits = mm_nt(router_rows(small_all[...]), mid)
    terms = jnp.exp(logits - jnp.max(logits, axis=0, keepdims=True))
    probs = terms / jnp.sum(terms, axis=0, keepdims=True)
    ids = lax.broadcasted_iota(jnp.int32, (32, 128), 0)
    picks = jnp.zeros((32, 128), F32)
    for k in range(TOP):
        picks = picks + (ids == routes[k : k + 1, :]).astype(F32)
    before = lax.broadcasted_iota(jnp.int32, (128, 128), 0) < lax.broadcasted_iota(jnp.int32, (128, 128), 1)
    slots = mm(picks.astype(BF16), before.astype(F32).astype(BF16))
    slots = jnp.where(picks > 0.0, slots, -1.0)
    probs_out[...] = probs
    picks_out[...] = picks
    gates = probs * picks
    for i in range(8):
        metasend[i, 0:4, :] = gates[4 * i : 4 * i + 4, :]
        metasend[i, 4:8, :] = slots[4 * i : 4 * i + 4, :]
    meta[me] = metasend[me]
    meta_copies = []
    for o in range(1, 8):
        to = lax.rem(me + o, 8)
        copy = remote(metasend.at[to], meta.at[me], sm.at[o], rm.at[o], (to, c, d))
        copy.start()
        meta_copies.append(copy)
    bulk.lines_on(3)
    line_gather_finish(mid_gather, lambda i: xall.at[i], sx, rx)
    for copy in meta_copies:
        copy.wait()
    bulk.lines_on(4)
    bulk.lines_on(5)
    bulk.finish()
    for copy in nx_copies:
        copy.wait()
    for copy in valid_copies + kv_copies + q_copies:
        copy.wait_send()
    store.wait()


def front(tokens, wq, wk, wv, wo, small, ew, valid, cosine, sine, routes):
    vm = pl.BlockSpec(memory_space=pltpu.VMEM)
    hbm = pl.BlockSpec(memory_space=pl.ANY)
    sems = pltpu.SemaphoreType.DMA
    shape = jax.ShapeDtypeStruct
    return pl.pallas_call(
        front_kernel,
        out_shape=(
            shape((12, 2, 4, 2, 64, 512), BF16),
            shape((8, 128, 3072), BF16),
            shape((8, 48, 128), BF16),
            shape((16, 8, 128), F32),
            shape((16, 128, 128), BF16),
            shape((8, 128, 128), BF16),
            shape((8, 128, 128), F32),
            shape((8, 256, 128), F32),
            shape((8, 128, 128), BF16),
            shape((128, 1024), F32),
            shape((8, 128, 128), BF16),
            shape((128, 1024), F32),
            shape((128, 512), F32),
            shape((8, 128, 1024), BF16),
            shape((8, 8, 128), F32),
            shape((32, 128), F32),
            shape((32, 128), F32),
            shape((8, 128, 128), BF16),
            shape((8, 128, 128), BF16),
        ),
        in_specs=[vm, hbm, hbm, hbm, hbm, vm, hbm, vm, vm, vm, vm],
        out_specs=(hbm, hbm) + (vm,) * 17,
        scratch_shapes=[
            pltpu.VMEM((8, 128, 3072), BF16),
            pltpu.VMEM((8, 128, 128), BF16),
            pltpu.VMEM((8, 128, 128), BF16),
            pltpu.VMEM((8, 128, 128), BF16),
            pltpu.VMEM((128, 1024), BF16),
            pltpu.VMEM((8, 8, 128), F32),
            sems((4,)), sems(()), sems(()),
            sems((8,)), sems((8,)), sems((8,)), sems((8,)), sems((8,)), sems((8,)),
            sems((16,)), sems((16,)),
            sems((56,)), sems((56,)), sems((8,)), sems((8,)), sems((8,)), sems((8,)),
            sems((16,)), sems((16,)),
            sems((8,)), sems((8,)), sems((8,)), sems((8,)), sems((8,)), sems((8,)), sems((8,)), sems((8,)),
        ],
        compiler_params=pltpu.CompilerParams(
            collective_id=0, has_side_effects=True, vmem_limit_bytes=48 << 20
        ),
        cost_estimate=pl.CostEstimate(flops=3 * 10**9, bytes_accessed=30 << 20, transcendentals=3 << 20),
        name="front",
    )(tokens, wq, wk, wv, wo, small, ew, valid, cosine, sine, routes)


def plane_peer(o):
    e, c, d = lax.axis_index("expert"), lax.axis_index("ctx"), lax.axis_index("dp")
    q = lax.rem(c * 2 + d + o, 16)
    return q, (e, lax.div(q, 2), lax.rem(q, 2))


def plane_sum_send(pieces, n, inbox, send, recv):
    copies = []
    for o in range(1, 16):
        q, device = plane_peer(o)
        copy = remote(pieces.at[pl.ds(q * n, n)], inbox.at[o], send.at[o], recv.at[o], device)
        copy.start()
        copies.append(copy)
    return copies


def plane_sum_share(copies, pieces, n, inbox, result, send, recv):
    p = lax.axis_index("ctx") * 2 + lax.axis_index("dp")
    total = pieces[pl.ds(p * n, n)].astype(F32)
    for at, copy in enumerate(copies):
        copy.wait_recv()
        total = total + inbox[at + 1].astype(F32)
    result[pl.ds(p * n, n)] = total.astype(BF16)
    shares = []
    view = result.at[pl.ds(p * n, n)]
    for o in range(1, 16):
        _, device = plane_peer(o)
        copy = remote(view, view, send.at[o], recv.at[o], device)
        copy.start()
        shares.append(copy)
    return shares


def rms_back(values, inverse, grad):
    hat = values * inverse
    return inverse * (grad - hat * jnp.mean(grad * hat, axis=1, keepdims=True))


class PlaneScatter:
    def __init__(self, dw, own, near, far_in, near_in, far2_in, near2_in, load, send, recv):
        self.dw, self.own, self.near, self.far_in, self.near_in = dw, own, near, far_in, near_in
        self.far2_in, self.near2_in, self.load, self.send, self.recv = far2_in, near2_in, load, send, recv
        self.y, self.z = yz()
        self.copies = {}
        self.loads = []

    def go(self, n, src, dst, device):
        copy = remote(src, dst, self.send.at[n], self.recv.at[n], device)
        copy.start()
        self.copies[n] = copy

    def block(self, half, m, at):
        if half == 0:
            return self.dw.at[m, lax.div(at, 2), :, lax.rem(at, 2)]
        return self.dw.at[6 + m, :, at]

    def all_blocks(self, half, at):
        if half == 0:
            return self.dw.at[pl.ds(0, 6), lax.div(at, 2), :, lax.rem(at, 2)]
        return self.dw.at[pl.ds(6, 6), :, at]

    def due(self, half, m, at):
        if half == 0:
            return self.own[0].at[m, at]
        return self.own[1].at[m, lax.div(at, 2), lax.rem(at, 2)]

    def device(self, half, at):
        return plane_device(self.y, at) if half == 0 else plane_device(at, self.z)

    def place(self, half):
        return self.z if half == 0 else self.y

    def loads_start(self):
        for half in range(2):
            me = self.place(half)
            spots = [(self.own[half], me)] + [(self.near[half].at[i], lax.rem(me + o, 4)) for i, o in enumerate((1, 3))]
            for n, (ref, at) in enumerate(spots):
                copy = pltpu.make_async_copy(self.all_blocks(half, at), ref, self.load.at[3 * half + n])
                copy.start()
                self.loads.append(copy)

    def far(self, j):
        for half in range(2):
            me = self.place(half)
            far = lax.rem(me + 2, 4)
            for i, o in enumerate((1, 3)):
                view = self.block(half, j, far)
                view = view.at[pl.ds(2 * i, 2)] if half == 0 else view.at[i]
                dst = self.far_in.at[half, i, j]
                self.go(8 * j + 2 * half + i, view, dst, self.device(half, lax.rem(me + o, 4)))

    def near_out(self, j):
        for half in range(2):
            me = self.place(half)
            for i, o in enumerate((1, 3)):
                self.copies[8 * j + 2 * half + i].wait_recv()
                part = self.near[0].at[i, j, pl.ds(2 * i, 2)] if half == 0 else self.near[1].at[i, j, i]
                part[...] = (part[...].astype(F32) + self.far_in[half, i, j].astype(F32)).astype(BF16)
                self.go(
                    8 * j + 4 + 2 * half + i, self.near[half].at[i, j], self.near_in[half].at[i, j],
                    self.device(half, lax.rem(me + o, 4)),
                )

    def near_sum(self, j):
        for half in range(2):
            for i in range(2):
                self.copies[8 * j + 4 + 2 * half + i].wait_recv()
            own, near_in = self.own[half], self.near_in[half]
            own[j] = (own[j].astype(F32) + near_in[0, j].astype(F32) + near_in[1, j].astype(F32)).astype(BF16)

    def place2(self, half):
        return self.y if half == 0 else self.z

    def device2(self, half, at):
        return plane_device(at, self.z) if half == 0 else plane_device(self.y, at)

    def far2(self):
        for half in range(2):
            me = self.place2(half)
            for i, o in enumerate((1, 3)):
                view = self.due(half, pl.ds(0, 6), lax.rem(me + 2, 4)).at[:, pl.ds(32 * i, 32)]
                self.go(48 + 2 * half + i, view, self.far2_in.at[half, i], self.device2(half, lax.rem(me + o, 4)))

    def near2(self):
        for half in range(2):
            me = self.place2(half)
            for i, o in enumerate((1, 3)):
                self.copies[48 + 2 * half + i].wait_recv()
                to = lax.rem(me + o, 4)

                def add(m, _):
                    part = self.due(half, m, to).at[pl.ds(32 * i, 32)]
                    part[...] = (part[...].astype(F32) + self.far2_in[half, i, m].astype(F32)).astype(BF16)
                    return 0

                lax.fori_loop(0, 6, add, 0)
                self.go(52 + 2 * half + i, self.due(half, pl.ds(0, 6), to), self.near2_in.at[half, i], self.device2(half, to))

    def finish(self, result):
        for half in range(2):
            me = self.place2(half)
            for i in range(2):
                self.copies[52 + 2 * half + i].wait_recv()

            def add(m, _):
                result[6 * half + m] = (
                    self.due(half, m, me)[...].astype(F32)
                    + self.near2_in[half, 0, m].astype(F32)
                    + self.near2_in[half, 1, m].astype(F32)
                )
                return 0

            lax.fori_loop(0, 6, add, 0)

    def drain(self):
        for copy in self.copies.values():
            copy.wait_send()


def back_kernel(
    dw, wall_hbm, small_in, vbuf, kvbuf, qbuf, oheads, lse, att, residual, normed_t, qpre, kpre, xall,
    probs_in, picks_in, nx, attx, err, stats, dmid_in, dgates, tokens, cosine, sine,
    gw, gtok, gq, gk, gv, gout, gsmall,
    wall, own_a, own_b, near_a, near_b, wfar_in, near_in_a, near_in_b, wfar2_in, wnear2_in,
    dsend, dattbuf, qpad, dop, delta, dqacc, dkvsend, dqsend, dqbuf, dkvbuf, dqkv, dnorm, dlog,
    dball, dqall, low, smsend, sminbox, smsum, small,
    pieces_o, pin_o, res_o, pieces_n, pin_n, res_n,
    wall_sem, wload, sw, rw, sd, rd, sdq, rdq, sdkv, rdkv,
    so, ro, sn, rn, ssm, rsm, sp1, rp1, sp2, rp2, sp3, rp3, sp4, rp4, sp5, rp5,
):
    x, core, c, d = places()
    me = x * 2 + core
    p = c * 2 + d
    y, z = yz()
    zh, zl = lax.div(z, 2), lax.rem(z, 2)
    e = lax.axis_index("expert")
    wall_load = pltpu.make_async_copy(wall_hbm, wall, wall_sem)
    wall_load.start()
    bulk = PlaneScatter(
        dw, (own_a, own_b), (near_a, near_b), wfar_in, (near_in_a, near_in_b), wfar2_in, wnear2_in, wload, sw, rw
    )
    bulk.loads_start()
    greet_all()
    for j in range(2):
        bulk.far(j)

    gains = small_in[...].astype(F32)
    lo = low_lanes()
    probs = probs_in[...]
    dprobs = jnp.concatenate([dgates[i, 0:4, :] for i in range(8)], axis=0) * picks_in[...]
    dlogits = probs * (dprobs - jnp.sum(probs * dprobs, axis=0, keepdims=True))
    high = dlogits.astype(BF16)
    rest = (dlogits - high.astype(F32)).astype(BF16)
    dlog[0:32, :] = high
    dlog[32:64, :] = rest

    def router_back(i, _):
        at = pl.ds(pl.multiple_of(128 * i, 128), 128)
        part = mm(dlog[...], xall[me, :, at])
        smsend[i, 16:48, :] = part[:32] + part[32:]
        router = small_in[i, 16:48, :]
        dnorm[i] = mm_tn(dlog[...], jnp.concatenate([router, router], axis=0))
        return 0

    lax.fori_loop(0, 8, router_back, 0)
    dmid = dmid_in[...] + jnp.concatenate([dnorm[i] for i in range(8)], axis=1)
    res = residual[...]
    res_inv = inverse_rms(res)
    dgain_mid = jnp.sum(dmid * (res * res_inv), axis=0, keepdims=True)
    dres = err[...] + rms_back(res, res_inv, dmid * gain_row(gains, 2))
    dbranch = dres.astype(BF16)
    gtok[...] = dres
    wall_load.wait()
    dqkv[:, 0:1024] = dbranch
    low[...] = dbranch
    dball[me] = dbranch
    branch_gather = line_gather_start(low, lambda i: dball.at[i], so, ro)

    def attended_back(t, _):
        dsend[t] = mm_nt(dqkv[:, 0:1024], wall[t, :, 2048:3072]).astype(BF16)
        return 0

    lax.fori_loop(0, 8, attended_back, 0)
    dattbuf[c] = dsend[c]
    d_copies = []
    for o in range(1, 8):
        to = lax.rem(c + o, 8)
        copy = remote(dsend.at[to], dattbuf.at[c], sd.at[o], rd.at[o], (e, to, d))
        copy.start()
        d_copies.append(copy)

    def prepare(b, _):
        qpad[b] = (stack_heads(qbuf[b].astype(F32), False) * (HEAD**-0.5)).astype(BF16)
        return 0

    lax.fori_loop(0, 8, prepare, 0)
    for copy in d_copies:
        copy.wait_recv()

    for copy in bulk.loads:
        copy.wait()
    for j in range(2, 4):
        bulk.far(j)
    for j in range(2):
        bulk.near_out(j)

    def prepare_back(b, _):
        tile = dattbuf[b].astype(F32)
        dop[b] = stack_heads(tile, True).astype(BF16)
        both = tile * oheads[b]
        first = jnp.sum(jnp.where(lo, both, 0.0), axis=1, keepdims=True)
        second = jnp.sum(jnp.where(lo, 0.0, both), axis=1, keepdims=True)
        delta[b] = jnp.broadcast_to(jnp.concatenate([first, second], axis=0), (256, 128))
        dqacc[b] = jnp.zeros((256, 128), F32)
        return 0

    lax.fori_loop(0, 8, prepare_back, 0)

    def key_block(k, _):
        block = kvbuf[pl.ds(2 * k, 2)].reshape(256, 128)
        bias = key_bias(vbuf, k)

        def one(b, acc, scores):
            weights = jnp.exp(scores - lse[b][:, 0:1])
            dweights = mm_nt(dop[b], block)
            dscores = (weights * (dweights - delta[b][:, 0:1])).astype(BF16)
            dqacc[b] = dqacc[b] + mm(dscores, block)
            return acc + mm_tn(weights.astype(BF16), dop[b]) + mm_tn(dscores, qpad[b])

        scores = mm_nt(qpad[k], block)
        acc = one(k, jnp.zeros((256, 128), F32), jnp.where(diagonal(d), scores, scores + bias))
        acc = lax.fori_loop(k + 1, 8, lambda b, acc: one(b, acc, mm_nt(qpad[b], block) + bias), acc)
        dkvsend[pl.ds(2 * k, 2)] = acc.astype(BF16).reshape(2, 128, 128)
        done = dqacc[k] * (HEAD**-0.5)
        dqsend[k] = jnp.where(lo, done[:128], pltpu.roll(done[128:], 64, 1)).astype(BF16)

        @pl.when(k != c)
        def _():
            remote(dqsend.at[k], dqbuf.at[c], sdq.at[k], rdq.at[c], (e, k, d)).start()
            remote(dkvsend.at[2 * k], dkvbuf.at[p], sdkv.at[2 * k], rdkv.at[p], (e, k, 0)).start()
            remote(dkvsend.at[2 * k + 1], dkvbuf.at[p], sdkv.at[2 * k + 1], rdkv.at[p], (e, k, 1)).start()

        @pl.when(k == c)
        def _():
            dqbuf[c] = dqsend[c]
            dkvbuf[p] = dkvsend[p]
            other = c * 2 + 1 - d
            remote(dkvsend.at[other], dkvbuf.at[p], sdkv.at[other], rdkv.at[p], (e, c, 1 - d)).start()

        return 0

    lax.fori_loop(0, 8, key_block, 0)
    line_gather_finish(branch_gather, lambda i: dball.at[i], so, ro)

    def wait_dq(i, _):
        b = lax.rem(c + 1 + i, 8)
        copy = remote(dqsend.at[b], dqbuf.at[b], sdq.at[b], rdq.at[b], (e, b, d))
        copy.wait_send()
        copy.wait_recv()
        return 0

    def wait_dkv(i, _):
        q = lax.rem(p + 1 + i, 16)
        copy = remote(dkvsend.at[q], dkvbuf.at[q], sdkv.at[q], rdkv.at[q], (e, lax.div(q, 2), lax.rem(q, 2)))
        copy.wait_send()
        copy.wait_recv()
        return 0

    lax.fori_loop(0, 7, wait_dq, 0)
    lax.fori_loop(0, 15, wait_dkv, 0)
    cos, sin = cosine[...], -sine[...]
    dq = jnp.concatenate([dqbuf[t] for t in range(8)], axis=1).astype(F32)
    dq = jnp.concatenate(
        [dq[:, 128 * t : 128 * t + 128] * cos + swap_halves(dq[:, 128 * t : 128 * t + 128]) * sin for t in range(8)], axis=1
    )
    q_pre = qpre[...]
    q_inv = inverse_rms(q_pre)
    dgain_q = jnp.sum(dq * (q_pre * q_inv), axis=0, keepdims=True)
    dqkv[:, 0:1024] = rms_back(q_pre, q_inv, dq * gain_row(gains, 1)).astype(BF16)
    dk_tiles, dv_tiles = [], []
    for t in range(4):
        even = dkvbuf[4 * t].astype(F32) + dkvbuf[4 * t + 1].astype(F32)
        odd = dkvbuf[4 * t + 2].astype(F32) + dkvbuf[4 * t + 3].astype(F32)
        tile = jnp.where(lo, even, pltpu.roll(odd, 64, 1))
        dk_tiles.append(tile * cos + swap_halves(tile) * sin)
        dv_tiles.append(jnp.where(lo, pltpu.roll(even, 64, 1), odd))
    dk = jnp.concatenate(dk_tiles, axis=1)
    k_pre = kpre[...]
    k_inv = inverse_rms(k_pre)
    dgain_k = jnp.sum(dk * (k_pre * k_inv), axis=0, keepdims=True)
    dqkv[:, 1024:1536] = rms_back(k_pre, k_inv, dk * key_gain_row(gains)).astype(BF16)
    dqkv[:, 1536:2048] = jnp.concatenate(dv_tiles, axis=1).astype(BF16)
    dqall[me] = dqkv[...]
    dqkv_gather = line_gather_start(dqkv, lambda i: dqall.at[i], sn, rn)
    for j in range(2, 6):
        if j >= 4:
            bulk.far(j)
    for j in range(2, 4):
        bulk.near_out(j)

    def out_grad(t, _):
        at = pl.ds(pl.multiple_of(128 * t, 128), 128)
        tile = mm_tn(attx[...].reshape(1024, 128), dball[:, :, at].reshape(1024, 128)).astype(BF16)
        pieces_o[pl.ds(2 * t, 2)] = tile.reshape(2, 64, 128)
        return 0

    lax.fori_loop(0, 8, out_grad, 0)

    p_copies_o = plane_sum_send(pieces_o, 1, pin_o, sp1, rp1)

    def normed_back(t, _):
        dnorm[t] = mm_nt(dqkv[...], wall[t, :, 0:2048])
        return 0

    lax.fori_loop(0, 8, normed_back, 0)
    dnormed = jnp.concatenate([dnorm[t] for t in range(8)], axis=1)
    values = tokens[...].astype(F32)
    inv = inverse_rms(values)
    dgain_in = jnp.sum(dnormed * (values * inv), axis=0, keepdims=True)
    gtok[...] = gtok[...] + rms_back(values, inv, dnormed * gain_row(gains, 0))
    for i in range(8):
        at = slice(128 * i, 128 * i + 128)
        smsend[i, 0:1, :] = dgain_in[:, at]
        smsend[i, 1:2, :] = dgain_q[:, at]
        smsend[i, 2:3, :] = dgain_mid[:, at]
        half = dgain_k[:, 128 * (i // 2) : 128 * (i // 2) + 128]
        smsend[i, 3:4, :] = half if i % 2 == 0 else pltpu.roll(jnp.broadcast_to(half, (8, 128)), 64, 1)[0:1]
        smsend[i, 4:6, :] = stats[0:2, :]
        smsend[i, 6:16, :] = jnp.zeros((10, 128), F32)
    sm_copies = []
    for o in range(1, 8):
        to = lax.rem(me + o, 8)
        copy = remote(smsend.at[to], sminbox.at[o], ssm.at[o], rsm.at[o], (to, c, d))
        copy.start()
        sm_copies.append(copy)

    for j in range(4, 6):
        bulk.near_out(j)
    for j in range(4):
        bulk.near_sum(j)
    shares_o = plane_sum_share(p_copies_o, pieces_o, 1, pin_o, res_o, sp2, rp2)
    total = smsend[me]
    for at, copy in enumerate(sm_copies):
        copy.wait_recv()
        total = total + sminbox[at + 1]
    smsum[...] = total
    small_copies = []
    for o in range(1, 16):
        _, device = plane_peer(o)
        copy = remote(smsum, small.at[o], sp5.at[o], rp5.at[o], device)
        copy.start()
        small_copies.append(copy)
    line_gather_finish(dqkv_gather, lambda i: dqall.at[i], sn, rn)

    def qkv_grad(t, _):
        at = pl.ds(pl.multiple_of(128 * t, 128), 128)
        tile = mm_tn(nx[...].reshape(1024, 128), dqall[:, :, at].reshape(1024, 128)).astype(BF16)
        pieces_n[pl.ds(2 * t, 2)] = tile.reshape(2, 64, 128)
        return 0

    lax.fori_loop(0, 16, qkv_grad, 0)
    p_copies_n = plane_sum_send(pieces_n, 2, pin_n, sp3, rp3)
    for j in range(4, 6):
        bulk.near_sum(j)
    bulk.far2()
    for copy in shares_o:
        copy.wait_recv()
    for t in range(8):
        gout[:, 128 * t : 128 * t + 128] = jnp.concatenate([res_o[2 * t], res_o[2 * t + 1]], axis=0).astype(F32)
    bulk.near2()
    shares_n = plane_sum_share(p_copies_n, pieces_n, 2, pin_n, res_n, sp4, rp4)
    for at, copy in enumerate(small_copies):
        copy.wait_recv()
        total = total + small[at + 1]
    gsmall[...] = total
    bulk.finish(gw)
    for copy in shares_n:
        copy.wait_recv()
    for t in range(16):
        tile = jnp.concatenate([res_n[2 * t], res_n[2 * t + 1]], axis=0).astype(F32)
        if t < 8:
            gq[:, 128 * t : 128 * t + 128] = tile
        elif t < 12:
            gk[:, 128 * (t - 8) : 128 * (t - 8) + 128] = tile
        else:
            gv[:, 128 * (t - 12) : 128 * (t - 12) + 128] = tile
    bulk.drain()
    for copy in d_copies + sm_copies + small_copies + p_copies_o + p_copies_n + shares_o + shares_n:
        copy.wait_send()


def back(*args):
    vm = pl.BlockSpec(memory_space=pltpu.VMEM)
    hbm = pl.BlockSpec(memory_space=pl.ANY)
    sems = pltpu.SemaphoreType.DMA
    shape = jax.ShapeDtypeStruct
    return pl.pallas_call(
        back_kernel,
        out_shape=(
            shape((12, 64, 512), F32),
            shape((128, 1024), F32),
            shape((128, 1024), F32),
            shape((128, 512), F32),
            shape((128, 512), F32),
            shape((128, 1024), F32),
            shape((48, 128), F32),
        ),
        in_specs=[hbm, hbm] + [vm] * 23,
        out_specs=(vm,) * 7,
        scratch_shapes=[
            pltpu.VMEM((8, 128, 3072), BF16),
            pltpu.VMEM((6, 4, 64, 512), BF16),
            pltpu.VMEM((6, 2, 2, 64, 512), BF16),
            pltpu.VMEM((2, 6, 4, 64, 512), BF16),
            pltpu.VMEM((2, 6, 2, 2, 64, 512), BF16),
            pltpu.VMEM((2, 2, 6, 2, 64, 512), BF16),
            pltpu.VMEM((2, 6, 4, 64, 512), BF16),
            pltpu.VMEM((2, 6, 2, 2, 64, 512), BF16),
            pltpu.VMEM((2, 2, 6, 32, 512), BF16),
            pltpu.VMEM((2, 2, 6, 64, 512), BF16),
            pltpu.VMEM((8, 128, 128), BF16),
            pltpu.VMEM((8, 128, 128), BF16),
            pltpu.VMEM((8, 256, 128), BF16),
            pltpu.VMEM((8, 256, 128), BF16),
            pltpu.VMEM((8, 256, 128), F32),
            pltpu.VMEM((8, 256, 128), F32),
            pltpu.VMEM((16, 128, 128), BF16),
            pltpu.VMEM((8, 128, 128), BF16),
            pltpu.VMEM((8, 128, 128), BF16),
            pltpu.VMEM((16, 128, 128), BF16),
            pltpu.VMEM((128, 2048), BF16),
            pltpu.VMEM((8, 128, 128), F32),
            pltpu.VMEM((64, 128), BF16),
            pltpu.VMEM((8, 128, 1024), BF16),
            pltpu.VMEM((8, 128, 2048), BF16),
            pltpu.VMEM((128, 1024), BF16),
            pltpu.VMEM((8, 48, 128), F32),
            pltpu.VMEM((8, 48, 128), F32),
            pltpu.VMEM((48, 128), F32),
            pltpu.VMEM((16, 48, 128), F32),
            pltpu.VMEM((16, 64, 128), BF16),
            pltpu.VMEM((16, 1, 64, 128), BF16),
            pltpu.VMEM((16, 64, 128), BF16),
            pltpu.VMEM((32, 64, 128), BF16),
            pltpu.VMEM((16, 2, 64, 128), BF16),
            pltpu.VMEM((32, 64, 128), BF16),
            sems(()), sems((6,)), sems((56,)), sems((56,)),
            sems((8,)), sems((8,)), sems((8,)), sems((8,)), sems((16,)), sems((16,)),
            sems((8,)), sems((8,)), sems((8,)), sems((8,)), sems((8,)), sems((8,)),
        ] + [sems((16,))] * 10,
        compiler_params=pltpu.CompilerParams(
            collective_id=2, has_side_effects=True, vmem_limit_bytes=60 << 20
        ),
        cost_estimate=pl.CostEstimate(flops=6 * 10**9, bytes_accessed=60 << 20, transcendentals=3 << 20),
        name="back",
    )(*args)


def per_device(
    tokens,
    norm_in,
    w_query,
    w_key,
    w_value,
    query_gain,
    key_gain,
    w_out,
    norm_mid,
    w_router,
    expert_gate,
    expert_up,
    expert_down,
    routes,
    valid,
    teacher,
):
    positions = (lax.axis_index("ctx") * 2 + lax.axis_index("dp")) * 128 + jnp.arange(128, dtype=jnp.int32)
    frequency = THETA ** (-(jnp.arange(HEAD // 2).astype(F32) * (2.0 / HEAD)))
    angles = positions.astype(F32)[:, None] * frequency[None, :]
    cos, sin = jnp.cos(angles), jnp.sin(angles)
    cosine = jnp.concatenate([cos, cos, cos, cos], axis=1)
    sine = jnp.concatenate([-sin, sin, -sin, sin], axis=1)
    rows = jnp.stack([norm_in, query_gain, norm_mid, jnp.concatenate([key_gain, key_gain])])
    small = jnp.concatenate([rows, jnp.zeros((12, 128), BF16), w_router.T], axis=0)
    ew = jnp.concatenate([jnp.transpose(w, (1, 0, 2)) for w in (expert_gate, expert_up, expert_down)], axis=0)
    valid_rows = jnp.broadcast_to(valid.astype(F32)[None, :], (8, 128))
    (
        wg, wall, small_all, vbuf, kvbuf, qbuf, oheads, lse, att, residual, normed_t, qpre, kpre, xall, meta, probs, picks,
        nx, attx,
    ) = front(tokens, w_query, w_key, w_value, w_out, small, ew, valid_rows, cosine, sine, routes.T)
    mixed, err, stats, dw, dmid, dgates = moe(
        wg.reshape(12, 1024, 512), xall, meta, residual, teacher, valid_rows
    )
    gw, gtok, gq, gk, gv, gout, gsmall = back(
        dw.reshape(12, 2, 4, 2, 64, 512), wall, small_all, vbuf, kvbuf, qbuf, oheads, lse, att, residual, normed_t,
        qpre, kpre, xall, probs, picks, nx, attx, err, stats, dmid, dgates, tokens, cosine, sine,
    )
    loss = gsmall[4, 0] / (gsmall[5, 0] * 1024.0)
    grad_gate, grad_up, grad_down = [jnp.transpose(gw[4 * m : 4 * m + 4], (1, 0, 2)) for m in range(3)]
    return (
        mixed, loss, gtok, gsmall[0], gq, gk, gv, gsmall[1], gsmall[3, :64], gout, gsmall[2], gsmall[16:48].T,
        grad_gate, grad_up, grad_down,
    )


def solution(mesh):
    placed = (
        P(("expert", "ctx", "dp"), None),
        P("expert"),
        P("expert", None),
        P("expert", None),
        P("expert", None),
        P("expert"),
        P("expert"),
        P("expert", None),
        P("expert"),
        P("expert", None),
        P(("ctx", "dp"), "expert", None),
        P(("ctx", "dp"), "expert", None),
        P(("ctx", "dp"), "expert", None),
        P(("expert", "ctx", "dp"), None),
        P(("expert", "ctx", "dp")),
        P(("expert", "ctx", "dp"), None),
    )
    return jax.shard_map(
        per_device,
        mesh=mesh,
        in_specs=placed,
        out_specs=(
            P(("expert", "ctx", "dp"), None),
            P(),
            P(("expert", "ctx", "dp"), None),
            P("expert"),
            P("expert", None),
            P("expert", None),
            P("expert", None),
            P("expert"),
            P("expert"),
            P("expert", None),
            P("expert"),
            P("expert", None),
            P(("ctx", "dp"), "expert", None),
            P(("ctx", "dp"), "expert", None),
            P(("ctx", "dp"), "expert", None),
        ),
        check_vma=False,
    )
```

```python
import jax
import jax.numpy as jnp
from jax import lax
from jax.experimental import pallas as pl
from jax.experimental.pallas import tpu as pltpu
from jax.sharding import PartitionSpec as P

MESH = pl.DeviceIdType.MESH
F32 = jnp.float32
BF16 = jnp.bfloat16

HEAD = 64
TOP = 8
EPS = 1e-06
THETA = 10000.0
NEG = -1e30
SCALE = HEAD**-0.5


def mm(a, b):
    return lax.dot_general(a, b, (((1,), (0,)), ((), ())), preferred_element_type=F32)


def mm_nt(a, b):
    return lax.dot_general(a, b, (((1,), (1,)), ((), ())), preferred_element_type=F32)


def mm_tn(a, b):
    return lax.dot_general(a, b, (((0,), (0,)), ((), ())), preferred_element_type=F32)


def places():
    e, c, d = lax.axis_index("expert"), lax.axis_index("ctx"), lax.axis_index("dp")
    return e // 2, e % 2, c, d


def yz():
    c, d = lax.axis_index("ctx"), lax.axis_index("dp")
    return lax.rem(c, 4), lax.div(c, 4) * 2 + d


def remote(src, dst, send, recv, device):
    return pltpu.make_async_remote_copy(
        src_ref=src, dst_ref=dst, send_sem=send, recv_sem=recv, device_id=device, device_id_type=MESH
    )


def line_device(x, core):
    return (lax.rem(x + 4, 4) * 2 + core, lax.axis_index("ctx"), lax.axis_index("dp"))


def plane_device(y, z):
    return (lax.axis_index("expert"), lax.div(z, 2) * 4 + y, lax.rem(z, 2))


def plane_peer(o):
    e, c, d = lax.axis_index("expert"), lax.axis_index("ctx"), lax.axis_index("dp")
    q = lax.rem(c * 2 + d + o, 16)
    return q, (e, lax.div(q, 2), lax.rem(q, 2))


def greet_all():
    barrier = pltpu.get_barrier_semaphore()
    e, c, d = lax.axis_index("expert"), lax.axis_index("ctx"), lax.axis_index("dp")
    for o in range(1, 8):
        pl.semaphore_signal(barrier, inc=1, device_id=(lax.rem(e + o, 8), c, d), device_id_type=MESH)
    for o in range(1, 16):
        _, device = plane_peer(o)
        pl.semaphore_signal(barrier, inc=1, device_id=device, device_id_type=MESH)
    pl.semaphore_wait(barrier, 22)


def line_gather_start(own, buf, send, recv):
    x, core, _, _ = places()
    me = x * 2 + core
    copies = [remote(own, buf(me), send.at[o], recv.at[o], line_device(x + o, core)) for o in (2, 1, 3)]
    copies.append(remote(own, buf(me), send.at[0], recv.at[0], line_device(x, 1 - core)))
    for copy in copies:
        copy.start()
    return copies


def line_gather_finish(copies, buf, send, recv):
    x, core, _, _ = places()
    forwards = []
    for at, o in ((1, 1), (2, 3), (0, 2)):
        copies[at].wait_recv()
        block = buf(lax.rem(x - o + 4, 4) * 2 + core)
        copy = remote(block, block, send.at[4 + o], recv.at[4 + o], line_device(x, 1 - core))
        copy.start()
        forwards.append(copy)
    copies[3].wait_recv()
    for copy in forwards:
        copy.wait_recv()
    for copy in copies + forwards:
        copy.wait_send()


def line_scatter_send_pair(pair, sib, send, recv):
    x, core, _, _ = places()
    copy = remote(pair, sib, send.at[0], recv.at[0], line_device(x, 1 - core))
    copy.start()
    return copy


def line_scatter_send_x(mine, pair_copy, sib, inbox, send, recv):
    x, core, _, _ = places()
    pair_copy.wait_recv()
    copies = []
    for o in (2, 1, 3):
        to = lax.rem(x + o, 4)
        mine[to] = (mine[to].astype(F32) + sib[to].astype(F32)).astype(mine.dtype)
        copy = remote(mine.at[to], inbox.at[o - 1], send.at[o], recv.at[o], line_device(x + o, core))
        copy.start()
        copies.append(copy)
    return copies


def line_scatter_sum(mine, sib, inbox, copies):
    x, _, _, _ = places()
    total = mine[x].astype(F32) + sib[x].astype(F32)
    for at, o in ((1, 1), (2, 3), (0, 2)):
        copies[at].wait_recv()
        total = total + inbox[o - 1].astype(F32)
    return total


def plane_sum_send(pieces, n, inbox, send, recv):
    copies = []
    for o in range(1, 16):
        q, device = plane_peer(o)
        copy = remote(pieces.at[pl.ds(q * n, n)], inbox.at[o], send.at[o], recv.at[o], device)
        copy.start()
        copies.append(copy)
    return copies


def plane_sum_share(copies, pieces, n, inbox, result, send, recv):
    p = lax.axis_index("ctx") * 2 + lax.axis_index("dp")
    total = pieces[pl.ds(p * n, n)].astype(F32)
    for at, copy in enumerate(copies):
        copy.wait_recv()
        total = total + inbox[at + 1].astype(F32)
    result[pl.ds(p * n, n)] = total.astype(BF16)
    shares = []
    view = result.at[pl.ds(p * n, n)]
    for o in range(1, 16):
        _, device = plane_peer(o)
        copy = remote(view, view, send.at[o], recv.at[o], device)
        copy.start()
        shares.append(copy)
    return shares


class Copies:
    def __init__(self, send, recv):
        self.send, self.recv = send, recv
        self.y, self.z = yz()
        self.copies = {}

    def go(self, n, src, dst, device):
        copy = remote(src, dst, self.send.at[n], self.recv.at[n], device)
        copy.start()
        self.copies[n] = copy

    def drain(self):
        for copy in self.copies.values():
            copy.wait_send()


class PlaneGather(Copies):
    def __init__(self, wg, send, recv):
        super().__init__(send, recv)
        self.wg = wg

    def place(self, m, y, z):
        return self.wg.at[m, lax.div(z, 2), y, lax.rem(z, 2)]

    def shards(self):
        y, z = self.y, self.z
        a, b = pl.ds(0, 6), pl.ds(6, 6)
        for i, o in enumerate((1, 3)):
            view = self.place(a, y, z)
            self.go(i, view, view, plane_device(lax.rem(y + o, 4), z))
            view = self.place(b, y, z)
            self.go(2 + i, view, view, plane_device(y, lax.rem(z + o, 4)))

    def shards_on(self):
        y, z = self.y, self.z
        a, b = pl.ds(0, 6), pl.ds(6, 6)
        for i, o in enumerate((1, 3)):
            rows = pl.ds(32 * i, 32)
            self.copies[i].wait_recv()
            view = self.place(a, lax.rem(y - o + 4, 4), z).at[:, rows]
            self.go(4 + i, view, view, plane_device(lax.rem(y + o, 4), z))
            self.copies[2 + i].wait_recv()
            view = self.place(b, y, lax.rem(z - o + 4, 4)).at[:, rows]
            self.go(6 + i, view, view, plane_device(y, lax.rem(z + o, 4)))

    def shards_wait(self):
        for n in range(4, 8):
            self.copies[n].wait_recv()

    def lines(self, j):
        y, z = self.y, self.z
        for i, o in enumerate((1, 3)):
            view = self.wg.at[j, lax.div(z, 2), :, lax.rem(z, 2)]
            self.go(8 + 8 * j + i, view, view, plane_device(y, lax.rem(z + o, 4)))
            view = self.wg.at[6 + j, :, y]
            self.go(10 + 8 * j + i, view, view, plane_device(lax.rem(y + o, 4), z))

    def lines_on(self, j):
        y, z = self.y, self.z
        for i, o in enumerate((1, 3)):
            self.copies[8 + 8 * j + i].wait_recv()
            from_z = lax.rem(z - o + 4, 4)
            view = self.wg.at[j, lax.div(from_z, 2), pl.ds(2 * i, 2), lax.rem(from_z, 2)]
            self.go(12 + 8 * j + i, view, view, plane_device(y, lax.rem(z + o, 4)))
            self.copies[10 + 8 * j + i].wait_recv()
            view = self.wg.at[6 + j, i, lax.rem(y - o + 4, 4)]
            self.go(14 + 8 * j + i, view, view, plane_device(lax.rem(y + o, 4), z))

    def lines_wait(self, j):
        for n in range(12 + 8 * j, 16 + 8 * j):
            self.copies[n].wait_recv()


class PlaneScatter(Copies):
    def __init__(self, dw, far_in, near_in, far2_in, near2_in, stage, load, send, recv):
        super().__init__(send, recv)
        self.dw, self.far_in, self.near_in = dw, far_in, near_in
        self.far2_in, self.near2_in, self.stage, self.load = far2_in, near2_in, stage, load

    def block(self, half, m, at):
        if half == 0:
            return self.dw.at[m, lax.div(at, 2), :, lax.rem(at, 2)]
        return self.dw.at[6 + m, :, at]

    def due(self, half, m, at):
        if half == 0:
            return self.dw.at[m, lax.div(self.z, 2), at, lax.rem(self.z, 2)]
        return self.dw.at[m, lax.div(at, 2), self.y, lax.rem(at, 2)]

    def device(self, half, at):
        return plane_device(self.y, at) if half == 0 else plane_device(at, self.z)

    def place(self, half):
        return self.z if half == 0 else self.y

    def far(self, j):
        for half in range(2):
            me = self.place(half)
            for i, o in enumerate((1, 3)):
                view = self.block(half, j, lax.rem(me + 2, 4))
                view = view.at[pl.ds(2 * i, 2)] if half == 0 else view.at[i]
                self.go(8 * j + 2 * half + i, view, self.far_in.at[half, i, j], self.device(half, lax.rem(me + o, 4)))

    def near_out(self, j):
        loads = []
        for half in range(2):
            for i in range(2):
                self.copies[8 * j + 2 * half + i].wait_recv()
                spot = self.stage[0].at[i, pl.ds(0, 2)] if half == 0 else self.stage[1].at[i, 0]
                load = pltpu.make_async_copy(self.far_in.at[half, i, j], spot, self.load.at[2 * half + i])
                load.start()
                loads.append((load, spot))
        for half in range(2):
            me = self.place(half)
            for i, o in enumerate((1, 3)):
                load, spot = loads[2 * half + i]
                load.wait()
                to = lax.rem(me + o, 4)
                whole = self.block(half, j, to)
                part = whole.at[pl.ds(2 * i, 2)] if half == 0 else whole.at[i]
                part[...] = (part[...].astype(F32) + spot[...].astype(F32)).astype(BF16)
                self.go(8 * j + 4 + 2 * half + i, whole, self.near_in[half].at[i, j], self.device(half, to))

    def near_load(self, j):
        self.loads = []
        for half in range(2):
            for i in range(2):
                self.copies[8 * j + 4 + 2 * half + i].wait_recv()
                load = pltpu.make_async_copy(
                    self.near_in[half].at[i, j], self.stage[half].at[i], self.load.at[2 * half + i]
                )
                load.start()
                self.loads.append(load)

    def near_sum(self, j):
        self.near_load(j)
        for half in range(2):
            own, stage = self.block(half, j, self.place(half)), self.stage[half]
            self.loads[2 * half].wait()
            self.loads[2 * half + 1].wait()
            own[...] = (own[...].astype(F32) + stage[0].astype(F32) + stage[1].astype(F32)).astype(BF16)

    def place2(self, half):
        return self.y if half == 0 else self.z

    def device2(self, half, at):
        return plane_device(at, self.z) if half == 0 else plane_device(self.y, at)

    def far2(self):
        for half in range(2):
            me = self.place2(half)
            for i, o in enumerate((1, 3)):
                view = self.due(half, pl.ds(6 * half, 6), lax.rem(me + 2, 4)).at[:, pl.ds(32 * i, 32)]
                self.go(48 + 2 * half + i, view, self.far2_in.at[half, i], self.device2(half, lax.rem(me + o, 4)))

    def near2(self):
        for half in range(2):
            me = self.place2(half)
            for i, o in enumerate((1, 3)):
                self.copies[48 + 2 * half + i].wait_recv()
                to = lax.rem(me + o, 4)

                def add(m, _):
                    part = self.due(half, 6 * half + m, to).at[pl.ds(32 * i, 32)]
                    part[...] = (part[...].astype(F32) + self.far2_in[half, i, m].astype(F32)).astype(BF16)
                    return 0

                lax.fori_loop(0, 6, add, 0)
                view = self.due(half, pl.ds(6 * half, 6), to)
                self.go(52 + 2 * half + i, view, self.near2_in.at[half, i], self.device2(half, to))

    def finish(self, result):
        for half in range(2):
            me = self.place2(half)
            for i in range(2):
                self.copies[52 + 2 * half + i].wait_recv()

            def add(m, _):
                result[6 * half + m] = (
                    self.due(half, 6 * half + m, me)[...].astype(F32)
                    + self.near2_in[half, 0, m].astype(F32)
                    + self.near2_in[half, 1, m].astype(F32)
                )
                return 0

            lax.fori_loop(0, 6, add, 0)


def low_lanes():
    return lax.broadcasted_iota(jnp.int32, (128, 128), 1) < 64


def swap_halves(tile):
    lane = lax.rem(lax.broadcasted_iota(jnp.int32, (128, 128), 1), 64)
    return jnp.where(lane < 32, pltpu.roll(tile, 96, 1), pltpu.roll(tile, 32, 1))


def gain_row(small, row):
    return jnp.concatenate([small[i, row : row + 1, :] for i in range(8)], axis=1)


def key_gain_row(small):
    lane = lax.broadcasted_iota(jnp.int32, (1, 128), 1)
    return jnp.concatenate(
        [jnp.where(lane < 64, small[2 * t, 3:4, :], small[2 * t + 1, 3:4, :]) for t in range(4)], axis=1
    )


def router_rows(small):
    return jnp.concatenate([small[i, 16:48, :] for i in range(8)], axis=1)


def inverse_rms(values):
    return lax.rsqrt(jnp.mean(values * values, axis=1, keepdims=True) + EPS)


def rms_back(values, inverse, grad):
    hat = values * inverse
    return inverse * (grad - hat * jnp.mean(grad * hat, axis=1, keepdims=True))


def stack_heads(tile, upper):
    lo = low_lanes()
    turned = pltpu.roll(tile, 64, 1)
    first, second = (turned, tile) if upper else (tile, turned)
    keep = jnp.logical_not(lo) if upper else lo
    return jnp.concatenate([jnp.where(keep, first, 0.0), jnp.where(keep, second, 0.0)], axis=0)


def key_rows(kvbuf, k):
    return kvbuf[pl.ds(4 * k, 4)].reshape(512, 128)


def key_bias(vbuf, k):
    row = jnp.concatenate([vbuf[4 * k + i, 0:1, :] for i in range(4)], axis=1)
    return (row - 1.0) * 1e30


def mask_last(scores, bias, b, d):
    half = lax.rem(b, 2) * 256
    column = lax.broadcasted_iota(jnp.int32, (256, 512), 1)
    row = lax.rem(lax.broadcasted_iota(jnp.int32, (256, 512), 0), 128)
    masked = jnp.where(column < half + 256, scores + bias, NEG)
    return jnp.where(column == row + (half + 128 * d), scores, masked)


def down(e):
    return 4 + e + 4 * lax.div(e, 2)


class Refs:
    def __init__(self, names, refs):
        for name, ref in zip(names, refs, strict=True):
            setattr(self, name, ref)


INPUTS = (
    "tokens", "wq", "wk", "wv", "wo", "norm_in", "query_gain", "norm_mid", "key_gain", "w_router",
    "expert_gate", "expert_up", "expert_down", "valid", "cosine", "sine", "routes", "teacher",
)
OUTPUTS = (
    ("mixed", (128, 1024), BF16),
    ("gtok", (128, 1024), F32),
    ("res_o", (16, 64, 128), BF16),
    ("res_n", (32, 64, 128), BF16),
    ("gsmall", (48, 128), F32),
    ("gw", (12, 64, 512), F32),
)
SPILLS = (
    ("wall_keep", (8, 256, 1024), BF16),
    ("far_in", (2, 2, 6, 2, 64, 512), BF16),
    ("near_in_a", (2, 6, 4, 64, 512), BF16),
    ("near_in_b", (2, 6, 2, 2, 64, 512), BF16),
)
SCRATCH = (
    ("big1", (8, 256, 1024), BF16),
    ("big2", (8, 256, 1024), BF16),
    ("big3", (8, 256, 1024), BF16),
    ("rows", (8, 128, 1024), BF16),
    ("wo_all", (8, 128, 1024), BF16),
    ("wg", (12, 2, 4, 2, 64, 512), BF16),
    ("gbuf", (4, 512, 512), BF16),
    ("ubuf", (4, 512, 512), BF16),
    ("mine", (4, 128, 1024), BF16),
    ("pair", (4, 128, 1024), BF16),
    ("sib", (4, 128, 1024), BF16),
    ("inbox", (3, 128, 1024), BF16),
    ("stage_a", (2, 4, 64, 512), BF16),
    ("stage_b", (2, 2, 2, 64, 512), BF16),
    ("far2_in", (2, 2, 6, 32, 512), BF16),
    ("near2_in", (2, 2, 6, 64, 512), BF16),
    ("small_all", (8, 48, 128), BF16),
    ("vbuf", (16, 8, 128), F32),
    ("kvbuf", (16, 128, 128), BF16),
    ("qbuf", (8, 128, 128), BF16),
    ("oheads", (8, 128, 128), F32),
    ("lse", (8, 256, 128), F32),
    ("att", (8, 128, 128), BF16),
    ("attx", (8, 128, 128), BF16),
    ("normed_t", (8, 128, 128), BF16),
    ("nx", (8, 128, 128), BF16),
    ("sendq", (8, 128, 128), BF16),
    ("osend", (8, 128, 128), BF16),
    ("residual", (128, 1024), F32),
    ("qpre", (128, 1024), F32),
    ("kpre", (128, 512), F32),
    ("midl", (128, 1024), BF16),
    ("low", (128, 1024), BF16),
    ("meta", (8, 8, 128), F32),
    ("metasend", (8, 8, 128), F32),
    ("probs", (32, 128), F32),
    ("picks", (32, 128), F32),
    ("stats", (8, 128), F32),
    ("pcat", (8, 256, 128), BF16),
    ("gslot", (8, 256, 128), F32),
    ("dgates", (8, 8, 128), F32),
    ("dgsend", (8, 8, 128), F32),
    ("dattbuf", (8, 128, 128), BF16),
    ("qpad", (8, 256, 128), BF16),
    ("dop", (8, 256, 128), BF16),
    ("dkvsend", (16, 128, 128), BF16),
    ("dkvbuf", (16, 128, 128), BF16),
    ("dqkv", (256, 1024), BF16),
    ("dnorm", (8, 128, 128), F32),
    ("dlog", (64, 128), BF16),
    ("smsend", (8, 48, 128), F32),
    ("sminbox", (8, 48, 128), F32),
    ("smsum", (48, 128), F32),
    ("smplane", (16, 48, 128), F32),
    ("pieces_o", (16, 64, 128), BF16),
    ("pin_o", (16, 1, 64, 128), BF16),
    ("pieces_n", (32, 64, 128), BF16),
    ("pin_n", (16, 2, 64, 128), BF16),
)
SEMAPHORES = (
    ("own_sem", 6), ("keep_sem", 2), ("teacher_sem", 1), ("load_sem", 4),
    ("ssm", 8), ("rsm", 8), ("sqkv", 8), ("rqkv", 8), ("swo", 8), ("rwo", 8), ("sv", 16), ("rv", 16),
    ("sew", 56), ("rew", 56), ("snx", 8), ("rnx", 8), ("sax", 8), ("rax", 8),
    ("skv", 16), ("rkv", 16), ("sq", 8), ("rq", 8), ("so", 8), ("ro", 8), ("sx", 8), ("rx", 8), ("sm", 8), ("rm", 8),
    ("s1", 4), ("r1", 4), ("s2", 8), ("r2", 8), ("s3", 4), ("r3", 4), ("s4", 8), ("r4", 8),
    ("sw", 56), ("rw", 56), ("sd", 8), ("rd", 8), ("sdq", 8), ("rdq", 8), ("sdkv", 16), ("rdkv", 16),
    ("sb", 8), ("rb", 8), ("sn", 8), ("rn", 8), ("sms", 8), ("rms", 8),
    ("sp1", 16), ("rp1", 16), ("sp2", 16), ("rp2", 16), ("sp3", 16), ("rp3", 16), ("sp4", 16), ("rp4", 16),
    ("sp5", 16), ("rp5", 16),
)
NAMES = INPUTS + tuple(n for part in (OUTPUTS, SPILLS, SCRATCH, SEMAPHORES) for n, *_ in part)


def layer_kernel(*refs):
    r = Refs(NAMES, refs)
    x, core, c, d = places()
    me = x * 2 + core
    p = c * 2 + d
    y, z = yz()
    e_at = lax.axis_index("expert")
    lo = low_lanes()

    wall = r.big1
    own = [
        pltpu.make_async_copy(r.wq, wall.at[me, pl.ds(0, 128)], r.own_sem.at[0]),
        pltpu.make_async_copy(r.wk, wall.at[me, pl.ds(128, 128), pl.ds(0, 512)], r.own_sem.at[1]),
        pltpu.make_async_copy(r.wv, wall.at[me, pl.ds(128, 128), pl.ds(512, 512)], r.own_sem.at[2]),
        pltpu.make_async_copy(r.wo, r.wo_all.at[me], r.own_sem.at[3]),
    ]
    for copy in own:
        copy.start()
    teacher_load = pltpu.make_async_copy(r.teacher, r.gtok, r.teacher_sem.at[0])
    teacher_load.start()
    eye = lax.broadcasted_iota(jnp.int32, (128, 128), 0) == lax.broadcasted_iota(jnp.int32, (128, 128), 1)
    rows = [ref[...].astype(F32).reshape(1, 128) for ref in (r.norm_in, r.query_gain, r.norm_mid)]
    key_row = r.key_gain[...].astype(F32).reshape(1, 64)
    rows += [jnp.concatenate([key_row, key_row], axis=1), jnp.zeros((12, 128), F32), r.w_router[...].astype(F32)]
    r.small_all[me] = jnp.concatenate(rows, axis=0).astype(BF16)
    valid_row = r.valid[...].astype(F32).reshape(1, 128)
    r.vbuf[p] = jnp.broadcast_to(valid_row, (8, 128))
    greet_all()

    gather = PlaneGather(r.wg, r.sew, r.rew)
    small_gather = line_gather_start(r.small_all.at[me], lambda i: r.small_all.at[i], r.ssm, r.rsm)
    for copy in own[:3]:
        copy.wait()
    qkv_gather = line_gather_start(wall.at[me], lambda i: wall.at[i], r.sqkv, r.rqkv)
    for ref, first in ((r.expert_gate, (0, 1, 2, 3)), (r.expert_up, (6, 7, 8, 9)), (r.expert_down, (4, 5, 10, 11))):
        whole = ref[...].astype(F32)
        for e, m in enumerate(first):
            r.wg[m, lax.div(z, 2), y, lax.rem(z, 2)] = whole[:, e, :].astype(BF16)
    gather.shards()
    own[3].wait()
    out_gather = line_gather_start(r.wo_all.at[me], lambda i: r.wo_all.at[i], r.swo, r.rwo)
    valid_copies = []
    for o in range(1, 16):
        _, device = plane_peer(o)
        copy = remote(r.vbuf.at[p], r.vbuf.at[p], r.sv.at[o], r.rv.at[o], device)
        copy.start()
        valid_copies.append(copy)

    line_gather_finish(small_gather, lambda i: r.small_all.at[i], r.ssm, r.rsm)
    gains = r.small_all[...].astype(F32)
    values = r.tokens[...].astype(F32)
    normed = (values * inverse_rms(values) * gain_row(gains, 0)).astype(BF16)
    for t in range(8):
        r.normed_t[t] = normed[:, 128 * t : 128 * t + 128]
    r.nx[me] = r.normed_t[me]
    spread_copies = []
    for o in range(1, 8):
        to = lax.rem(me + o, 8)
        copy = remote(r.normed_t.at[to], r.nx.at[me], r.snx.at[o], r.rnx.at[o], (to, c, d))
        copy.start()
        spread_copies.append(copy)
    gather.shards_on()
    gather.shards_wait()
    for j in range(2):
        gather.lines(j)

    line_gather_finish(qkv_gather, lambda i: wall.at[i], r.sqkv, r.rqkv)
    for j in range(2):
        gather.lines_on(j)
    q_pre = mm(normed, wall[:, 0:128, :].reshape(1024, 1024))
    kv_pre = mm(normed, wall[:, 128:256, :].reshape(1024, 1024))
    k_pre = kv_pre[:, 0:512]
    v_low = kv_pre[:, 512:1024].astype(BF16).astype(F32)
    r.qpre[...] = q_pre
    r.kpre[...] = k_pre
    cos, sin = r.cosine[...], r.sine[...]
    kn = k_pre * inverse_rms(k_pre) * key_gain_row(gains)
    for t in range(4):
        tile = kn[:, 128 * t : 128 * t + 128]
        k_rot = tile * cos + swap_halves(tile) * sin
        v_tile = v_low[:, 128 * t : 128 * t + 128]
        r.dkvsend[2 * t] = jnp.where(lo, k_rot, pltpu.roll(v_tile, 64, 1)).astype(BF16)
        r.dkvsend[2 * t + 1] = jnp.where(lo, pltpu.roll(k_rot, 64, 1), v_tile).astype(BF16)
    r.kvbuf[p] = r.dkvsend[c]
    kv_copies = []
    for o in range(1, 16):
        q, device = plane_peer(o)
        copy = remote(r.dkvsend.at[lax.div(q, 2)], r.kvbuf.at[p], r.skv.at[o], r.rkv.at[o], device)
        copy.start()
        kv_copies.append(copy)
    qn = q_pre * inverse_rms(q_pre) * gain_row(gains, 1)
    for t in range(8):
        tile = qn[:, 128 * t : 128 * t + 128]
        r.sendq[t] = (tile * cos + swap_halves(tile) * sin).astype(BF16)
    r.qbuf[c] = r.sendq[c]
    q_copies = []
    for o in range(1, 8):
        to = lax.rem(c + o, 8)
        copy = remote(r.sendq.at[to], r.qbuf.at[c], r.sq.at[o], r.rq.at[o], (e_at, to, d))
        copy.start()
        q_copies.append(copy)
    keep = pltpu.make_async_copy(wall, r.wall_keep, r.keep_sem.at[0])
    keep.start()
    for copy in valid_copies + kv_copies + q_copies:
        copy.wait()
    gather.lines(2)

    def prepare(b, _):
        r.qpad[b] = (stack_heads(r.qbuf[b].astype(F32), False) * SCALE).astype(BF16)
        return 0

    lax.fori_loop(0, 8, prepare, 0)

    def chunk(i, _):
        b = lax.rem(c + 1 + i, 8)
        queries = r.qpad[b]
        last = lax.div(b, 2)

        def update(carry, block, scores):
            top, total, acc = carry
            new_top = jnp.maximum(top, jnp.max(scores, axis=1, keepdims=True))
            weights = jnp.exp(scores - new_top)
            shrink = jnp.exp(top - new_top)
            total = total * shrink + jnp.sum(weights, axis=1, keepdims=True)
            acc = acc * shrink + mm(weights.astype(BF16), block)
            return (new_top, total, acc)

        def keys(k, carry):
            block = key_rows(r.kvbuf, k)
            return update(carry, block, mm_nt(queries, block) + key_bias(r.vbuf, k))

        zero = jnp.zeros((256, 1), F32)
        carry = lax.fori_loop(0, last, keys, (zero + NEG, zero, jnp.zeros((256, 128), F32)))
        block = key_rows(r.kvbuf, last)
        scores = mask_last(mm_nt(queries, block), key_bias(r.vbuf, last), b, d)
        top, total, acc = update(carry, block, scores)
        acc = acc / total
        r.lse[b] = jnp.broadcast_to(top + jnp.log(total), (256, 128))
        merged = jnp.where(lo, pltpu.roll(acc[:128], 64, 1), acc[128:])
        r.oheads[b] = merged
        r.osend[b] = merged.astype(BF16)

        @pl.when(b != c)
        def _():
            remote(r.osend.at[b], r.att.at[c], r.so.at[b], r.ro.at[c], (e_at, b, d)).start()

        @pl.when(b == c)
        def _():
            r.att[c] = r.osend[c]

        return 0

    lax.fori_loop(0, 4, chunk, 0)
    gather.lines_on(2)
    lax.fori_loop(4, 8, chunk, 0)
    line_gather_finish(out_gather, lambda i: r.wo_all.at[i], r.swo, r.rwo)

    def wait_rest(i, _):
        b = lax.rem(c + 1 + i, 8)
        copy = remote(r.osend.at[b], r.att.at[b], r.so.at[b], r.ro.at[b], (e_at, b, d))
        copy.wait_send()
        copy.wait_recv()
        return 0

    lax.fori_loop(0, 7, wait_rest, 0)
    for j in range(3, 6):
        gather.lines(j)
    r.attx[me] = r.att[me]
    for o in range(1, 8):
        to = lax.rem(me + o, 8)
        copy = remote(r.att.at[to], r.attx.at[me], r.sax.at[o], r.rax.at[o], (to, c, d))
        copy.start()
        spread_copies.append(copy)
    attended = jnp.concatenate([r.att[t] for t in range(8)], axis=1)
    res = r.tokens[...].astype(F32) + mm(attended, r.wo_all[...].reshape(1024, 1024))
    r.residual[...] = res
    mid = (res * inverse_rms(res) * gain_row(gains, 2)).astype(BF16)
    r.midl[...] = mid
    r.rows[me] = mid
    mid_gather = line_gather_start(r.midl, lambda i: r.rows.at[i], r.sx, r.rx)

    logits = mm_nt(router_rows(r.small_all[...]), mid)
    terms = jnp.exp(logits - jnp.max(logits, axis=0, keepdims=True))
    probs = terms / jnp.sum(terms, axis=0, keepdims=True)
    ids = lax.broadcasted_iota(jnp.int32, (32, 128), 0).astype(F32)
    routes = r.routes[...].astype(F32)
    picks = jnp.zeros((32, 128), F32)
    for k in range(TOP):
        picks = picks + (ids == routes[k : k + 1, :]).astype(F32)
    before = lax.broadcasted_iota(jnp.int32, (128, 128), 0) < lax.broadcasted_iota(jnp.int32, (128, 128), 1)
    slots = mm(picks.astype(BF16), before.astype(F32).astype(BF16))
    slots = jnp.where(picks > 0.0, slots, -1.0)
    r.probs[...] = probs
    r.picks[...] = picks
    gates = probs * picks
    for i in range(8):
        r.metasend[i, 0:4, :] = gates[4 * i : 4 * i + 4, :]
        r.metasend[i, 4:8, :] = slots[4 * i : 4 * i + 4, :]
    r.meta[me] = r.metasend[me]
    meta_copies = []
    for o in range(1, 8):
        to = lax.rem(me + o, 8)
        copy = remote(r.metasend.at[to], r.meta.at[me], r.sm.at[o], r.rm.at[o], (to, c, d))
        copy.start()
        meta_copies.append(copy)
    gather.lines_on(3)
    line_gather_finish(mid_gather, lambda i: r.rows.at[i], r.sx, r.rx)
    for copy in meta_copies:
        copy.wait()
    keep.wait()

    slot_ids = lax.broadcasted_iota(jnp.int32, (64, 128), 0).astype(F32)

    def compact(s, _):
        for e in range(4):
            hit = slot_ids == r.meta[s, 4 + e : 5 + e, :]
            at = slice(e * 64, (e + 1) * 64)
            r.pcat[s, at, :] = hit.astype(F32).astype(BF16)
            gate = jnp.sum(jnp.where(hit, r.meta[s, e : e + 1, :], 0.0), axis=1, keepdims=True)
            r.gslot[s, at, :] = jnp.broadcast_to(gate, (64, 128))
        r.big1[s] = mm(r.pcat[s], r.rows[s]).astype(BF16)
        return 0

    lax.fori_loop(0, 8, compact, 0)
    gather.lines_on(4)
    gather.lines_on(5)

    def slots_of(e):
        return pl.ds(pl.multiple_of(e * 64, 64), 64)

    def expert_rows(ref, e):
        return ref[:, slots_of(e), :].reshape(512, ref.shape[2])

    def weight(m):
        return r.wg[m].reshape(1024, 512)

    def forward_in(e, _):
        rows = expert_rows(r.big1, e)
        g = mm(rows, weight(e))
        u = mm(rows, weight(6 + e))
        r.gbuf[e] = g.astype(BF16)
        r.ubuf[e] = u.astype(BF16)
        r.big3[:, slots_of(e), 0:512] = (g * jax.nn.sigmoid(g) * u).astype(BF16).reshape(8, 64, 512)
        return 0

    def forward_out(e, _):
        act = r.big3[:, slots_of(e), 0:512].reshape(512, 512)
        gate = expert_rows(r.gslot, e)[:, 0:1]
        r.big3[:, slots_of(e), :] = (mm_nt(act, weight(down(e))) * gate).astype(BF16).reshape(8, 64, 1024)
        return 0

    for j in range(4):
        gather.lines_wait(j)
    lax.fori_loop(0, 4, forward_in, 0)
    for j in range(4, 6):
        gather.lines_wait(j)
    lax.fori_loop(0, 4, forward_out, 0)

    def combine_pair(xs, _):
        s = xs * 2 + 1 - core
        r.pair[xs] = mm_tn(r.pcat[s], r.big3[s]).astype(BF16)
        return 0

    def combine_mine(xs, _):
        s = xs * 2 + core
        r.mine[xs] = mm_tn(r.pcat[s], r.big3[s]).astype(BF16)
        return 0

    lax.fori_loop(0, 4, combine_pair, 0)
    pair_copy = line_scatter_send_pair(r.pair, r.sib, r.s1, r.r1)
    lax.fori_loop(0, 4, combine_mine, 0)
    x_copies = line_scatter_send_x(r.mine, pair_copy, r.sib, r.inbox, r.s1, r.r1)
    teacher_load.wait()
    out = r.residual[...] + line_scatter_sum(r.mine, r.sib, r.inbox, x_copies)
    r.mixed[...] = out.astype(BF16)
    valid_row = r.vbuf[p, 0:1, :]
    valid_col = jnp.sum(jnp.where(eye, valid_row, 0.0), axis=1, keepdims=True)
    err = (out - r.gtok[...]) * valid_col
    r.gtok[...] = err
    r.low[...] = err.astype(BF16)
    r.rows[me] = r.low[...]
    err_gather = line_gather_start(r.low, lambda i: r.rows.at[i], r.s2, r.r2)
    square = jnp.sum(jnp.sum(err * err, axis=1, keepdims=True), axis=0, keepdims=True)
    count = jnp.sum(valid_row, axis=1, keepdims=True)
    r.stats[0:1, :] = jnp.broadcast_to(square, (1, 128))
    r.stats[1:2, :] = jnp.broadcast_to(count, (1, 128))
    for copy in [pair_copy] + x_copies:
        copy.wait_send()
    line_gather_finish(err_gather, lambda i: r.rows.at[i], r.s2, r.r2)

    def spread(s, _):
        r.big2[s] = mm(r.pcat[s], r.rows[s]).astype(BF16)
        return 0

    lax.fori_loop(0, 8, spread, 0)
    gather.drain()

    def store_grad(m, value):
        r.wg[m] = value.astype(BF16).reshape(2, 4, 2, 64, 512)

    def backward_act(e, _):
        g = r.gbuf[e].astype(F32)
        u = r.ubuf[e].astype(F32)
        sigma = jax.nn.sigmoid(g)
        silu = g * sigma
        gate = expert_rows(r.gslot, e)[:, 0:1]
        raw = mm(expert_rows(r.big2, e), weight(down(e)))
        act = silu * u
        dgate = jnp.sum(raw * act, axis=1, keepdims=True)
        r.gslot[:, slots_of(e), :] = jnp.broadcast_to(dgate, (512, 128)).reshape(8, 64, 128)
        r.big3[:, slots_of(e), 0:512] = (act * gate).astype(BF16).reshape(8, 64, 512)
        da = raw * gate
        r.gbuf[e] = (da * u * (sigma * (1.0 + g * (1.0 - sigma)))).astype(BF16)
        r.ubuf[e] = (da * silu).astype(BF16)
        return 0

    def backward_down(e, _):
        gated = r.big3[:, slots_of(e), 0:512].reshape(512, 512)
        store_grad(down(e), mm_tn(expert_rows(r.big2, e), gated))
        return 0

    def backward_in(e, _):
        dx = mm_nt(r.gbuf[e], weight(e)) + mm_nt(r.ubuf[e], weight(6 + e))
        r.big3[:, slots_of(e), :] = dx.astype(BF16).reshape(8, 64, 1024)
        return 0

    scatter = PlaneScatter(
        r.wg, r.far_in, (r.near_in_a, r.near_in_b), r.far2_in, r.near2_in, (r.stage_a, r.stage_b), r.load_sem, r.sw, r.rw
    )
    lax.fori_loop(0, 4, backward_act, 0)
    lax.fori_loop(0, 4, backward_down, 0)
    scatter.far(4)
    scatter.far(5)
    lax.fori_loop(0, 4, backward_in, 0)
    lax.fori_loop(0, 4, combine_pair, 0)
    pair_copy = line_scatter_send_pair(r.pair, r.sib, r.s3, r.r3)
    lax.fori_loop(0, 4, combine_mine, 0)

    def gate_rows(s, _):
        for e in range(4):
            hit = r.pcat[s, e * 64 : (e + 1) * 64, :].astype(F32)
            r.dgsend[s, e : e + 1, :] = jnp.sum(hit * r.gslot[s, e * 64 : (e + 1) * 64, :], axis=0, keepdims=True)
        return 0

    x_copies = line_scatter_send_x(r.mine, pair_copy, r.sib, r.inbox, r.s3, r.r3)
    lax.fori_loop(0, 8, gate_rows, 0)
    gate_copies = []
    for o in range(1, 8):
        to = lax.rem(me + o, 8)
        copy = remote(r.dgsend.at[to], r.dgates.at[me], r.s4.at[o], r.r4.at[o], (to, c, d))
        copy.start()
        gate_copies.append(copy)
    r.dgates[me] = r.dgsend[me]
    for e in range(4):
        rows = r.big1[:, 64 * e : 64 * e + 64, :].reshape(512, 1024)
        store_grad(e, mm_tn(rows, r.gbuf[e]))
        store_grad(6 + e, mm_tn(rows, r.ubuf[e]))
        scatter.far(e)
    wall_back = pltpu.make_async_copy(r.wall_keep, wall, r.keep_sem.at[1])
    wall_back.start()
    dmid = line_scatter_sum(r.mine, r.sib, r.inbox, x_copies)
    for copy in gate_copies:
        copy.wait()

    probs = r.probs[...]
    dprobs = jnp.concatenate([r.dgates[i, 0:4, :] for i in range(8)], axis=0) * r.picks[...]
    dlogits = probs * (dprobs - jnp.sum(probs * dprobs, axis=0, keepdims=True))
    high = dlogits.astype(BF16)
    r.dlog[0:32, :] = high
    r.dlog[32:64, :] = (dlogits - high.astype(F32)).astype(BF16)

    def router_back(i, _):
        at = pl.ds(pl.multiple_of(128 * i, 128), 128)
        part = mm(r.dlog[...], r.midl[:, at])
        r.smsend[i, 16:48, :] = part[:32] + part[32:]
        router = r.small_all[i, 16:48, :]
        r.dnorm[i] = mm_tn(r.dlog[...], jnp.concatenate([router, router], axis=0))
        return 0

    lax.fori_loop(0, 8, router_back, 0)
    gains = r.small_all[...].astype(F32)
    dmid = dmid + jnp.concatenate([r.dnorm[i] for i in range(8)], axis=1)
    res = r.residual[...]
    res_inv = inverse_rms(res)
    dgain_mid = jnp.sum(dmid * (res * res_inv), axis=0, keepdims=True)
    dres = r.gtok[...] + rms_back(res, res_inv, dmid * gain_row(gains, 2))
    r.gtok[...] = dres
    r.low[...] = dres.astype(BF16)

    def attended_back(t, _):
        both = mm_nt(r.low[...], r.wo_all[pl.ds(2 * t, 2)].reshape(256, 1024)).astype(BF16)
        for h in range(2):
            r.osend[2 * t + h] = both[:, 128 * h : 128 * h + 128]
        return 0

    lax.fori_loop(0, 4, attended_back, 0)
    r.dattbuf[c] = r.osend[c]
    d_copies = []
    for o in range(1, 8):
        to = lax.rem(c + o, 8)
        copy = remote(r.osend.at[to], r.dattbuf.at[c], r.sd.at[o], r.rd.at[o], (e_at, to, d))
        copy.start()
        d_copies.append(copy)
    r.rows[me] = r.low[...]
    branch_gather = line_gather_start(r.low, lambda i: r.rows.at[i], r.sb, r.rb)
    for copy in spread_copies:
        copy.wait()
    for copy in d_copies:
        copy.wait_recv()
    scatter.near_out(4)
    scatter.near_out(5)

    def prepare_back(b, _):
        tile = r.dattbuf[b].astype(F32)
        r.dop[b] = stack_heads(tile, True).astype(BF16)
        both = tile * r.oheads[b]
        first = jnp.sum(jnp.where(lo, both, 0.0), axis=1, keepdims=True)
        second = jnp.sum(jnp.where(lo, 0.0, both), axis=1, keepdims=True)
        delta = jnp.concatenate([first, second], axis=0)
        lane = lax.broadcasted_iota(jnp.int32, (256, 128), 1)
        r.lse[b] = jnp.where(lane < 64, r.lse[b], delta)
        r.gslot[b] = jnp.zeros((256, 128), F32)
        return 0

    lax.fori_loop(0, 8, prepare_back, 0)

    def key_block(k, _):
        block = key_rows(r.kvbuf, k)
        bias = key_bias(r.vbuf, k)

        def one(b, acc, scores):
            weights = jnp.exp(scores - r.lse[b][:, 0:1])
            dweights = mm_nt(r.dop[b], block)
            dscores = (weights * (dweights - r.lse[b][:, 64:65])).astype(BF16)
            r.gslot[b] = r.gslot[b] + mm(dscores, block)
            return acc + mm_tn(weights.astype(BF16), r.dop[b]) + mm_tn(dscores, r.qpad[b])

        def edge(b, acc):
            return one(b, acc, mask_last(mm_nt(r.qpad[b], block), bias, b, d))

        acc = lax.fori_loop(2 * k, 2 * k + 2, edge, jnp.zeros((512, 128), F32))
        acc = lax.fori_loop(2 * k + 2, 8, lambda b, acc: one(b, acc, mm_nt(r.qpad[b], block) + bias), acc)
        r.dkvsend[pl.ds(4 * k, 4)] = acc.astype(BF16).reshape(4, 128, 128)
        for h in range(2):
            b = 2 * k + h
            done = r.gslot[b] * SCALE
            r.sendq[b] = jnp.where(lo, done[:128], pltpu.roll(done[128:], 64, 1)).astype(BF16)

            @pl.when(b != c)
            def _():
                remote(r.sendq.at[b], r.qbuf.at[c], r.sdq.at[b], r.rdq.at[c], (e_at, b, d)).start()
                for g in range(2):
                    to = 2 * b + g
                    remote(r.dkvsend.at[to], r.dkvbuf.at[p], r.sdkv.at[to], r.rdkv.at[p], (e_at, b, g)).start()

            @pl.when(b == c)
            def _():
                r.qbuf[c] = r.sendq[c]
                r.dkvbuf[p] = r.dkvsend[p]
                to = c * 2 + 1 - d
                remote(r.dkvsend.at[to], r.dkvbuf.at[p], r.sdkv.at[to], r.rdkv.at[p], (e_at, c, 1 - d)).start()

        return 0

    lax.fori_loop(0, 1, key_block, 0)
    scatter.near_out(0)
    lax.fori_loop(1, 4, key_block, 0)
    line_gather_finish(branch_gather, lambda i: r.rows.at[i], r.sb, r.rb)

    def wait_dq(i, _):
        b = lax.rem(c + 1 + i, 8)
        copy = remote(r.sendq.at[b], r.qbuf.at[b], r.sdq.at[b], r.rdq.at[b], (e_at, b, d))
        copy.wait_send()
        copy.wait_recv()
        return 0

    def wait_dkv(i, _):
        q = lax.rem(p + 1 + i, 16)
        copy = remote(
            r.dkvsend.at[q], r.dkvbuf.at[q], r.sdkv.at[q], r.rdkv.at[q], (e_at, lax.div(q, 2), lax.rem(q, 2))
        )
        copy.wait_send()
        copy.wait_recv()
        return 0

    lax.fori_loop(0, 7, wait_dq, 0)
    lax.fori_loop(0, 15, wait_dkv, 0)
    cos, sin = r.cosine[...], -r.sine[...]
    dq_tiles = []
    for t in range(8):
        tile = r.qbuf[t].astype(F32)
        dq_tiles.append(tile * cos + swap_halves(tile) * sin)
    dq = jnp.concatenate(dq_tiles, axis=1)
    q_pre = r.qpre[...]
    q_inv = inverse_rms(q_pre)
    dgain_q = jnp.sum(dq * (q_pre * q_inv), axis=0, keepdims=True)
    r.dqkv[0:128, :] = rms_back(q_pre, q_inv, dq * gain_row(gains, 1)).astype(BF16)
    dk_tiles, dv_tiles = [], []
    for t in range(4):
        even = r.dkvbuf[4 * t].astype(F32) + r.dkvbuf[4 * t + 1].astype(F32)
        odd = r.dkvbuf[4 * t + 2].astype(F32) + r.dkvbuf[4 * t + 3].astype(F32)
        tile = jnp.where(lo, even, pltpu.roll(odd, 64, 1))
        dk_tiles.append(tile * cos + swap_halves(tile) * sin)
        dv_tiles.append(jnp.where(lo, pltpu.roll(even, 64, 1), odd))
    dk = jnp.concatenate(dk_tiles, axis=1)
    k_pre = r.kpre[...]
    k_inv = inverse_rms(k_pre)
    dgain_k = jnp.sum(dk * (k_pre * k_inv), axis=0, keepdims=True)
    r.dqkv[128:256, 0:512] = rms_back(k_pre, k_inv, dk * key_gain_row(gains)).astype(BF16)
    r.dqkv[128:256, 512:1024] = jnp.concatenate(dv_tiles, axis=1).astype(BF16)
    r.big3[me] = r.dqkv[...]
    dqkv_gather = line_gather_start(r.dqkv, lambda i: r.big3.at[i], r.sn, r.rn)
    for j in range(1, 4):
        scatter.near_out(j)

    def out_grad(t, _):
        at = pl.ds(pl.multiple_of(512 * t, 512), 512)
        tiles = mm_tn(r.attx[...].reshape(1024, 128), r.rows[:, :, at].reshape(1024, 512)).astype(BF16)
        for i in range(4):
            r.pieces_o[pl.ds(8 * t + 2 * i, 2)] = tiles[:, 128 * i : 128 * i + 128].reshape(2, 64, 128)
        return 0

    lax.fori_loop(0, 2, out_grad, 0)
    p_copies_o = plane_sum_send(r.pieces_o, 1, r.pin_o, r.sp1, r.rp1)
    wall_back.wait()

    def normed_back(t, _):
        for i in range(2):
            part = slice(128 * i, 128 * i + 128)
            both = mm_nt(r.dqkv[part, :], wall[pl.ds(2 * t, 2), part, :].reshape(256, 1024))
            for h in range(2):
                tile = both[:, 128 * h : 128 * h + 128]
                r.dnorm[2 * t + h] = tile if i == 0 else r.dnorm[2 * t + h] + tile
        return 0

    lax.fori_loop(0, 4, normed_back, 0)
    dnormed = jnp.concatenate([r.dnorm[t] for t in range(8)], axis=1)
    values = r.tokens[...].astype(F32)
    inv = inverse_rms(values)
    dgain_in = jnp.sum(dnormed * (values * inv), axis=0, keepdims=True)
    r.gtok[...] = r.gtok[...] + rms_back(values, inv, dnormed * gain_row(gains, 0))
    for i in range(8):
        at = slice(128 * i, 128 * i + 128)
        r.smsend[i, 0:1, :] = dgain_in[:, at]
        r.smsend[i, 1:2, :] = dgain_q[:, at]
        r.smsend[i, 2:3, :] = dgain_mid[:, at]
        half = dgain_k[:, 128 * (i // 2) : 128 * (i // 2) + 128]
        r.smsend[i, 3:4, :] = half if i % 2 == 0 else pltpu.roll(jnp.broadcast_to(half, (8, 128)), 64, 1)[0:1]
        r.smsend[i, 4:6, :] = r.stats[0:2, :]
        r.smsend[i, 6:16, :] = jnp.zeros((10, 128), F32)
    sm_copies = []
    for o in range(1, 8):
        to = lax.rem(me + o, 8)
        copy = remote(r.smsend.at[to], r.sminbox.at[o], r.sms.at[o], r.rms.at[o], (to, c, d))
        copy.start()
        sm_copies.append(copy)
    for j in (4, 5, 0):
        scatter.near_sum(j)
    shares_o = plane_sum_share(p_copies_o, r.pieces_o, 1, r.pin_o, r.res_o, r.sp2, r.rp2)

    total = r.smsend[me]
    for at, copy in enumerate(sm_copies):
        copy.wait_recv()
        total = total + r.sminbox[at + 1]
    r.smsum[...] = total
    small_copies = []
    for o in range(1, 16):
        _, device = plane_peer(o)
        copy = remote(r.smsum, r.smplane.at[o], r.sp5.at[o], r.rp5.at[o], device)
        copy.start()
        small_copies.append(copy)
    line_gather_finish(dqkv_gather, lambda i: r.big3.at[i], r.sn, r.rn)

    def qkv_grad(t, _):
        at = pl.ds(pl.multiple_of(512 * lax.rem(t, 2), 512), 512)
        part = pl.ds(pl.multiple_of(128 * lax.div(t, 2), 128), 128)
        tiles = mm_tn(r.nx[...].reshape(1024, 128), r.big3[:, part, at].reshape(1024, 512)).astype(BF16)
        for i in range(4):
            r.pieces_n[pl.ds(8 * t + 2 * i, 2)] = tiles[:, 128 * i : 128 * i + 128].reshape(2, 64, 128)
        return 0

    lax.fori_loop(0, 4, qkv_grad, 0)
    p_copies_n = plane_sum_send(r.pieces_n, 2, r.pin_n, r.sp3, r.rp3)
    for j in range(1, 4):
        scatter.near_sum(j)
    scatter.far2()
    for copy in shares_o:
        copy.wait_recv()
    scatter.near2()
    shares_n = plane_sum_share(p_copies_n, r.pieces_n, 2, r.pin_n, r.res_n, r.sp4, r.rp4)
    for at, copy in enumerate(small_copies):
        copy.wait_recv()
        total = total + r.smplane[at + 1]
    r.gsmall[...] = total
    scatter.finish(r.gw)
    for copy in shares_n:
        copy.wait_recv()
    scatter.drain()
    for copy in (
        [pair_copy] + x_copies + d_copies + sm_copies
        + small_copies + p_copies_o + p_copies_n + shares_o + shares_n
    ):
        copy.wait_send()


def layer(*args):
    vm = pl.BlockSpec(memory_space=pltpu.VMEM)
    hbm = pl.BlockSpec(memory_space=pl.ANY)
    in_hbm = ("wq", "wk", "wv", "wo", "teacher")
    return pl.pallas_call(
        layer_kernel,
        out_shape=tuple(jax.ShapeDtypeStruct(shape, dtype) for _, shape, dtype in OUTPUTS + SPILLS),
        in_specs=[hbm if name in in_hbm else vm for name in INPUTS],
        out_specs=(vm,) * len(OUTPUTS) + (hbm,) * len(SPILLS),
        scratch_shapes=[pltpu.VMEM(shape, dtype) for _, shape, dtype in SCRATCH]
        + [pltpu.SemaphoreType.DMA((count,)) for _, count in SEMAPHORES],
        compiler_params=pltpu.CompilerParams(
            collective_id=0, has_side_effects=True, vmem_limit_bytes=64 << 20
        ),
        cost_estimate=pl.CostEstimate(flops=32 * 10**9, bytes_accessed=60 << 20, transcendentals=8 << 20),
        name="layer",
    )(*args)[: len(OUTPUTS)]


def finish_kernel(
    mixed, gtok, res_o_in, res_n_in, small_in, gw_in,
    mixed_out, loss, gtok_out, gnorm_in, gq, gk, gv, gq_gain, gk_gain, gout, gnorm_mid, grouter, ggate, gup, gdown,
    res_o, res_n, small, gw, sems,
):
    pairs = ((small_in, small), (res_o_in, res_o), (res_n_in, res_n), (gw_in, gw), (mixed, mixed_out), (gtok, gtok_out))
    copies = [pltpu.make_async_copy(src, dst, sems.at[i]) for i, (src, dst) in enumerate(pairs)]
    for copy in copies:
        copy.start()
    copies[0].wait()
    loss[...] = small[4:5, 0:1] / (small[5:6, 0:1] * 1024.0)
    gnorm_in[...] = small[0:1, :]
    gq_gain[...] = small[1:2, :]
    gnorm_mid[...] = small[2:3, :]
    gk_gain[...] = small[3:4, 0:64]
    grouter[...] = small[16:48, :]

    def tiles(ref, out, first, count):
        for t in range(count):
            n = 2 * (first + t)
            out[:, 128 * t : 128 * t + 128] = jnp.concatenate([ref[n], ref[n + 1]], axis=0).astype(F32)

    copies[1].wait()
    tiles(res_o, gout, 0, 8)
    copies[2].wait()
    tiles(res_n, gq, 0, 8)
    tiles(res_n, gk, 8, 4)
    tiles(res_n, gv, 12, 4)
    copies[3].wait()
    for e in range(4):
        ggate[:, e, :] = gw[e]
        gup[:, e, :] = gw[6 + e]
        gdown[:, e, :] = gw[4 + e + 4 * (e // 2)]
    for copy in copies[4:]:
        copy.wait()


def finish(*args):
    vm = pl.BlockSpec(memory_space=pltpu.VMEM)
    hbm = pl.BlockSpec(memory_space=pl.ANY)
    shapes = (
        (128, 1024), (1, 1), (128, 1024), (1, 128), (128, 1024), (128, 512), (128, 512), (1, 128), (1, 64), (128, 1024),
        (1, 128), (32, 128), (64, 4, 512), (64, 4, 512), (64, 4, 512),
    )
    return pl.pallas_call(
        finish_kernel,
        out_shape=tuple(jax.ShapeDtypeStruct(v, BF16 if i == 0 else F32) for i, v in enumerate(shapes)),
        in_specs=[hbm] * 6,
        out_specs=(vm,) * len(shapes),
        scratch_shapes=[
            pltpu.VMEM((16, 64, 128), BF16),
            pltpu.VMEM((32, 64, 128), BF16),
            pltpu.VMEM((48, 128), F32),
            pltpu.VMEM((12, 64, 512), F32),
            pltpu.SemaphoreType.DMA((6,)),
        ],
        compiler_params=pltpu.CompilerParams(vmem_limit_bytes=62 << 20),
        name="finish",
    )(*args)


def per_device(
    tokens,
    norm_in,
    w_query,
    w_key,
    w_value,
    query_gain,
    key_gain,
    w_out,
    norm_mid,
    w_router,
    expert_gate,
    expert_up,
    expert_down,
    routes,
    valid,
    teacher,
):
    positions = (lax.axis_index("ctx") * 2 + lax.axis_index("dp")) * 128 + jnp.arange(128, dtype=jnp.int32)
    lane = jnp.arange(128, dtype=jnp.int32)
    frequency = THETA ** (-((lane % 32).astype(F32) * (2.0 / HEAD)))
    angles = positions.astype(F32)[:, None] * frequency[None, :]
    sign = jnp.where(lane % 64 < 32, -1.0, 1.0)
    parts = layer(
        tokens, w_query, w_key, w_value, w_out, norm_in, query_gain, norm_mid, key_gain, w_router.T,
        expert_gate, expert_up, expert_down, valid, jnp.cos(angles), jnp.sin(angles) * sign, routes.T, teacher,
    )
    (
        mixed, loss, gtok, gnorm_in, gq, gk, gv, gq_gain, gk_gain, gout, gnorm_mid, grouter, ggate, gup, gdown
    ) = finish(*parts)
    return (
        mixed, loss.reshape(()), gtok, gnorm_in.reshape(128), gq, gk, gv, gq_gain.reshape(128), gk_gain.reshape(64), gout,
        gnorm_mid.reshape(128), grouter.T, ggate, gup, gdown,
    )


def solution(mesh):
    placed = (
        P(("expert", "ctx", "dp"), None),
        P("expert"),
        P("expert", None),
        P("expert", None),
        P("expert", None),
        P("expert"),
        P("expert"),
        P("expert", None),
        P("expert"),
        P("expert", None),
        P(("ctx", "dp"), "expert", None),
        P(("ctx", "dp"), "expert", None),
        P(("ctx", "dp"), "expert", None),
        P(("expert", "ctx", "dp"), None),
        P(("expert", "ctx", "dp")),
        P(("expert", "ctx", "dp"), None),
    )
    return jax.shard_map(
        per_device,
        mesh=mesh,
        in_specs=placed,
        out_specs=(
            P(("expert", "ctx", "dp"), None),
            P(),
            P(("expert", "ctx", "dp"), None),
            P("expert"),
            P("expert", None),
            P("expert", None),
            P("expert", None),
            P("expert"),
            P("expert"),
            P("expert", None),
            P("expert"),
            P("expert", None),
            P(("ctx", "dp"), "expert", None),
            P(("ctx", "dp"), "expert", None),
            P(("ctx", "dp"), "expert", None),
        ),
        check_vma=False,
    )
```

```python
import jax
import jax.numpy as jnp
from jax import lax
from jax.experimental import pallas as pl
from jax.experimental.pallas import tpu as pltpu
from jax.sharding import PartitionSpec as P

MESH = pl.DeviceIdType.MESH
F32 = jnp.float32
BF16 = jnp.bfloat16

HEAD = 64
TOP = 8
EPS = 1e-06
THETA = 10000.0
NEG = -1e30
SCALE = HEAD**-0.5


def mm(a, b):
    return lax.dot_general(a, b, (((1,), (0,)), ((), ())), preferred_element_type=F32)


def mm_nt(a, b):
    return lax.dot_general(a, b, (((1,), (1,)), ((), ())), preferred_element_type=F32)


def mm_tn(a, b):
    return lax.dot_general(a, b, (((0,), (0,)), ((), ())), preferred_element_type=F32)


def places():
    e, c, d = lax.axis_index("expert"), lax.axis_index("ctx"), lax.axis_index("dp")
    return e // 2, e % 2, c, d


def yz():
    c, d = lax.axis_index("ctx"), lax.axis_index("dp")
    return lax.rem(c, 4), lax.div(c, 4) * 2 + d


def remote(src, dst, send, recv, device):
    return pltpu.make_async_remote_copy(
        src_ref=src, dst_ref=dst, send_sem=send, recv_sem=recv, device_id=device, device_id_type=MESH
    )


def line_device(x, core):
    return (lax.rem(x + 4, 4) * 2 + core, lax.axis_index("ctx"), lax.axis_index("dp"))


def plane_device(y, z):
    return (lax.axis_index("expert"), lax.div(z, 2) * 4 + y, lax.rem(z, 2))


def plane_peer(o):
    e, c, d = lax.axis_index("expert"), lax.axis_index("ctx"), lax.axis_index("dp")
    q = lax.rem(c * 2 + d + o, 16)
    return q, (e, lax.div(q, 2), lax.rem(q, 2))


def greet_all():
    barrier = pltpu.get_barrier_semaphore()
    e, c, d = lax.axis_index("expert"), lax.axis_index("ctx"), lax.axis_index("dp")
    for o in range(1, 8):
        pl.semaphore_signal(barrier, inc=1, device_id=(lax.rem(e + o, 8), c, d), device_id_type=MESH)
    for o in range(1, 16):
        _, device = plane_peer(o)
        pl.semaphore_signal(barrier, inc=1, device_id=device, device_id_type=MESH)
    pl.semaphore_wait(barrier, 22)


def line_gather_start(own, buf, send, recv):
    x, core, _, _ = places()
    me = x * 2 + core
    copies = [remote(own, buf(me), send.at[o], recv.at[o], line_device(x + o, core)) for o in (2, 1, 3)]
    copies.append(remote(own, buf(me), send.at[0], recv.at[0], line_device(x, 1 - core)))
    for copy in copies:
        copy.start()
    return copies


def line_gather_finish(copies, buf, send, recv, use=None):
    x, core, _, _ = places()

    def used(o, c):
        if use is not None:
            use(lax.rem(x - o + 4, 4) * 2 + c)

    used(0, core)
    copies[3].wait_recv()
    used(0, 1 - core)
    forwards = []
    for at, o in ((1, 1), (2, 3), (0, 2)):
        copies[at].wait_recv()
        block = buf(lax.rem(x - o + 4, 4) * 2 + core)
        copy = remote(block, block, send.at[4 + o], recv.at[4 + o], line_device(x, 1 - core))
        copy.start()
        forwards.append((copy, o))
        used(o, core)
    for copy, o in forwards:
        copy.wait_recv()
        used(o, 1 - core)
    for copy in copies + [copy for copy, _ in forwards]:
        copy.wait_send()


def line_scatter(part, mine, pair, sib, inbox, send, recv):
    x, core, _, _ = places()
    copies, order = [], (2, 1, 3, 0)
    for o in order:
        at = lax.rem(x + o, 4)
        pair[at] = part(at * 2 + 1 - core).astype(BF16)
        copy = remote(pair.at[at], sib.at[at], send.at[o], recv.at[o], line_device(x, 1 - core))
        copy.start()
        copies.append(copy)
    out = []
    for n, o in enumerate(order):
        at = lax.rem(x + o, 4)
        own = part(at * 2 + core)
        copies[n].wait_recv()
        mine[at] = (own + sib[at].astype(F32)).astype(BF16)
        if o > 0:
            copy = remote(mine.at[at], inbox.at[o - 1], send.at[4 + o], recv.at[4 + o], line_device(x + o, core))
            copy.start()
            out.append(copy)
    return copies, out


def line_scatter_sum(mine, inbox, copies):
    x, _, _, _ = places()
    total = mine[x].astype(F32)
    for at, o in ((1, 1), (2, 3), (0, 2)):
        copies[at].wait_recv()
        total = total + inbox[o - 1].astype(F32)
    return total


def plane_sum_send(pieces, n, inbox, send, recv):
    copies = []
    for o in range(1, 16):
        q, device = plane_peer(o)
        copy = remote(pieces.at[pl.ds(q * n, n)], inbox.at[o], send.at[o], recv.at[o], device)
        copy.start()
        copies.append(copy)
    return copies


def plane_sum_share(copies, pieces, n, inbox, result, send, recv):
    p = lax.axis_index("ctx") * 2 + lax.axis_index("dp")
    total = pieces[pl.ds(p * n, n)].astype(F32)
    for at, copy in enumerate(copies):
        copy.wait_recv()
        total = total + inbox[at + 1].astype(F32)
    result[pl.ds(p * n, n)] = total.astype(BF16)
    shares = []
    view = result.at[pl.ds(p * n, n)]
    for o in range(1, 16):
        _, device = plane_peer(o)
        copy = remote(view, view, send.at[o], recv.at[o], device)
        copy.start()
        shares.append(copy)
    return shares


class Copies:
    def __init__(self, send, recv):
        self.send, self.recv = send, recv
        self.y, self.z = yz()
        self.copies = {}

    def go(self, n, src, dst, device):
        copy = remote(src, dst, self.send.at[n], self.recv.at[n], device)
        copy.start()
        self.copies[n] = copy

    def drain(self):
        for copy in self.copies.values():
            copy.wait_send()


class PlaneGather(Copies):
    def __init__(self, wg, send, recv):
        super().__init__(send, recv)
        self.wg = wg

    def place(self, m, y, z):
        return self.wg.at[m, lax.div(z, 2), y, lax.rem(z, 2)]

    def shards(self):
        y, z = self.y, self.z
        a, b = pl.ds(0, 6), pl.ds(6, 6)
        for i, o in enumerate((1, 3)):
            view = self.place(a, y, z)
            self.go(i, view, view, plane_device(lax.rem(y + o, 4), z))
            view = self.place(b, y, z)
            self.go(2 + i, view, view, plane_device(y, lax.rem(z + o, 4)))

    def shards_on(self):
        y, z = self.y, self.z
        a, b = pl.ds(0, 6), pl.ds(6, 6)
        for i, o in enumerate((1, 3)):
            rows = pl.ds(32 * i, 32)
            self.copies[i].wait_recv()
            view = self.place(a, lax.rem(y - o + 4, 4), z).at[:, rows]
            self.go(4 + i, view, view, plane_device(lax.rem(y + o, 4), z))
            self.copies[2 + i].wait_recv()
            view = self.place(b, y, lax.rem(z - o + 4, 4)).at[:, rows]
            self.go(6 + i, view, view, plane_device(y, lax.rem(z + o, 4)))

    def shards_wait(self):
        for n in range(4, 8):
            self.copies[n].wait_recv()

    def lines(self, j):
        y, z = self.y, self.z
        for i, o in enumerate((1, 3)):
            view = self.wg.at[j, lax.div(z, 2), :, lax.rem(z, 2)]
            self.go(8 + 8 * j + i, view, view, plane_device(y, lax.rem(z + o, 4)))
            view = self.wg.at[6 + j, :, y]
            self.go(10 + 8 * j + i, view, view, plane_device(lax.rem(y + o, 4), z))

    def lines_on(self, j):
        y, z = self.y, self.z
        for i, o in enumerate((1, 3)):
            self.copies[8 + 8 * j + i].wait_recv()
            from_z = lax.rem(z - o + 4, 4)
            view = self.wg.at[j, lax.div(from_z, 2), pl.ds(2 * i, 2), lax.rem(from_z, 2)]
            self.go(12 + 8 * j + i, view, view, plane_device(y, lax.rem(z + o, 4)))
            self.copies[10 + 8 * j + i].wait_recv()
            view = self.wg.at[6 + j, i, lax.rem(y - o + 4, 4)]
            self.go(14 + 8 * j + i, view, view, plane_device(lax.rem(y + o, 4), z))

    def lines_wait(self, j):
        for n in range(12 + 8 * j, 16 + 8 * j):
            self.copies[n].wait_recv()


class PlaneScatter(Copies):
    def __init__(self, dw, far_in, near_in, far2_in, near2_in, stage, load, send, recv):
        super().__init__(send, recv)
        self.dw, self.far_in, self.near_in = dw, far_in, near_in
        self.far2_in, self.near2_in, self.stage, self.load = far2_in, near2_in, stage, load

    def block(self, half, m, at):
        if half == 0:
            return self.dw.at[m, lax.div(at, 2), :, lax.rem(at, 2)]
        return self.dw.at[6 + m, :, at]

    def due(self, half, m, at):
        if half == 0:
            return self.dw.at[m, lax.div(self.z, 2), at, lax.rem(self.z, 2)]
        return self.dw.at[m, lax.div(at, 2), self.y, lax.rem(at, 2)]

    def device(self, half, at):
        return plane_device(self.y, at) if half == 0 else plane_device(at, self.z)

    def place(self, half):
        return self.z if half == 0 else self.y

    def far(self, j):
        for half in range(2):
            me = self.place(half)
            for i, o in enumerate((1, 3)):
                view = self.block(half, j, lax.rem(me + 2, 4))
                view = view.at[pl.ds(2 * i, 2)] if half == 0 else view.at[i]
                self.go(8 * j + 2 * half + i, view, self.far_in.at[half, i, j], self.device(half, lax.rem(me + o, 4)))

    def near_out(self, j):
        loads = []
        for half in range(2):
            for i in range(2):
                self.copies[8 * j + 2 * half + i].wait_recv()
                spot = self.stage[0].at[i, pl.ds(0, 2)] if half == 0 else self.stage[1].at[i, 0]
                load = pltpu.make_async_copy(self.far_in.at[half, i, j], spot, self.load.at[2 * half + i])
                load.start()
                loads.append((load, spot))
        for half in range(2):
            me = self.place(half)
            for i, o in enumerate((1, 3)):
                load, spot = loads[2 * half + i]
                load.wait()
                to = lax.rem(me + o, 4)
                whole = self.block(half, j, to)
                part = whole.at[pl.ds(2 * i, 2)] if half == 0 else whole.at[i]
                part[...] = (part[...].astype(F32) + spot[...].astype(F32)).astype(BF16)
                self.go(8 * j + 4 + 2 * half + i, whole, self.near_in[half].at[i, j], self.device(half, to))

    def near_load(self, j):
        self.loads = []
        for half in range(2):
            for i in range(2):
                self.copies[8 * j + 4 + 2 * half + i].wait_recv()
                load = pltpu.make_async_copy(
                    self.near_in[half].at[i, j], self.stage[half].at[i], self.load.at[2 * half + i]
                )
                load.start()
                self.loads.append(load)

    def near_sum(self, j):
        self.near_load(j)
        for half in range(2):
            own, stage = self.block(half, j, self.place(half)), self.stage[half]
            self.loads[2 * half].wait()
            self.loads[2 * half + 1].wait()
            own[...] = (own[...].astype(F32) + stage[0].astype(F32) + stage[1].astype(F32)).astype(BF16)

    def place2(self, half):
        return self.y if half == 0 else self.z

    def device2(self, half, at):
        return plane_device(at, self.z) if half == 0 else plane_device(self.y, at)

    def far2(self):
        for half in range(2):
            me = self.place2(half)
            for i, o in enumerate((1, 3)):
                view = self.due(half, pl.ds(6 * half, 6), lax.rem(me + 2, 4)).at[:, pl.ds(32 * i, 32)]
                self.go(48 + 2 * half + i, view, self.far2_in.at[half, i], self.device2(half, lax.rem(me + o, 4)))

    def near2(self):
        for half in range(2):
            me = self.place2(half)
            for i, o in enumerate((1, 3)):
                self.copies[48 + 2 * half + i].wait_recv()
                to = lax.rem(me + o, 4)

                def add(m, _):
                    part = self.due(half, 6 * half + m, to).at[pl.ds(32 * i, 32)]
                    part[...] = (part[...].astype(F32) + self.far2_in[half, i, m].astype(F32)).astype(BF16)
                    return 0

                lax.fori_loop(0, 6, add, 0)
                view = self.due(half, pl.ds(6 * half, 6), to)
                self.go(52 + 2 * half + i, view, self.near2_in.at[half, i], self.device2(half, to))

    def finish(self, result):
        for half in range(2):
            me = self.place2(half)
            for i in range(2):
                self.copies[52 + 2 * half + i].wait_recv()

            def add(m, _):
                result[6 * half + m] = (
                    self.due(half, 6 * half + m, me)[...].astype(F32)
                    + self.near2_in[half, 0, m].astype(F32)
                    + self.near2_in[half, 1, m].astype(F32)
                )
                return 0

            lax.fori_loop(0, 6, add, 0)


def low_lanes():
    return lax.broadcasted_iota(jnp.int32, (128, 128), 1) < 64


def swap_halves(tile):
    lane = lax.rem(lax.broadcasted_iota(jnp.int32, (128, 128), 1), 64)
    return jnp.where(lane < 32, pltpu.roll(tile, 96, 1), pltpu.roll(tile, 32, 1))


def gain_row(small, row):
    return jnp.concatenate([small[i, row : row + 1, :] for i in range(8)], axis=1)


def key_gain_row(small):
    lane = lax.broadcasted_iota(jnp.int32, (1, 128), 1)
    return jnp.concatenate(
        [jnp.where(lane < 64, small[2 * t, 3:4, :], small[2 * t + 1, 3:4, :]) for t in range(4)], axis=1
    )


def router_rows(small):
    return jnp.concatenate([small[i, 16:48, :] for i in range(8)], axis=1)


def inverse_rms(values):
    return lax.rsqrt(jnp.mean(values * values, axis=1, keepdims=True) + EPS)


def rms_back(values, inverse, grad):
    hat = values * inverse
    return inverse * (grad - hat * jnp.mean(grad * hat, axis=1, keepdims=True))


def stack_heads(tile, upper):
    lo = low_lanes()
    turned = pltpu.roll(tile, 64, 1)
    first, second = (turned, tile) if upper else (tile, turned)
    keep = jnp.logical_not(lo) if upper else lo
    return jnp.concatenate([jnp.where(keep, first, 0.0), jnp.where(keep, second, 0.0)], axis=0)


def key_rows(kvbuf, k):
    return kvbuf[pl.ds(4 * k, 4)].reshape(512, 128)


def key_bias(vbuf, k):
    row = jnp.concatenate([vbuf[4 * k + i, 0:1, :] for i in range(4)], axis=1)
    return (row - 1.0) * 1e30


def mask_last(scores, bias, b, d):
    half = lax.rem(b, 2) * 256
    column = lax.broadcasted_iota(jnp.int32, (256, 512), 1)
    row = lax.rem(lax.broadcasted_iota(jnp.int32, (256, 512), 0), 128)
    masked = jnp.where(column < half + 256, scores + bias, NEG)
    return jnp.where(column == row + (half + 128 * d), scores, masked)


def down(e):
    return 4 + e + 4 * lax.div(e, 2)


class Refs:
    def __init__(self, names, refs):
        for name, ref in zip(names, refs, strict=True):
            setattr(self, name, ref)


INPUTS = (
    "tokens", "wq", "wk", "wv", "wo", "norm_in", "query_gain", "norm_mid", "key_gain", "w_router",
    "expert_gate", "expert_up", "expert_down", "valid", "cosine", "sine", "routes", "teacher",
)
OUTPUTS = (
    ("mixed", (128, 1024), BF16),
    ("gtok", (128, 1024), F32),
    ("res_o", (16, 64, 128), BF16),
    ("res_q", (16, 64, 128), BF16),
    ("res_n", (16, 64, 128), BF16),
    ("gsmall", (48, 128), F32),
    ("gw", (12, 64, 512), F32),
)
SPILLS = (
    ("wall_keep", (8, 256, 1024), BF16),
    ("far_in", (2, 2, 6, 2, 64, 512), BF16),
    ("near_in_a", (2, 6, 4, 64, 512), BF16),
    ("near_in_b", (2, 6, 2, 2, 64, 512), BF16),
)
SCRATCH = (
    ("big1", (8, 256, 1024), BF16),
    ("big2", (8, 256, 1024), BF16),
    ("big3", (8, 256, 1024), BF16),
    ("rows", (8, 128, 1024), BF16),
    ("wo_all", (8, 128, 1024), BF16),
    ("wg", (12, 2, 4, 2, 64, 512), BF16),
    ("gbuf", (4, 512, 512), BF16),
    ("ubuf", (4, 512, 512), BF16),
    ("mine", (4, 128, 1024), BF16),
    ("pair", (4, 128, 1024), BF16),
    ("sib", (4, 128, 1024), BF16),
    ("inbox", (3, 128, 1024), BF16),
    ("stage_a", (2, 4, 64, 512), BF16),
    ("stage_b", (2, 2, 2, 64, 512), BF16),
    ("far2_in", (2, 2, 6, 32, 512), BF16),
    ("near2_in", (2, 2, 6, 64, 512), BF16),
    ("small_all", (8, 48, 128), BF16),
    ("vbuf", (16, 8, 128), F32),
    ("kvbuf", (16, 128, 128), BF16),
    ("qbuf", (8, 128, 128), BF16),
    ("oheads", (8, 128, 128), F32),
    ("lse", (8, 256, 128), F32),
    ("att", (8, 128, 128), BF16),
    ("attx", (8, 128, 128), BF16),
    ("normed_t", (8, 128, 128), BF16),
    ("nx", (8, 128, 128), BF16),
    ("sendq", (8, 128, 128), BF16),
    ("osend", (8, 128, 128), BF16),
    ("residual", (128, 1024), F32),
    ("qpre", (128, 1024), F32),
    ("kpre", (128, 512), F32),
    ("midl", (128, 1024), BF16),
    ("low", (128, 1024), BF16),
    ("meta", (8, 8, 128), F32),
    ("metasend", (8, 8, 128), F32),
    ("probs", (32, 128), F32),
    ("picks", (32, 128), F32),
    ("stats", (8, 128), F32),
    ("pcat", (8, 256, 128), BF16),
    ("gslot", (8, 256, 128), F32),
    ("dgates", (8, 8, 128), F32),
    ("dgsend", (8, 8, 128), F32),
    ("dattbuf", (8, 128, 128), BF16),
    ("qpad", (8, 256, 128), BF16),
    ("dop", (8, 256, 128), BF16),
    ("dkvsend", (16, 128, 128), BF16),
    ("dkvbuf", (16, 128, 128), BF16),
    ("dqkv", (256, 1024), BF16),
    ("dnorm", (8, 128, 128), F32),
    ("dlog", (64, 128), BF16),
    ("smsend", (8, 48, 128), F32),
    ("sminbox", (8, 48, 128), F32),
    ("smsum", (48, 128), F32),
    ("smplane", (16, 48, 128), F32),
    ("pieces_o", (16, 64, 128), BF16),
    ("pin_o", (16, 1, 64, 128), BF16),
    ("pieces_q", (16, 64, 128), BF16),
    ("pin_q", (16, 1, 64, 128), BF16),
    ("pieces_n", (16, 64, 128), BF16),
    ("pin_n", (16, 1, 64, 128), BF16),
)
SEMAPHORES = (
    ("own_sem", 6), ("keep_sem", 2), ("teacher_sem", 1), ("load_sem", 4),
    ("ssm", 8), ("rsm", 8), ("skvw", 8), ("rkvw", 8), ("sqw", 8), ("rqw", 8), ("swo", 8), ("rwo", 8), ("sv", 16), ("rv", 16),
    ("sew", 56), ("rew", 56), ("snx", 8), ("rnx", 8), ("sax", 8), ("rax", 8),
    ("skv", 16), ("rkv", 16), ("sq", 8), ("rq", 8), ("so", 8), ("ro", 8), ("sx", 8), ("rx", 8), ("sm", 8), ("rm", 8),
    ("s1", 8), ("r1", 8), ("s2", 8), ("r2", 8), ("s3", 8), ("r3", 8), ("s4", 8), ("r4", 8),
    ("sw", 56), ("rw", 56), ("sd", 8), ("rd", 8), ("sdq", 8), ("rdq", 8), ("sdkv", 16), ("rdkv", 16),
    ("sb", 8), ("rb", 8), ("sn", 8), ("rn", 8), ("sn2", 8), ("rn2", 8), ("sms", 8), ("rms", 8),
    ("sp1", 16), ("rp1", 16), ("sp2", 16), ("rp2", 16), ("sp3", 16), ("rp3", 16), ("sp4", 16), ("rp4", 16),
    ("sp5", 16), ("rp5", 16), ("sp6", 16), ("rp6", 16), ("sp7", 16), ("rp7", 16),
)
NAMES = INPUTS + tuple(n for part in (OUTPUTS, SPILLS, SCRATCH, SEMAPHORES) for n, *_ in part)


def layer_kernel(*refs):
    r = Refs(NAMES, refs)
    x, core, c, d = places()
    me = x * 2 + core
    p = c * 2 + d
    y, z = yz()
    e_at = lax.axis_index("expert")
    lo = low_lanes()

    wall = r.big1
    own = [
        pltpu.make_async_copy(r.wq, wall.at[me, pl.ds(0, 128)], r.own_sem.at[0]),
        pltpu.make_async_copy(r.wk, wall.at[me, pl.ds(128, 128), pl.ds(0, 512)], r.own_sem.at[1]),
        pltpu.make_async_copy(r.wv, wall.at[me, pl.ds(128, 128), pl.ds(512, 512)], r.own_sem.at[2]),
        pltpu.make_async_copy(r.wo, r.wo_all.at[me], r.own_sem.at[3]),
    ]
    for copy in own:
        copy.start()
    teacher_load = pltpu.make_async_copy(r.teacher, r.gtok, r.teacher_sem.at[0])
    teacher_load.start()
    eye = lax.broadcasted_iota(jnp.int32, (128, 128), 0) == lax.broadcasted_iota(jnp.int32, (128, 128), 1)
    rows = [ref[...].astype(F32).reshape(1, 128) for ref in (r.norm_in, r.query_gain, r.norm_mid)]
    key_row = r.key_gain[...].astype(F32).reshape(1, 64)
    rows += [jnp.concatenate([key_row, key_row], axis=1), jnp.zeros((12, 128), F32), r.w_router[...].astype(F32)]
    r.small_all[me] = jnp.concatenate(rows, axis=0).astype(BF16)
    valid_row = r.valid[...].astype(F32).reshape(1, 128)
    r.vbuf[p] = jnp.broadcast_to(valid_row, (8, 128))
    greet_all()

    gather = PlaneGather(r.wg, r.sew, r.rew)
    small_gather = line_gather_start(r.small_all.at[me], lambda i: r.small_all.at[i], r.ssm, r.rsm)
    for copy in own[:3]:
        copy.wait()
    kv_part, q_part = pl.ds(128, 128), pl.ds(0, 128)
    kv_gather = line_gather_start(wall.at[me, kv_part], lambda i: wall.at[i, kv_part], r.skvw, r.rkvw)
    q_gather = line_gather_start(wall.at[me, q_part], lambda i: wall.at[i, q_part], r.sqw, r.rqw)
    for ref, first in ((r.expert_gate, (0, 1, 2, 3)), (r.expert_up, (6, 7, 8, 9)), (r.expert_down, (4, 5, 10, 11))):
        whole = ref[...].astype(F32)
        for e, m in enumerate(first):
            r.wg[m, lax.div(z, 2), y, lax.rem(z, 2)] = whole[:, e, :].astype(BF16)
    gather.shards()
    own[3].wait()
    out_gather = line_gather_start(r.wo_all.at[me], lambda i: r.wo_all.at[i], r.swo, r.rwo)
    valid_copies = []
    for o in range(1, 16):
        _, device = plane_peer(o)
        copy = remote(r.vbuf.at[p], r.vbuf.at[p], r.sv.at[o], r.rv.at[o], device)
        copy.start()
        valid_copies.append(copy)

    line_gather_finish(small_gather, lambda i: r.small_all.at[i], r.ssm, r.rsm)
    gains = r.small_all[...].astype(F32)
    values = r.tokens[...].astype(F32)
    normed = (values * inverse_rms(values) * gain_row(gains, 0)).astype(BF16)
    for t in range(8):
        r.normed_t[t] = normed[:, 128 * t : 128 * t + 128]
    r.nx[me] = r.normed_t[me]
    spread_copies = []
    for o in range(1, 8):
        to = lax.rem(me + o, 8)
        copy = remote(r.normed_t.at[to], r.nx.at[me], r.snx.at[o], r.rnx.at[o], (to, c, d))
        copy.start()
        spread_copies.append(copy)
    gather.shards_on()
    gather.shards_wait()

    line_gather_finish(kv_gather, lambda i: wall.at[i, kv_part], r.skvw, r.rkvw)
    kv_pre = mm(normed, wall[:, 128:256, :].reshape(1024, 1024))
    k_pre = kv_pre[:, 0:512]
    v_low = kv_pre[:, 512:1024].astype(BF16).astype(F32)
    r.kpre[...] = k_pre
    cos, sin = r.cosine[...], r.sine[...]
    kn = k_pre * inverse_rms(k_pre) * key_gain_row(gains)
    for t in range(4):
        tile = kn[:, 128 * t : 128 * t + 128]
        k_rot = tile * cos + swap_halves(tile) * sin
        v_tile = v_low[:, 128 * t : 128 * t + 128]
        r.dkvsend[2 * t] = jnp.where(lo, k_rot, pltpu.roll(v_tile, 64, 1)).astype(BF16)
        r.dkvsend[2 * t + 1] = jnp.where(lo, pltpu.roll(k_rot, 64, 1), v_tile).astype(BF16)
    r.kvbuf[p] = r.dkvsend[c]
    kv_copies = []
    for o in range(1, 16):
        q, device = plane_peer(o)
        copy = remote(r.dkvsend.at[lax.div(q, 2)], r.kvbuf.at[p], r.skv.at[o], r.rkv.at[o], device)
        copy.start()
        kv_copies.append(copy)
    for j in range(2):
        gather.lines(j)
    line_gather_finish(q_gather, lambda i: wall.at[i, q_part], r.sqw, r.rqw)
    q_pre = mm(normed, wall[:, 0:128, :].reshape(1024, 1024))
    r.qpre[...] = q_pre
    qn = q_pre * inverse_rms(q_pre) * gain_row(gains, 1)
    for t in range(8):
        tile = qn[:, 128 * t : 128 * t + 128]
        r.sendq[t] = (tile * cos + swap_halves(tile) * sin).astype(BF16)
    r.qbuf[c] = r.sendq[c]
    q_copies = []
    for o in range(1, 8):
        to = lax.rem(c + o, 8)
        copy = remote(r.sendq.at[to], r.qbuf.at[c], r.sq.at[o], r.rq.at[o], (e_at, to, d))
        copy.start()
        q_copies.append(copy)
    keep = pltpu.make_async_copy(wall, r.wall_keep, r.keep_sem.at[0])
    keep.start()
    for j in range(2):
        gather.lines_on(j)
    gather.lines(2)
    for copy in valid_copies + kv_copies + q_copies:
        copy.wait()

    def prepare(b, _):
        r.qpad[b] = (stack_heads(r.qbuf[b].astype(F32), False) * SCALE).astype(BF16)
        return 0

    lax.fori_loop(0, 8, prepare, 0)

    def chunk(i, _):
        b = lax.rem(c + 1 + i, 8)
        queries = r.qpad[b]
        last = lax.div(b, 2)

        def update(carry, block, scores):
            top, total, acc = carry
            new_top = jnp.maximum(top, jnp.max(scores, axis=1, keepdims=True))
            weights = jnp.exp(scores - new_top)
            shrink = jnp.exp(top - new_top)
            total = total * shrink + jnp.sum(weights, axis=1, keepdims=True)
            acc = acc * shrink + mm(weights.astype(BF16), block)
            return (new_top, total, acc)

        def keys(k, carry):
            block = key_rows(r.kvbuf, k)
            return update(carry, block, mm_nt(queries, block) + key_bias(r.vbuf, k))

        zero = jnp.zeros((256, 1), F32)
        carry = lax.fori_loop(0, last, keys, (zero + NEG, zero, jnp.zeros((256, 128), F32)))
        block = key_rows(r.kvbuf, last)
        scores = mask_last(mm_nt(queries, block), key_bias(r.vbuf, last), b, d)
        top, total, acc = update(carry, block, scores)
        acc = acc / total
        r.lse[b] = jnp.broadcast_to(top + jnp.log(total), (256, 128))
        merged = jnp.where(lo, pltpu.roll(acc[:128], 64, 1), acc[128:])
        r.oheads[b] = merged
        r.osend[b] = merged.astype(BF16)

        @pl.when(b != c)
        def _():
            remote(r.osend.at[b], r.att.at[c], r.so.at[b], r.ro.at[c], (e_at, b, d)).start()

        @pl.when(b == c)
        def _():
            r.att[c] = r.osend[c]

        return 0

    lax.fori_loop(0, 4, chunk, 0)
    gather.lines_on(2)
    lax.fori_loop(4, 8, chunk, 0)
    line_gather_finish(out_gather, lambda i: r.wo_all.at[i], r.swo, r.rwo)

    def wait_rest(i, _):
        b = lax.rem(c + 1 + i, 8)
        copy = remote(r.osend.at[b], r.att.at[b], r.so.at[b], r.ro.at[b], (e_at, b, d))
        copy.wait_send()
        copy.wait_recv()
        return 0

    lax.fori_loop(0, 7, wait_rest, 0)
    gather.lines(3)
    gather.lines(4)
    r.attx[me] = r.att[me]
    for o in range(1, 8):
        to = lax.rem(me + o, 8)
        copy = remote(r.att.at[to], r.attx.at[me], r.sax.at[o], r.rax.at[o], (to, c, d))
        copy.start()
        spread_copies.append(copy)
    attended = jnp.concatenate([r.att[t] for t in range(8)], axis=1)
    res = r.tokens[...].astype(F32) + mm(attended, r.wo_all[...].reshape(1024, 1024))
    r.residual[...] = res
    mid = (res * inverse_rms(res) * gain_row(gains, 2)).astype(BF16)
    r.midl[...] = mid
    r.rows[me] = mid
    mid_gather = line_gather_start(r.midl, lambda i: r.rows.at[i], r.sx, r.rx)

    logits = mm_nt(router_rows(r.small_all[...]), mid)
    terms = jnp.exp(logits - jnp.max(logits, axis=0, keepdims=True))
    probs = terms / jnp.sum(terms, axis=0, keepdims=True)
    ids = lax.broadcasted_iota(jnp.int32, (32, 128), 0).astype(F32)
    routes = r.routes[...].astype(F32)
    picks = jnp.zeros((32, 128), F32)
    for k in range(TOP):
        picks = picks + (ids == routes[k : k + 1, :]).astype(F32)
    before = lax.broadcasted_iota(jnp.int32, (128, 128), 0) < lax.broadcasted_iota(jnp.int32, (128, 128), 1)
    slots = mm(picks.astype(BF16), before.astype(F32).astype(BF16))
    slots = jnp.where(picks > 0.0, slots, -1.0)
    r.probs[...] = probs
    r.picks[...] = picks
    gates = probs * picks
    for i in range(8):
        r.metasend[i, 0:4, :] = gates[4 * i : 4 * i + 4, :]
        r.metasend[i, 4:8, :] = slots[4 * i : 4 * i + 4, :]
    r.meta[me] = r.metasend[me]
    meta_copies = []
    for o in range(1, 8):
        to = lax.rem(me + o, 8)
        copy = remote(r.metasend.at[to], r.meta.at[me], r.sm.at[o], r.rm.at[o], (to, c, d))
        copy.start()
        meta_copies.append(copy)
    gather.lines_on(3)
    gather.lines(5)
    for copy in meta_copies:
        copy.wait()
    keep.wait()

    slot_ids = lax.broadcasted_iota(jnp.int32, (64, 128), 0).astype(F32)

    def compact(s):
        for e in range(4):
            hit = slot_ids == r.meta[s, 4 + e : 5 + e, :]
            at = slice(e * 64, (e + 1) * 64)
            r.pcat[s, at, :] = hit.astype(F32).astype(BF16)
            gate = jnp.sum(jnp.where(hit, r.meta[s, e : e + 1, :], 0.0), axis=1, keepdims=True)
            r.gslot[s, at, :] = jnp.broadcast_to(gate, (64, 128))
        r.big1[s] = mm(r.pcat[s], r.rows[s]).astype(BF16)

    line_gather_finish(mid_gather, lambda i: r.rows.at[i], r.sx, r.rx, compact)
    gather.lines_on(4)

    def slots_of(e):
        return pl.ds(pl.multiple_of(e * 64, 64), 64)

    def expert_rows(ref, e):
        return ref[:, slots_of(e), :].reshape(512, ref.shape[2])

    def weight(m):
        return r.wg[m].reshape(1024, 512)

    def forward_in(e, _):
        rows = expert_rows(r.big1, e)
        g = mm(rows, weight(e))
        u = mm(rows, weight(6 + e))
        r.gbuf[e] = g.astype(BF16)
        r.ubuf[e] = u.astype(BF16)
        r.big3[:, slots_of(e), 0:512] = (g * jax.nn.sigmoid(g) * u).astype(BF16).reshape(8, 64, 512)
        return 0

    def forward_out(e, _):
        act = r.big3[:, slots_of(e), 0:512].reshape(512, 512)
        gate = expert_rows(r.gslot, e)[:, 0:1]
        r.big3[:, slots_of(e), :] = (mm_nt(act, weight(down(e))) * gate).astype(BF16).reshape(8, 64, 1024)
        return 0

    for e in range(4):
        if e == 1:
            gather.lines_on(5)
        gather.lines_wait(e)
        forward_in(e, 0)
    for e in range(4):
        if e % 2 == 0:
            gather.lines_wait(4 + e // 2)
        forward_out(2 * (e % 2) + e // 2, 0)

    def combine(s):
        return mm_tn(r.pcat[s], r.big3[s])

    pair_copies, x_copies = line_scatter(combine, r.mine, r.pair, r.sib, r.inbox, r.s1, r.r1)
    teacher_load.wait()
    out = r.residual[...] + line_scatter_sum(r.mine, r.inbox, x_copies)
    r.mixed[...] = out.astype(BF16)
    valid_row = r.vbuf[p, 0:1, :]
    valid_col = jnp.sum(jnp.where(eye, valid_row, 0.0), axis=1, keepdims=True)
    err = (out - r.gtok[...]) * valid_col
    r.gtok[...] = err
    r.low[...] = err.astype(BF16)
    r.rows[me] = r.low[...]
    err_gather = line_gather_start(r.low, lambda i: r.rows.at[i], r.s2, r.r2)
    square = jnp.sum(jnp.sum(err * err, axis=1, keepdims=True), axis=0, keepdims=True)
    count = jnp.sum(valid_row, axis=1, keepdims=True)
    r.stats[0:1, :] = jnp.broadcast_to(square, (1, 128))
    r.stats[1:2, :] = jnp.broadcast_to(count, (1, 128))
    for copy in pair_copies + x_copies:
        copy.wait_send()

    def spread(s):
        r.big2[s] = mm(r.pcat[s], r.rows[s]).astype(BF16)

    line_gather_finish(err_gather, lambda i: r.rows.at[i], r.s2, r.r2, spread)
    gather.drain()

    def store_grad(m, value):
        r.wg[m] = value.astype(BF16).reshape(2, 4, 2, 64, 512)

    def backward_act(e, _):
        g = r.gbuf[e].astype(F32)
        u = r.ubuf[e].astype(F32)
        sigma = jax.nn.sigmoid(g)
        silu = g * sigma
        gate = expert_rows(r.gslot, e)[:, 0:1]
        raw = mm(expert_rows(r.big2, e), weight(down(e)))
        act = silu * u
        dgate = jnp.sum(raw * act, axis=1, keepdims=True)
        r.gslot[:, slots_of(e), :] = jnp.broadcast_to(dgate, (512, 128)).reshape(8, 64, 128)
        r.big3[:, slots_of(e), 0:512] = (act * gate).astype(BF16).reshape(8, 64, 512)
        da = raw * gate
        r.gbuf[e] = (da * u * (sigma * (1.0 + g * (1.0 - sigma)))).astype(BF16)
        r.ubuf[e] = (da * silu).astype(BF16)
        return 0

    def backward_down(e, _):
        gated = r.big3[:, slots_of(e), 0:512].reshape(512, 512)
        store_grad(down(e), mm_tn(expert_rows(r.big2, e), gated))
        return 0

    def backward_in(e, _):
        dx = mm_nt(r.gbuf[e], weight(e)) + mm_nt(r.ubuf[e], weight(6 + e))
        r.big3[:, slots_of(e), :] = dx.astype(BF16).reshape(8, 64, 1024)
        return 0

    scatter = PlaneScatter(
        r.wg, r.far_in, (r.near_in_a, r.near_in_b), r.far2_in, r.near2_in, (r.stage_a, r.stage_b), r.load_sem, r.sw, r.rw
    )
    lax.fori_loop(0, 4, backward_act, 0)
    lax.fori_loop(0, 4, backward_down, 0)
    scatter.far(4)
    scatter.far(5)
    lax.fori_loop(0, 4, backward_in, 0)
    pair_copies, x_copies = line_scatter(combine, r.mine, r.pair, r.sib, r.inbox, r.s3, r.r3)

    def gate_rows(s, _):
        for e in range(4):
            hit = r.pcat[s, e * 64 : (e + 1) * 64, :].astype(F32)
            r.dgsend[s, e : e + 1, :] = jnp.sum(hit * r.gslot[s, e * 64 : (e + 1) * 64, :], axis=0, keepdims=True)
        return 0

    lax.fori_loop(0, 8, gate_rows, 0)
    gate_copies = []
    for o in range(1, 8):
        to = lax.rem(me + o, 8)
        copy = remote(r.dgsend.at[to], r.dgates.at[me], r.s4.at[o], r.r4.at[o], (to, c, d))
        copy.start()
        gate_copies.append(copy)
    r.dgates[me] = r.dgsend[me]
    for e in range(4):
        rows = r.big1[:, 64 * e : 64 * e + 64, :].reshape(512, 1024)
        store_grad(e, mm_tn(rows, r.gbuf[e]))
        store_grad(6 + e, mm_tn(rows, r.ubuf[e]))
        scatter.far(e)
    wall_back = pltpu.make_async_copy(r.wall_keep, wall, r.keep_sem.at[1])
    wall_back.start()
    dmid = line_scatter_sum(r.mine, r.inbox, x_copies)
    for copy in gate_copies:
        copy.wait()

    probs = r.probs[...]
    dprobs = jnp.concatenate([r.dgates[i, 0:4, :] for i in range(8)], axis=0) * r.picks[...]
    dlogits = probs * (dprobs - jnp.sum(probs * dprobs, axis=0, keepdims=True))
    high = dlogits.astype(BF16)
    r.dlog[0:32, :] = high
    r.dlog[32:64, :] = (dlogits - high.astype(F32)).astype(BF16)

    def router_back(i, _):
        at = pl.ds(pl.multiple_of(128 * i, 128), 128)
        part = mm(r.dlog[...], r.midl[:, at])
        r.smsend[i, 16:48, :] = part[:32] + part[32:]
        router = r.small_all[i, 16:48, :]
        r.dnorm[i] = mm_tn(r.dlog[...], jnp.concatenate([router, router], axis=0))
        return 0

    lax.fori_loop(0, 8, router_back, 0)
    gains = r.small_all[...].astype(F32)
    dmid = dmid + jnp.concatenate([r.dnorm[i] for i in range(8)], axis=1)
    res = r.residual[...]
    res_inv = inverse_rms(res)
    dgain_mid = jnp.sum(dmid * (res * res_inv), axis=0, keepdims=True)
    dres = r.gtok[...] + rms_back(res, res_inv, dmid * gain_row(gains, 2))
    r.gtok[...] = dres
    r.low[...] = dres.astype(BF16)

    def attended_back(t, _):
        both = mm_nt(r.low[...], r.wo_all[pl.ds(2 * t, 2)].reshape(256, 1024)).astype(BF16)
        for h in range(2):
            r.osend[2 * t + h] = both[:, 128 * h : 128 * h + 128]
        return 0

    lax.fori_loop(0, 4, attended_back, 0)
    r.dattbuf[c] = r.osend[c]
    d_copies = []
    for o in range(1, 8):
        to = lax.rem(c + o, 8)
        copy = remote(r.osend.at[to], r.dattbuf.at[c], r.sd.at[o], r.rd.at[o], (e_at, to, d))
        copy.start()
        d_copies.append(copy)
    r.rows[me] = r.low[...]
    branch_gather = line_gather_start(r.low, lambda i: r.rows.at[i], r.sb, r.rb)
    scatter.near_out(4)
    scatter.near_out(5)
    for copy in spread_copies:
        copy.wait()
    for copy in d_copies:
        copy.wait_recv()

    def prepare_back(b, _):
        tile = r.dattbuf[b].astype(F32)
        r.dop[b] = stack_heads(tile, True).astype(BF16)
        both = tile * r.oheads[b]
        first = jnp.sum(jnp.where(lo, both, 0.0), axis=1, keepdims=True)
        second = jnp.sum(jnp.where(lo, 0.0, both), axis=1, keepdims=True)
        delta = jnp.concatenate([first, second], axis=0)
        lane = lax.broadcasted_iota(jnp.int32, (256, 128), 1)
        r.lse[b] = jnp.where(lane < 64, r.lse[b], delta)
        r.gslot[b] = jnp.zeros((256, 128), F32)
        return 0

    lax.fori_loop(0, 8, prepare_back, 0)

    def key_block(k, _):
        block = key_rows(r.kvbuf, k)
        bias = key_bias(r.vbuf, k)

        def one(b, acc, scores):
            weights = jnp.exp(scores - r.lse[b][:, 0:1])
            dweights = mm_nt(r.dop[b], block)
            dscores = (weights * (dweights - r.lse[b][:, 64:65])).astype(BF16)
            r.gslot[b] = r.gslot[b] + mm(dscores, block)
            return acc + mm_tn(weights.astype(BF16), r.dop[b]) + mm_tn(dscores, r.qpad[b])

        def edge(b, acc):
            return one(b, acc, mask_last(mm_nt(r.qpad[b], block), bias, b, d))

        acc = lax.fori_loop(2 * k, 2 * k + 2, edge, jnp.zeros((512, 128), F32))
        acc = lax.fori_loop(2 * k + 2, 8, lambda b, acc: one(b, acc, mm_nt(r.qpad[b], block) + bias), acc)
        r.dkvsend[pl.ds(4 * k, 4)] = acc.astype(BF16).reshape(4, 128, 128)
        for h in range(2):
            b = 2 * k + h
            done = r.gslot[b] * SCALE
            r.sendq[b] = jnp.where(lo, done[:128], pltpu.roll(done[128:], 64, 1)).astype(BF16)

            @pl.when(b != c)
            def _():
                remote(r.sendq.at[b], r.qbuf.at[c], r.sdq.at[b], r.rdq.at[c], (e_at, b, d)).start()
                for g in range(2):
                    to = 2 * b + g
                    remote(r.dkvsend.at[to], r.dkvbuf.at[p], r.sdkv.at[to], r.rdkv.at[p], (e_at, b, g)).start()

            @pl.when(b == c)
            def _():
                r.qbuf[c] = r.sendq[c]
                r.dkvbuf[p] = r.dkvsend[p]
                to = c * 2 + 1 - d
                remote(r.dkvsend.at[to], r.dkvbuf.at[p], r.sdkv.at[to], r.rdkv.at[p], (e_at, c, 1 - d)).start()

        return 0

    lax.fori_loop(0, 1, key_block, 0)
    scatter.near_out(0)
    lax.fori_loop(1, 4, key_block, 0)
    line_gather_finish(branch_gather, lambda i: r.rows.at[i], r.sb, r.rb)

    def wait_dq(i, _):
        b = lax.rem(c + 1 + i, 8)
        copy = remote(r.sendq.at[b], r.qbuf.at[b], r.sdq.at[b], r.rdq.at[b], (e_at, b, d))
        copy.wait_send()
        copy.wait_recv()
        return 0

    def wait_dkv(i, _):
        q = lax.rem(p + 1 + i, 16)
        copy = remote(
            r.dkvsend.at[q], r.dkvbuf.at[q], r.sdkv.at[q], r.rdkv.at[q], (e_at, lax.div(q, 2), lax.rem(q, 2))
        )
        copy.wait_send()
        copy.wait_recv()
        return 0

    lax.fori_loop(0, 7, wait_dq, 0)
    lax.fori_loop(0, 15, wait_dkv, 0)
    cos, sin = r.cosine[...], -r.sine[...]
    dq_tiles = []
    for t in range(8):
        tile = r.qbuf[t].astype(F32)
        dq_tiles.append(tile * cos + swap_halves(tile) * sin)
    dq = jnp.concatenate(dq_tiles, axis=1)
    q_pre = r.qpre[...]
    q_inv = inverse_rms(q_pre)
    dgain_q = jnp.sum(dq * (q_pre * q_inv), axis=0, keepdims=True)
    r.dqkv[0:128, :] = rms_back(q_pre, q_inv, dq * gain_row(gains, 1)).astype(BF16)
    r.big3[me, 0:128, :] = r.dqkv[0:128, :]
    dq_gather = line_gather_start(r.dqkv.at[q_part], lambda i: r.big3.at[i, q_part], r.sn, r.rn)
    dk_tiles, dv_tiles = [], []
    for t in range(4):
        even = r.dkvbuf[4 * t].astype(F32) + r.dkvbuf[4 * t + 1].astype(F32)
        odd = r.dkvbuf[4 * t + 2].astype(F32) + r.dkvbuf[4 * t + 3].astype(F32)
        tile = jnp.where(lo, even, pltpu.roll(odd, 64, 1))
        dk_tiles.append(tile * cos + swap_halves(tile) * sin)
        dv_tiles.append(jnp.where(lo, pltpu.roll(even, 64, 1), odd))
    dk = jnp.concatenate(dk_tiles, axis=1)
    k_pre = r.kpre[...]
    k_inv = inverse_rms(k_pre)
    dgain_k = jnp.sum(dk * (k_pre * k_inv), axis=0, keepdims=True)
    r.dqkv[128:256, 0:512] = rms_back(k_pre, k_inv, dk * key_gain_row(gains)).astype(BF16)
    r.dqkv[128:256, 512:1024] = jnp.concatenate(dv_tiles, axis=1).astype(BF16)
    r.big3[me, 128:256, :] = r.dqkv[128:256, :]
    dkv_gather = line_gather_start(r.dqkv.at[kv_part], lambda i: r.big3.at[i, kv_part], r.sn2, r.rn2)
    for j in range(1, 4):
        scatter.near_out(j)

    def out_grad(t, _):
        at = pl.ds(pl.multiple_of(512 * t, 512), 512)
        tiles = mm_tn(r.attx[...].reshape(1024, 128), r.rows[:, :, at].reshape(1024, 512)).astype(BF16)
        for i in range(4):
            r.pieces_o[pl.ds(8 * t + 2 * i, 2)] = tiles[:, 128 * i : 128 * i + 128].reshape(2, 64, 128)
        return 0

    lax.fori_loop(0, 2, out_grad, 0)
    p_copies_o = plane_sum_send(r.pieces_o, 1, r.pin_o, r.sp1, r.rp1)
    wall_back.wait()

    def normed_back(t, _):
        for i in range(2):
            part = slice(128 * i, 128 * i + 128)
            both = mm_nt(r.dqkv[part, :], wall[pl.ds(2 * t, 2), part, :].reshape(256, 1024))
            for h in range(2):
                tile = both[:, 128 * h : 128 * h + 128]
                r.dnorm[2 * t + h] = tile if i == 0 else r.dnorm[2 * t + h] + tile
        return 0

    lax.fori_loop(0, 4, normed_back, 0)
    dnormed = jnp.concatenate([r.dnorm[t] for t in range(8)], axis=1)
    values = r.tokens[...].astype(F32)
    inv = inverse_rms(values)
    dgain_in = jnp.sum(dnormed * (values * inv), axis=0, keepdims=True)
    r.gtok[...] = r.gtok[...] + rms_back(values, inv, dnormed * gain_row(gains, 0))
    for i in range(8):
        at = slice(128 * i, 128 * i + 128)
        r.smsend[i, 0:1, :] = dgain_in[:, at]
        r.smsend[i, 1:2, :] = dgain_q[:, at]
        r.smsend[i, 2:3, :] = dgain_mid[:, at]
        half = dgain_k[:, 128 * (i // 2) : 128 * (i // 2) + 128]
        r.smsend[i, 3:4, :] = half if i % 2 == 0 else pltpu.roll(jnp.broadcast_to(half, (8, 128)), 64, 1)[0:1]
        r.smsend[i, 4:6, :] = r.stats[0:2, :]
        r.smsend[i, 6:16, :] = jnp.zeros((10, 128), F32)
    sm_copies = []
    for o in range(1, 8):
        to = lax.rem(me + o, 8)
        copy = remote(r.smsend.at[to], r.sminbox.at[o], r.sms.at[o], r.rms.at[o], (to, c, d))
        copy.start()
        sm_copies.append(copy)
    for j in (4, 5, 0):
        scatter.near_sum(j)
    shares_o = plane_sum_share(p_copies_o, r.pieces_o, 1, r.pin_o, r.res_o, r.sp2, r.rp2)

    total = r.smsend[me]
    for at, copy in enumerate(sm_copies):
        copy.wait_recv()
        total = total + r.sminbox[at + 1]
    r.smsum[...] = total
    small_copies = []
    for o in range(1, 16):
        _, device = plane_peer(o)
        copy = remote(r.smsum, r.smplane.at[o], r.sp5.at[o], r.rp5.at[o], device)
        copy.start()
        small_copies.append(copy)

    def qkv_grad(part, pieces):
        def one(t, _):
            at = pl.ds(pl.multiple_of(512 * t, 512), 512)
            tiles = mm_tn(r.nx[...].reshape(1024, 128), r.big3[:, part, at].reshape(1024, 512)).astype(BF16)
            for i in range(4):
                pieces[pl.ds(8 * t + 2 * i, 2)] = tiles[:, 128 * i : 128 * i + 128].reshape(2, 64, 128)
            return 0

        lax.fori_loop(0, 2, one, 0)

    line_gather_finish(dq_gather, lambda i: r.big3.at[i, q_part], r.sn, r.rn)
    qkv_grad(slice(0, 128), r.pieces_q)
    p_copies_q = plane_sum_send(r.pieces_q, 1, r.pin_q, r.sp3, r.rp3)
    for j in range(1, 4):
        scatter.near_sum(j)
    scatter.far2()
    line_gather_finish(dkv_gather, lambda i: r.big3.at[i, kv_part], r.sn2, r.rn2)
    qkv_grad(slice(128, 256), r.pieces_n)
    p_copies_n = plane_sum_send(r.pieces_n, 1, r.pin_n, r.sp6, r.rp6)
    scatter.near2()
    shares_q = plane_sum_share(p_copies_q, r.pieces_q, 1, r.pin_q, r.res_q, r.sp4, r.rp4)
    shares_n = plane_sum_share(p_copies_n, r.pieces_n, 1, r.pin_n, r.res_n, r.sp7, r.rp7)
    for at, copy in enumerate(small_copies):
        copy.wait_recv()
        total = total + r.smplane[at + 1]
    r.gsmall[...] = total
    scatter.finish(r.gw)
    for copy in shares_o + shares_q + shares_n:
        copy.wait_recv()
    scatter.drain()
    for copy in (
        pair_copies + x_copies + d_copies + sm_copies
        + small_copies + p_copies_o + p_copies_q + p_copies_n + shares_o + shares_q + shares_n
    ):
        copy.wait_send()


def layer(*args):
    vm = pl.BlockSpec(memory_space=pltpu.VMEM)
    hbm = pl.BlockSpec(memory_space=pl.ANY)
    in_hbm = ("wq", "wk", "wv", "wo", "teacher")
    return pl.pallas_call(
        layer_kernel,
        out_shape=tuple(jax.ShapeDtypeStruct(shape, dtype) for _, shape, dtype in OUTPUTS + SPILLS),
        in_specs=[hbm if name in in_hbm else vm for name in INPUTS],
        out_specs=(vm,) * len(OUTPUTS) + (hbm,) * len(SPILLS),
        scratch_shapes=[pltpu.VMEM(shape, dtype) for _, shape, dtype in SCRATCH]
        + [pltpu.SemaphoreType.DMA((count,)) for _, count in SEMAPHORES],
        compiler_params=pltpu.CompilerParams(
            collective_id=0, has_side_effects=True, vmem_limit_bytes=64 << 20
        ),
        cost_estimate=pl.CostEstimate(flops=32 * 10**9, bytes_accessed=60 << 20, transcendentals=8 << 20),
        name="layer",
    )(*args)[: len(OUTPUTS)]


def finish_kernel(
    mixed, gtok, res_o_in, res_q_in, res_n_in, small_in, gw_in,
    mixed_out, loss, gtok_out, gnorm_in, gq, gk, gv, gq_gain, gk_gain, gout, gnorm_mid, grouter, ggate, gup, gdown,
    res_o, res_q, res_n, small, gw, sems,
):
    pairs = (
        (small_in, small), (res_o_in, res_o), (res_q_in, res_q), (res_n_in, res_n), (gw_in, gw),
        (mixed, mixed_out), (gtok, gtok_out),
    )
    copies = [pltpu.make_async_copy(src, dst, sems.at[i]) for i, (src, dst) in enumerate(pairs)]
    for copy in copies:
        copy.start()
    copies[0].wait()
    loss[...] = small[4:5, 0:1] / (small[5:6, 0:1] * 1024.0)
    gnorm_in[...] = small[0:1, :]
    gq_gain[...] = small[1:2, :]
    gnorm_mid[...] = small[2:3, :]
    gk_gain[...] = small[3:4, 0:64]
    grouter[...] = small[16:48, :]

    def tiles(ref, out, first, count):
        for t in range(count):
            n = 2 * (first + t)
            out[:, 128 * t : 128 * t + 128] = jnp.concatenate([ref[n], ref[n + 1]], axis=0).astype(F32)

    copies[1].wait()
    tiles(res_o, gout, 0, 8)
    copies[2].wait()
    tiles(res_q, gq, 0, 8)
    copies[3].wait()
    tiles(res_n, gk, 0, 4)
    tiles(res_n, gv, 4, 4)
    copies[4].wait()
    for e in range(4):
        ggate[:, e, :] = gw[e]
        gup[:, e, :] = gw[6 + e]
        gdown[:, e, :] = gw[4 + e + 4 * (e // 2)]
    for copy in copies[5:]:
        copy.wait()


def finish(*args):
    vm = pl.BlockSpec(memory_space=pltpu.VMEM)
    hbm = pl.BlockSpec(memory_space=pl.ANY)
    shapes = (
        (128, 1024), (1, 1), (128, 1024), (1, 128), (128, 1024), (128, 512), (128, 512), (1, 128), (1, 64), (128, 1024),
        (1, 128), (32, 128), (64, 4, 512), (64, 4, 512), (64, 4, 512),
    )
    return pl.pallas_call(
        finish_kernel,
        out_shape=tuple(jax.ShapeDtypeStruct(v, BF16 if i == 0 else F32) for i, v in enumerate(shapes)),
        in_specs=[hbm] * 7,
        out_specs=(vm,) * len(shapes),
        scratch_shapes=[
            pltpu.VMEM((16, 64, 128), BF16),
            pltpu.VMEM((16, 64, 128), BF16),
            pltpu.VMEM((16, 64, 128), BF16),
            pltpu.VMEM((48, 128), F32),
            pltpu.VMEM((12, 64, 512), F32),
            pltpu.SemaphoreType.DMA((7,)),
        ],
        compiler_params=pltpu.CompilerParams(vmem_limit_bytes=62 << 20),
        name="finish",
    )(*args)


def per_device(
    tokens,
    norm_in,
    w_query,
    w_key,
    w_value,
    query_gain,
    key_gain,
    w_out,
    norm_mid,
    w_router,
    expert_gate,
    expert_up,
    expert_down,
    routes,
    valid,
    teacher,
):
    positions = (lax.axis_index("ctx") * 2 + lax.axis_index("dp")) * 128 + jnp.arange(128, dtype=jnp.int32)
    lane = jnp.arange(128, dtype=jnp.int32)
    frequency = THETA ** (-((lane % 32).astype(F32) * (2.0 / HEAD)))
    angles = positions.astype(F32)[:, None] * frequency[None, :]
    sign = jnp.where(lane % 64 < 32, -1.0, 1.0)
    parts = layer(
        tokens, w_query, w_key, w_value, w_out, norm_in, query_gain, norm_mid, key_gain, w_router.T,
        expert_gate, expert_up, expert_down, valid, jnp.cos(angles), jnp.sin(angles) * sign, routes.T, teacher,
    )
    (
        mixed, loss, gtok, gnorm_in, gq, gk, gv, gq_gain, gk_gain, gout, gnorm_mid, grouter, ggate, gup, gdown
    ) = finish(*parts)
    return (
        mixed, loss.reshape(()), gtok, gnorm_in.reshape(128), gq, gk, gv, gq_gain.reshape(128), gk_gain.reshape(64), gout,
        gnorm_mid.reshape(128), grouter.T, ggate, gup, gdown,
    )


def solution(mesh):
    placed = (
        P(("expert", "ctx", "dp"), None),
        P("expert"),
        P("expert", None),
        P("expert", None),
        P("expert", None),
        P("expert"),
        P("expert"),
        P("expert", None),
        P("expert"),
        P("expert", None),
        P(("ctx", "dp"), "expert", None),
        P(("ctx", "dp"), "expert", None),
        P(("ctx", "dp"), "expert", None),
        P(("expert", "ctx", "dp"), None),
        P(("expert", "ctx", "dp")),
        P(("expert", "ctx", "dp"), None),
    )
    return jax.shard_map(
        per_device,
        mesh=mesh,
        in_specs=placed,
        out_specs=(
            P(("expert", "ctx", "dp"), None),
            P(),
            P(("expert", "ctx", "dp"), None),
            P("expert"),
            P("expert", None),
            P("expert", None),
            P("expert", None),
            P("expert"),
            P("expert"),
            P("expert", None),
            P("expert"),
            P("expert", None),
            P(("ctx", "dp"), "expert", None),
            P(("ctx", "dp"), "expert", None),
            P(("ctx", "dp"), "expert", None),
        ),
        check_vma=False,
    )
```

```python
import jax
import jax.numpy as jnp
from jax import lax
from jax.experimental import pallas as pl
from jax.experimental.pallas import tpu as pltpu
from jax.sharding import PartitionSpec as P

MESH = pl.DeviceIdType.MESH
F32 = jnp.float32
BF16 = jnp.bfloat16

HEAD = 64
TOP = 8
EPS = 1e-06
THETA = 10000.0
NEG = -1e30
SCALE = HEAD**-0.5


def mm(a, b):
    return lax.dot_general(a, b, (((1,), (0,)), ((), ())), preferred_element_type=F32)


def mm_nt(a, b):
    return lax.dot_general(a, b, (((1,), (1,)), ((), ())), preferred_element_type=F32)


def mm_tn(a, b):
    return lax.dot_general(a, b, (((0,), (0,)), ((), ())), preferred_element_type=F32)


def places():
    e, c, d = lax.axis_index("expert"), lax.axis_index("ctx"), lax.axis_index("dp")
    return e // 2, e % 2, c, d


def yz():
    c, d = lax.axis_index("ctx"), lax.axis_index("dp")
    return lax.rem(c, 4), lax.div(c, 4) * 2 + d


def remote(src, dst, send, recv, device):
    return pltpu.make_async_remote_copy(
        src_ref=src, dst_ref=dst, send_sem=send, recv_sem=recv, device_id=device, device_id_type=MESH
    )


def line_device(x, core):
    return (lax.rem(x + 4, 4) * 2 + core, lax.axis_index("ctx"), lax.axis_index("dp"))


def plane_device(y, z):
    return (lax.axis_index("expert"), lax.div(z, 2) * 4 + y, lax.rem(z, 2))


def plane_peer(o):
    e, c, d = lax.axis_index("expert"), lax.axis_index("ctx"), lax.axis_index("dp")
    q = lax.rem(c * 2 + d + o, 16)
    return q, (e, lax.div(q, 2), lax.rem(q, 2))


def greet_all():
    barrier = pltpu.get_barrier_semaphore()
    e, c, d = lax.axis_index("expert"), lax.axis_index("ctx"), lax.axis_index("dp")
    for o in range(1, 8):
        pl.semaphore_signal(barrier, inc=1, device_id=(lax.rem(e + o, 8), c, d), device_id_type=MESH)
    for o in range(1, 16):
        _, device = plane_peer(o)
        pl.semaphore_signal(barrier, inc=1, device_id=device, device_id_type=MESH)
    pl.semaphore_wait(barrier, 22)


def line_gather_start(own, buf, send, recv):
    x, core, _, _ = places()
    me = x * 2 + core
    copies = [remote(own, buf(me), send.at[o], recv.at[o], line_device(x + o, core)) for o in (2, 1, 3)]
    copies.append(remote(own, buf(me), send.at[0], recv.at[0], line_device(x, 1 - core)))
    for copy in copies:
        copy.start()
    return copies


def line_gather_finish(copies, buf, send, recv, use=None):
    x, core, _, _ = places()

    def used(o, c):
        if use is not None:
            use(lax.rem(x - o + 4, 4) * 2 + c)

    used(0, core)
    copies[3].wait_recv()
    used(0, 1 - core)
    forwards = []
    for at, o in ((1, 1), (2, 3), (0, 2)):
        copies[at].wait_recv()
        block = buf(lax.rem(x - o + 4, 4) * 2 + core)
        copy = remote(block, block, send.at[4 + o], recv.at[4 + o], line_device(x, 1 - core))
        copy.start()
        forwards.append((copy, o))
        used(o, core)
    for copy, o in forwards:
        copy.wait_recv()
        used(o, 1 - core)
    for copy in copies + [copy for copy, _ in forwards]:
        copy.wait_send()


def line_scatter(part, mine, pair, sib, inbox, send, recv):
    x, core, _, _ = places()
    copies, order = [], (2, 1, 3, 0)
    for o in order:
        at = lax.rem(x + o, 4)
        pair[at] = part(at * 2 + 1 - core).astype(BF16)
        copy = remote(pair.at[at], sib.at[at], send.at[o], recv.at[o], line_device(x, 1 - core))
        copy.start()
        copies.append(copy)
    out = []
    for n, o in enumerate(order):
        at = lax.rem(x + o, 4)
        own = part(at * 2 + core)
        copies[n].wait_recv()
        mine[at] = (own + sib[at].astype(F32)).astype(BF16)
        if o > 0:
            copy = remote(mine.at[at], inbox.at[o - 1], send.at[4 + o], recv.at[4 + o], line_device(x + o, core))
            copy.start()
            out.append(copy)
    return copies, out


def line_scatter_sum(mine, inbox, copies):
    x, _, _, _ = places()
    total = mine[x].astype(F32)
    for at, o in ((1, 1), (2, 3), (0, 2)):
        copies[at].wait_recv()
        total = total + inbox[o - 1].astype(F32)
    return total


def plane_sum_send(pieces, n, inbox, send, recv):
    copies = []
    for o in range(1, 16):
        q, device = plane_peer(o)
        copy = remote(pieces.at[pl.ds(q * n, n)], inbox.at[o], send.at[o], recv.at[o], device)
        copy.start()
        copies.append(copy)
    return copies


def plane_sum_share(copies, pieces, n, inbox, result, send, recv):
    p = lax.axis_index("ctx") * 2 + lax.axis_index("dp")
    total = pieces[pl.ds(p * n, n)].astype(F32)
    for at, copy in enumerate(copies):
        copy.wait_recv()
        total = total + inbox[at + 1].astype(F32)
    result[pl.ds(p * n, n)] = total.astype(BF16)
    shares = []
    view = result.at[pl.ds(p * n, n)]
    for o in range(1, 16):
        _, device = plane_peer(o)
        copy = remote(view, view, send.at[o], recv.at[o], device)
        copy.start()
        shares.append(copy)
    return shares


class Copies:
    def __init__(self, send, recv):
        self.send, self.recv = send, recv
        self.y, self.z = yz()
        self.copies = {}

    def go(self, n, src, dst, device):
        copy = remote(src, dst, self.send.at[n], self.recv.at[n], device)
        copy.start()
        self.copies[n] = copy

    def drain(self):
        for copy in self.copies.values():
            copy.wait_send()


class PlaneGather(Copies):
    def __init__(self, wg, send, recv):
        super().__init__(send, recv)
        self.wg = wg

    def place(self, m, y, z):
        return self.wg.at[m, lax.div(z, 2), y, lax.rem(z, 2)]

    def shards(self):
        y, z = self.y, self.z
        a, b = pl.ds(0, 6), pl.ds(6, 6)
        for i, o in enumerate((1, 3)):
            view = self.place(a, y, z)
            self.go(i, view, view, plane_device(lax.rem(y + o, 4), z))
            view = self.place(b, y, z)
            self.go(2 + i, view, view, plane_device(y, lax.rem(z + o, 4)))

    def shards_on(self):
        y, z = self.y, self.z
        a, b = pl.ds(0, 6), pl.ds(6, 6)
        for i, o in enumerate((1, 3)):
            rows = pl.ds(32 * i, 32)
            self.copies[i].wait_recv()
            view = self.place(a, lax.rem(y - o + 4, 4), z).at[:, rows]
            self.go(4 + i, view, view, plane_device(lax.rem(y + o, 4), z))
            self.copies[2 + i].wait_recv()
            view = self.place(b, y, lax.rem(z - o + 4, 4)).at[:, rows]
            self.go(6 + i, view, view, plane_device(y, lax.rem(z + o, 4)))

    def shards_wait(self):
        for n in range(4, 8):
            self.copies[n].wait_recv()

    def lines(self, j):
        y, z = self.y, self.z
        for i, o in enumerate((1, 3)):
            view = self.wg.at[j, lax.div(z, 2), :, lax.rem(z, 2)]
            self.go(8 + 8 * j + i, view, view, plane_device(y, lax.rem(z + o, 4)))
            view = self.wg.at[6 + j, :, y]
            self.go(10 + 8 * j + i, view, view, plane_device(lax.rem(y + o, 4), z))

    def lines_on(self, j):
        y, z = self.y, self.z
        for i, o in enumerate((1, 3)):
            self.copies[8 + 8 * j + i].wait_recv()
            from_z = lax.rem(z - o + 4, 4)
            view = self.wg.at[j, lax.div(from_z, 2), pl.ds(2 * i, 2), lax.rem(from_z, 2)]
            self.go(12 + 8 * j + i, view, view, plane_device(y, lax.rem(z + o, 4)))
            self.copies[10 + 8 * j + i].wait_recv()
            view = self.wg.at[6 + j, i, lax.rem(y - o + 4, 4)]
            self.go(14 + 8 * j + i, view, view, plane_device(lax.rem(y + o, 4), z))

    def lines_wait(self, j):
        for n in range(12 + 8 * j, 16 + 8 * j):
            self.copies[n].wait_recv()


class PlaneScatter(Copies):
    def __init__(self, dw, far_in, near_in, far2_in, near2_in, stage, load, send, recv):
        super().__init__(send, recv)
        self.dw, self.far_in, self.near_in = dw, far_in, near_in
        self.far2_in, self.near2_in, self.stage, self.load = far2_in, near2_in, stage, load

    def block(self, half, m, at):
        if half == 0:
            return self.dw.at[m, lax.div(at, 2), :, lax.rem(at, 2)]
        return self.dw.at[6 + m, :, at]

    def due(self, half, m, at):
        if half == 0:
            return self.dw.at[m, lax.div(self.z, 2), at, lax.rem(self.z, 2)]
        return self.dw.at[m, lax.div(at, 2), self.y, lax.rem(at, 2)]

    def device(self, half, at):
        return plane_device(self.y, at) if half == 0 else plane_device(at, self.z)

    def place(self, half):
        return self.z if half == 0 else self.y

    def far(self, j):
        for half in range(2):
            me = self.place(half)
            for i, o in enumerate((1, 3)):
                view = self.block(half, j, lax.rem(me + 2, 4))
                view = view.at[pl.ds(2 * i, 2)] if half == 0 else view.at[i]
                self.go(8 * j + 2 * half + i, view, self.far_in.at[half, i, j], self.device(half, lax.rem(me + o, 4)))

    def far_load(self, j, slot):
        loads = []
        for half in range(2):
            for i in range(2):
                self.copies[8 * j + 2 * half + i].wait_recv()
                spot = self.stage[0].at[i, pl.ds(2 * slot, 2)] if half == 0 else self.stage[1].at[i, slot]
                load = pltpu.make_async_copy(self.far_in.at[half, i, j], spot, self.load.at[4 * slot + 2 * half + i])
                load.start()
                loads.append((load, spot))
        return loads

    def near_out(self, *steps):
        loads = self.far_load(steps[0], 0)
        for n, j in enumerate(steps):
            now = loads
            if n + 1 < len(steps):
                loads = self.far_load(steps[n + 1], (n + 1) % 2)
            for half in range(2):
                me = self.place(half)
                for i, o in enumerate((1, 3)):
                    load, spot = now[2 * half + i]
                    load.wait()
                    to = lax.rem(me + o, 4)
                    whole = self.block(half, j, to)
                    part = whole.at[pl.ds(2 * i, 2)] if half == 0 else whole.at[i]
                    part[...] = part[...] + spot[...]
                    self.go(8 * j + 4 + 2 * half + i, whole, self.near_in[half].at[i, j], self.device(half, to))

    def near_load(self, j, half):
        loads = []
        for i in range(2):
            self.copies[8 * j + 4 + 2 * half + i].wait_recv()
            load = pltpu.make_async_copy(
                self.near_in[half].at[i, j], self.stage[half].at[i], self.load.at[2 * half + i]
            )
            load.start()
            loads.append(load)
        return loads

    def near_sum(self, *steps):
        loads = [self.near_load(steps[0], half) for half in range(2)]
        for n, j in enumerate(steps):
            for half in range(2):
                own, stage = self.block(half, j, self.place(half)), self.stage[half]
                for load in loads[half]:
                    load.wait()
                own[...] = own[...] + (stage[0] + stage[1])
                if n + 1 < len(steps):
                    loads[half] = self.near_load(steps[n + 1], half)

    def place2(self, half):
        return self.y if half == 0 else self.z

    def device2(self, half, at):
        return plane_device(at, self.z) if half == 0 else plane_device(self.y, at)

    def far2(self):
        for half in range(2):
            me = self.place2(half)
            for i, o in enumerate((1, 3)):
                view = self.due(half, pl.ds(6 * half, 6), lax.rem(me + 2, 4)).at[:, pl.ds(32 * i, 32)]
                self.go(48 + 2 * half + i, view, self.far2_in.at[half, i], self.device2(half, lax.rem(me + o, 4)))

    def near2(self):
        for half in range(2):
            me = self.place2(half)
            for i, o in enumerate((1, 3)):
                self.copies[48 + 2 * half + i].wait_recv()
                to = lax.rem(me + o, 4)

                def add(m, _):
                    part = self.due(half, 6 * half + m, to).at[pl.ds(32 * i, 32)]
                    part[...] = part[...] + self.far2_in[half, i, m]
                    return 0

                lax.fori_loop(0, 6, add, 0)
                view = self.due(half, pl.ds(6 * half, 6), to)
                self.go(52 + 2 * half + i, view, self.near2_in.at[half, i], self.device2(half, to))

    def finish(self, result):
        for half in range(2):
            me = self.place2(half)
            for i in range(2):
                self.copies[52 + 2 * half + i].wait_recv()

            def add(m, _):
                result[6 * half + m] = (
                    self.due(half, 6 * half + m, me)[...].astype(F32)
                    + self.near2_in[half, 0, m].astype(F32)
                    + self.near2_in[half, 1, m].astype(F32)
                )
                return 0

            lax.fori_loop(0, 6, add, 0)


def low_lanes():
    return lax.broadcasted_iota(jnp.int32, (128, 128), 1) < 64


def swap_halves(tile):
    lane = lax.rem(lax.broadcasted_iota(jnp.int32, (128, 128), 1), 64)
    return jnp.where(lane < 32, pltpu.roll(tile, 96, 1), pltpu.roll(tile, 32, 1))


def gain_row(small, row):
    return jnp.concatenate([small[i, row : row + 1, :] for i in range(8)], axis=1)


def key_gain_row(small):
    lane = lax.broadcasted_iota(jnp.int32, (1, 128), 1)
    return jnp.concatenate(
        [jnp.where(lane < 64, small[2 * t, 3:4, :], small[2 * t + 1, 3:4, :]) for t in range(4)], axis=1
    )


def router_rows(small):
    return jnp.concatenate([small[i, 16:48, :] for i in range(8)], axis=1)


def inverse_rms(values):
    return lax.rsqrt(jnp.mean(values * values, axis=1, keepdims=True) + EPS)


def rms_back(values, inverse, grad):
    hat = values * inverse
    return inverse * (grad - hat * jnp.mean(grad * hat, axis=1, keepdims=True))


def stack_heads(tile, upper):
    lo = low_lanes()
    turned = pltpu.roll(tile, 64, 1)
    first, second = (turned, tile) if upper else (tile, turned)
    keep = jnp.logical_not(lo) if upper else lo
    return jnp.concatenate([jnp.where(keep, first, 0.0), jnp.where(keep, second, 0.0)], axis=0)


def key_rows(kvbuf, k):
    return kvbuf[pl.ds(4 * k, 4)].reshape(512, 128)


def key_bias(vbuf, k):
    row = jnp.concatenate([vbuf[4 * k + i, 0:1, :] for i in range(4)], axis=1)
    return (row - 1.0) * 1e30


def mask_last(scores, bias, b, d):
    half = lax.rem(b, 2) * 256
    column = lax.broadcasted_iota(jnp.int32, (256, 512), 1)
    row = lax.rem(lax.broadcasted_iota(jnp.int32, (256, 512), 0), 128)
    masked = jnp.where(column < half + 256, scores + bias, NEG)
    return jnp.where(column == row + (half + 128 * d), scores, masked)


def down(e):
    return 4 + e + 4 * lax.div(e, 2)


class Refs:
    def __init__(self, names, refs):
        for name, ref in zip(names, refs, strict=True):
            setattr(self, name, ref)


INPUTS = (
    "tokens", "wq", "wk", "wv", "wo", "norm_in", "query_gain", "norm_mid", "key_gain", "w_router",
    "expert_gate", "expert_up", "expert_down", "valid", "cosine", "sine", "routes", "teacher",
)
OUTPUTS = (
    ("mixed", (128, 1024), BF16),
    ("gtok", (128, 1024), F32),
    ("res_o", (16, 64, 128), BF16),
    ("res_q", (16, 64, 128), BF16),
    ("res_n", (16, 64, 128), BF16),
    ("gsmall", (48, 128), F32),
    ("gw", (12, 64, 512), F32),
)
SPILLS = (
    ("wall_keep", (8, 256, 1024), BF16),
    ("far_in", (2, 2, 6, 2, 64, 512), BF16),
    ("near_in_a", (2, 6, 4, 64, 512), BF16),
    ("near_in_b", (2, 6, 2, 2, 64, 512), BF16),
)
SCRATCH = (
    ("big1", (8, 256, 1024), BF16),
    ("big2", (8, 256, 1024), BF16),
    ("big3", (8, 256, 1024), BF16),
    ("rows", (8, 128, 1024), BF16),
    ("wo_all", (8, 128, 1024), BF16),
    ("wg", (12, 2, 4, 2, 64, 512), BF16),
    ("gbuf", (4, 512, 512), BF16),
    ("ubuf", (4, 512, 512), BF16),
    ("mine", (4, 128, 1024), BF16),
    ("pair", (4, 128, 1024), BF16),
    ("sib", (4, 128, 1024), BF16),
    ("inbox", (3, 128, 1024), BF16),
    ("stage_a", (2, 4, 64, 512), BF16),
    ("stage_b", (2, 2, 2, 64, 512), BF16),
    ("far2_in", (2, 2, 6, 32, 512), BF16),
    ("near2_in", (2, 2, 6, 64, 512), BF16),
    ("small_all", (8, 48, 128), BF16),
    ("vbuf", (16, 8, 128), F32),
    ("kvbuf", (16, 128, 128), BF16),
    ("qbuf", (8, 128, 128), BF16),
    ("oheads", (8, 128, 128), F32),
    ("lse", (8, 256, 128), F32),
    ("att", (8, 128, 128), BF16),
    ("attx", (8, 128, 128), BF16),
    ("normed_t", (8, 128, 128), BF16),
    ("nx", (8, 128, 128), BF16),
    ("sendq", (8, 128, 128), BF16),
    ("osend", (8, 128, 128), BF16),
    ("residual", (128, 1024), F32),
    ("qpre", (128, 1024), F32),
    ("kpre", (128, 512), F32),
    ("midl", (128, 1024), BF16),
    ("low", (128, 1024), BF16),
    ("meta", (8, 8, 128), F32),
    ("metasend", (8, 8, 128), F32),
    ("probs", (32, 128), F32),
    ("picks", (32, 128), F32),
    ("stats", (8, 128), F32),
    ("pcat", (8, 256, 128), BF16),
    ("gslot", (8, 256, 128), F32),
    ("dgates", (8, 8, 128), F32),
    ("dgsend", (8, 8, 128), F32),
    ("dattbuf", (8, 128, 128), BF16),
    ("qpad", (8, 256, 128), BF16),
    ("dop", (8, 256, 128), BF16),
    ("dkvsend", (16, 128, 128), BF16),
    ("dkvbuf", (16, 128, 128), BF16),
    ("dqkv", (256, 1024), BF16),
    ("dnorm", (8, 128, 128), F32),
    ("dlog", (64, 128), BF16),
    ("smsend", (8, 48, 128), F32),
    ("sminbox", (8, 48, 128), F32),
    ("smsum", (48, 128), F32),
    ("smplane", (16, 48, 128), F32),
    ("pieces_o", (16, 64, 128), BF16),
    ("pin_o", (16, 1, 64, 128), BF16),
    ("pieces_q", (16, 64, 128), BF16),
    ("pin_q", (16, 1, 64, 128), BF16),
    ("pieces_n", (16, 64, 128), BF16),
    ("pin_n", (16, 1, 64, 128), BF16),
)
SEMAPHORES = (
    ("own_sem", 6), ("keep_sem", 2), ("teacher_sem", 1), ("load_sem", 8),
    ("ssm", 8), ("rsm", 8), ("skvw", 8), ("rkvw", 8), ("sqw", 8), ("rqw", 8), ("swo", 8), ("rwo", 8), ("sv", 16), ("rv", 16),
    ("sew", 56), ("rew", 56), ("snx", 8), ("rnx", 8), ("sax", 8), ("rax", 8),
    ("skv", 16), ("rkv", 16), ("sq", 8), ("rq", 8), ("so", 8), ("ro", 8), ("sx", 8), ("rx", 8), ("sm", 8), ("rm", 8),
    ("s1", 8), ("r1", 8), ("s2", 8), ("r2", 8), ("s3", 8), ("r3", 8), ("s4", 8), ("r4", 8),
    ("sw", 56), ("rw", 56), ("sd", 8), ("rd", 8), ("sdq", 8), ("rdq", 8), ("sdkv", 16), ("rdkv", 16),
    ("sb", 8), ("rb", 8), ("sn", 8), ("rn", 8), ("sn2", 8), ("rn2", 8), ("sms", 8), ("rms", 8),
    ("sp1", 16), ("rp1", 16), ("sp2", 16), ("rp2", 16), ("sp3", 16), ("rp3", 16), ("sp4", 16), ("rp4", 16),
    ("sp5", 16), ("rp5", 16), ("sp6", 16), ("rp6", 16), ("sp7", 16), ("rp7", 16),
)
NAMES = INPUTS + tuple(n for part in (OUTPUTS, SPILLS, SCRATCH, SEMAPHORES) for n, *_ in part)


def layer_kernel(*refs):
    r = Refs(NAMES, refs)
    x, core, c, d = places()
    me = x * 2 + core
    p = c * 2 + d
    y, z = yz()
    e_at = lax.axis_index("expert")
    lo = low_lanes()

    wall = r.big1
    own = [
        pltpu.make_async_copy(r.wq, wall.at[me, pl.ds(0, 128)], r.own_sem.at[0]),
        pltpu.make_async_copy(r.wk, wall.at[me, pl.ds(128, 128), pl.ds(0, 512)], r.own_sem.at[1]),
        pltpu.make_async_copy(r.wv, wall.at[me, pl.ds(128, 128), pl.ds(512, 512)], r.own_sem.at[2]),
        pltpu.make_async_copy(r.wo, r.wo_all.at[me], r.own_sem.at[3]),
    ]
    for copy in own:
        copy.start()
    teacher_load = pltpu.make_async_copy(r.teacher, r.gtok, r.teacher_sem.at[0])
    teacher_load.start()
    eye = lax.broadcasted_iota(jnp.int32, (128, 128), 0) == lax.broadcasted_iota(jnp.int32, (128, 128), 1)
    rows = [ref[...].astype(F32).reshape(1, 128) for ref in (r.norm_in, r.query_gain, r.norm_mid)]
    key_row = r.key_gain[...].astype(F32).reshape(1, 64)
    rows += [jnp.concatenate([key_row, key_row], axis=1), jnp.zeros((12, 128), F32), r.w_router[...].astype(F32)]
    r.small_all[me] = jnp.concatenate(rows, axis=0).astype(BF16)
    valid_row = r.valid[...].astype(F32).reshape(1, 128)
    r.vbuf[p] = jnp.broadcast_to(valid_row, (8, 128))
    greet_all()

    gather = PlaneGather(r.wg, r.sew, r.rew)
    small_gather = line_gather_start(r.small_all.at[me], lambda i: r.small_all.at[i], r.ssm, r.rsm)
    for copy in own[:3]:
        copy.wait()
    kv_part, q_part = pl.ds(128, 128), pl.ds(0, 128)
    kv_gather = line_gather_start(wall.at[me, kv_part], lambda i: wall.at[i, kv_part], r.skvw, r.rkvw)
    q_gather = line_gather_start(wall.at[me, q_part], lambda i: wall.at[i, q_part], r.sqw, r.rqw)
    for ref, first in ((r.expert_gate, (0, 1, 2, 3)), (r.expert_up, (6, 7, 8, 9)), (r.expert_down, (4, 5, 10, 11))):
        whole = ref[...].astype(F32)
        for e, m in enumerate(first):
            r.wg[m, lax.div(z, 2), y, lax.rem(z, 2)] = whole[:, e, :].astype(BF16)
    gather.shards()
    own[3].wait()
    out_gather = line_gather_start(r.wo_all.at[me], lambda i: r.wo_all.at[i], r.swo, r.rwo)
    valid_copies = []
    for o in range(1, 16):
        _, device = plane_peer(o)
        copy = remote(r.vbuf.at[p], r.vbuf.at[p], r.sv.at[o], r.rv.at[o], device)
        copy.start()
        valid_copies.append(copy)

    line_gather_finish(small_gather, lambda i: r.small_all.at[i], r.ssm, r.rsm)
    gains = r.small_all[...].astype(F32)
    values = r.tokens[...].astype(F32)
    normed = (values * inverse_rms(values) * gain_row(gains, 0)).astype(BF16)
    for t in range(8):
        r.normed_t[t] = normed[:, 128 * t : 128 * t + 128]
    r.nx[me] = r.normed_t[me]
    spread_copies = []
    for o in range(1, 8):
        to = lax.rem(me + o, 8)
        copy = remote(r.normed_t.at[to], r.nx.at[me], r.snx.at[o], r.rnx.at[o], (to, c, d))
        copy.start()
        spread_copies.append(copy)
    gather.shards_on()
    gather.shards_wait()

    line_gather_finish(kv_gather, lambda i: wall.at[i, kv_part], r.skvw, r.rkvw)
    kv_pre = mm(normed, wall[:, 128:256, :].reshape(1024, 1024))
    k_pre = kv_pre[:, 0:512]
    v_low = kv_pre[:, 512:1024].astype(BF16).astype(F32)
    r.kpre[...] = k_pre
    cos, sin = r.cosine[...], r.sine[...]
    kn = k_pre * inverse_rms(k_pre) * key_gain_row(gains)
    for t in range(4):
        tile = kn[:, 128 * t : 128 * t + 128]
        k_rot = tile * cos + swap_halves(tile) * sin
        v_tile = v_low[:, 128 * t : 128 * t + 128]
        r.dkvsend[2 * t] = jnp.where(lo, k_rot, pltpu.roll(v_tile, 64, 1)).astype(BF16)
        r.dkvsend[2 * t + 1] = jnp.where(lo, pltpu.roll(k_rot, 64, 1), v_tile).astype(BF16)
    r.kvbuf[p] = r.dkvsend[c]
    kv_copies = []
    for o in range(1, 16):
        q, device = plane_peer(o)
        copy = remote(r.dkvsend.at[lax.div(q, 2)], r.kvbuf.at[p], r.skv.at[o], r.rkv.at[o], device)
        copy.start()
        kv_copies.append(copy)
    for j in range(2):
        gather.lines(j)
    line_gather_finish(q_gather, lambda i: wall.at[i, q_part], r.sqw, r.rqw)
    q_pre = mm(normed, wall[:, 0:128, :].reshape(1024, 1024))
    r.qpre[...] = q_pre
    qn = q_pre * inverse_rms(q_pre) * gain_row(gains, 1)
    for t in range(8):
        tile = qn[:, 128 * t : 128 * t + 128]
        r.sendq[t] = (tile * cos + swap_halves(tile) * sin).astype(BF16)
    r.qbuf[c] = r.sendq[c]
    q_copies = []
    for o in range(1, 8):
        to = lax.rem(c + o, 8)
        copy = remote(r.sendq.at[to], r.qbuf.at[c], r.sq.at[o], r.rq.at[o], (e_at, to, d))
        copy.start()
        q_copies.append(copy)
    keep = pltpu.make_async_copy(wall, r.wall_keep, r.keep_sem.at[0])
    keep.start()
    for j in range(2):
        gather.lines_on(j)
    gather.lines(2)
    for copy in valid_copies + kv_copies + q_copies:
        copy.wait()

    def prepare(b, _):
        r.qpad[b] = (stack_heads(r.qbuf[b].astype(F32), False) * SCALE).astype(BF16)
        return 0

    lax.fori_loop(0, 8, prepare, 0)

    def chunk(i, _):
        b = lax.rem(c + 1 + i, 8)
        queries = r.qpad[b]
        last = lax.div(b, 2)

        def update(carry, block, scores):
            top, total, acc = carry
            new_top = jnp.maximum(top, jnp.max(scores, axis=1, keepdims=True))
            weights = jnp.exp(scores - new_top)
            shrink = jnp.exp(top - new_top)
            total = total * shrink + jnp.sum(weights, axis=1, keepdims=True)
            acc = acc * shrink + mm(weights.astype(BF16), block)
            return (new_top, total, acc)

        def keys(k, carry):
            block = key_rows(r.kvbuf, k)
            return update(carry, block, mm_nt(queries, block) + key_bias(r.vbuf, k))

        zero = jnp.zeros((256, 1), F32)
        carry = lax.fori_loop(0, last, keys, (zero + NEG, zero, jnp.zeros((256, 128), F32)))
        block = key_rows(r.kvbuf, last)
        scores = mask_last(mm_nt(queries, block), key_bias(r.vbuf, last), b, d)
        top, total, acc = update(carry, block, scores)
        acc = acc / total
        r.lse[b] = jnp.broadcast_to(top + jnp.log(total), (256, 128))
        merged = jnp.where(lo, pltpu.roll(acc[:128], 64, 1), acc[128:])
        r.oheads[b] = merged
        r.osend[b] = merged.astype(BF16)

        @pl.when(b != c)
        def _():
            remote(r.osend.at[b], r.att.at[c], r.so.at[b], r.ro.at[c], (e_at, b, d)).start()

        @pl.when(b == c)
        def _():
            r.att[c] = r.osend[c]

        return 0

    lax.fori_loop(0, 4, chunk, 0)
    gather.lines_on(2)
    lax.fori_loop(4, 8, chunk, 0)
    line_gather_finish(out_gather, lambda i: r.wo_all.at[i], r.swo, r.rwo)

    def wait_rest(i, _):
        b = lax.rem(c + 1 + i, 8)
        copy = remote(r.osend.at[b], r.att.at[b], r.so.at[b], r.ro.at[b], (e_at, b, d))
        copy.wait_send()
        copy.wait_recv()
        return 0

    lax.fori_loop(0, 7, wait_rest, 0)
    gather.lines(3)
    gather.lines(4)
    r.attx[me] = r.att[me]
    for o in range(1, 8):
        to = lax.rem(me + o, 8)
        copy = remote(r.att.at[to], r.attx.at[me], r.sax.at[o], r.rax.at[o], (to, c, d))
        copy.start()
        spread_copies.append(copy)
    attended = jnp.concatenate([r.att[t] for t in range(8)], axis=1)
    res = r.tokens[...].astype(F32) + mm(attended, r.wo_all[...].reshape(1024, 1024))
    r.residual[...] = res
    mid = (res * inverse_rms(res) * gain_row(gains, 2)).astype(BF16)
    r.midl[...] = mid
    r.rows[me] = mid
    mid_gather = line_gather_start(r.midl, lambda i: r.rows.at[i], r.sx, r.rx)

    logits = mm_nt(router_rows(r.small_all[...]), mid)
    terms = jnp.exp(logits - jnp.max(logits, axis=0, keepdims=True))
    probs = terms / jnp.sum(terms, axis=0, keepdims=True)
    ids = lax.broadcasted_iota(jnp.int32, (32, 128), 0).astype(F32)
    routes = r.routes[...].astype(F32)
    picks = jnp.zeros((32, 128), F32)
    for k in range(TOP):
        picks = picks + (ids == routes[k : k + 1, :]).astype(F32)
    before = lax.broadcasted_iota(jnp.int32, (128, 128), 0) < lax.broadcasted_iota(jnp.int32, (128, 128), 1)
    slots = mm(picks.astype(BF16), before.astype(F32).astype(BF16))
    slots = jnp.where(picks > 0.0, slots, -1.0)
    r.probs[...] = probs
    r.picks[...] = picks
    gates = probs * picks
    for i in range(8):
        r.metasend[i, 0:4, :] = gates[4 * i : 4 * i + 4, :]
        r.metasend[i, 4:8, :] = slots[4 * i : 4 * i + 4, :]
    r.meta[me] = r.metasend[me]
    meta_copies = []
    for o in range(1, 8):
        to = lax.rem(me + o, 8)
        copy = remote(r.metasend.at[to], r.meta.at[me], r.sm.at[o], r.rm.at[o], (to, c, d))
        copy.start()
        meta_copies.append(copy)
    gather.lines_on(3)
    gather.lines(5)
    for copy in meta_copies:
        copy.wait()
    keep.wait()

    slot_ids = lax.broadcasted_iota(jnp.int32, (64, 128), 0).astype(F32)

    def compact(s):
        for e in range(4):
            hit = slot_ids == r.meta[s, 4 + e : 5 + e, :]
            at = slice(e * 64, (e + 1) * 64)
            r.pcat[s, at, :] = hit.astype(F32).astype(BF16)
            gate = jnp.sum(jnp.where(hit, r.meta[s, e : e + 1, :], 0.0), axis=1, keepdims=True)
            r.gslot[s, at, :] = jnp.broadcast_to(gate, (64, 128))
        r.big1[s] = mm(r.pcat[s], r.rows[s]).astype(BF16)

    line_gather_finish(mid_gather, lambda i: r.rows.at[i], r.sx, r.rx, compact)
    gather.lines_on(4)

    def slots_of(e):
        return pl.ds(pl.multiple_of(e * 64, 64), 64)

    def expert_rows(ref, e):
        return ref[:, slots_of(e), :].reshape(512, ref.shape[2])

    def weight(m):
        return r.wg[m].reshape(1024, 512)

    def forward_in(e, _):
        rows = expert_rows(r.big1, e)
        g = mm(rows, weight(e))
        u = mm(rows, weight(6 + e))
        r.gbuf[e] = g.astype(BF16)
        r.ubuf[e] = u.astype(BF16)
        r.big3[:, slots_of(e), 0:512] = (g * jax.nn.sigmoid(g) * u).astype(BF16).reshape(8, 64, 512)
        return 0

    def forward_out(e, _):
        act = r.big3[:, slots_of(e), 0:512].reshape(512, 512)
        gate = expert_rows(r.gslot, e)[:, 0:1]
        r.big3[:, slots_of(e), :] = (mm_nt(act, weight(down(e))) * gate).astype(BF16).reshape(8, 64, 1024)
        return 0

    for e in range(4):
        if e == 1:
            gather.lines_on(5)
        gather.lines_wait(e)
        forward_in(e, 0)
    for e in range(4):
        if e % 2 == 0:
            gather.lines_wait(4 + e // 2)
        forward_out(2 * (e % 2) + e // 2, 0)

    def combine(s):
        return mm_tn(r.pcat[s], r.big3[s])

    pair_copies, x_copies = line_scatter(combine, r.mine, r.pair, r.sib, r.inbox, r.s1, r.r1)
    teacher_load.wait()
    out = r.residual[...] + line_scatter_sum(r.mine, r.inbox, x_copies)
    r.mixed[...] = out.astype(BF16)
    valid_row = r.vbuf[p, 0:1, :]
    valid_col = jnp.sum(jnp.where(eye, valid_row, 0.0), axis=1, keepdims=True)
    err = (out - r.gtok[...]) * valid_col
    r.gtok[...] = err
    r.low[...] = err.astype(BF16)
    r.rows[me] = r.low[...]
    err_gather = line_gather_start(r.low, lambda i: r.rows.at[i], r.s2, r.r2)
    square = jnp.sum(jnp.sum(err * err, axis=1, keepdims=True), axis=0, keepdims=True)
    count = jnp.sum(valid_row, axis=1, keepdims=True)
    r.stats[0:1, :] = jnp.broadcast_to(square, (1, 128))
    r.stats[1:2, :] = jnp.broadcast_to(count, (1, 128))
    for copy in pair_copies + x_copies:
        copy.wait_send()

    def spread(s):
        r.big2[s] = mm(r.pcat[s], r.rows[s]).astype(BF16)

    line_gather_finish(err_gather, lambda i: r.rows.at[i], r.s2, r.r2, spread)
    gather.drain()

    def store_grad(m, value):
        r.wg[m] = value.astype(BF16).reshape(2, 4, 2, 64, 512)

    def backward_act(e, _):
        g = r.gbuf[e].astype(F32)
        u = r.ubuf[e].astype(F32)
        sigma = jax.nn.sigmoid(g)
        silu = g * sigma
        gate = expert_rows(r.gslot, e)[:, 0:1]
        raw = mm(expert_rows(r.big2, e), weight(down(e)))
        act = silu * u
        dgate = jnp.sum(raw * act, axis=1, keepdims=True)
        r.gslot[:, slots_of(e), :] = jnp.broadcast_to(dgate, (512, 128)).reshape(8, 64, 128)
        r.big3[:, slots_of(e), 0:512] = (act * gate).astype(BF16).reshape(8, 64, 512)
        da = raw * gate
        r.gbuf[e] = (da * u * (sigma * (1.0 + g * (1.0 - sigma)))).astype(BF16)
        r.ubuf[e] = (da * silu).astype(BF16)
        return 0

    def backward_down(e, _):
        gated = r.big3[:, slots_of(e), 0:512].reshape(512, 512)
        store_grad(down(e), mm_tn(expert_rows(r.big2, e), gated))
        return 0

    def backward_in(e, _):
        dx = mm_nt(r.gbuf[e], weight(e)) + mm_nt(r.ubuf[e], weight(6 + e))
        r.big3[:, slots_of(e), :] = dx.astype(BF16).reshape(8, 64, 1024)
        return 0

    scatter = PlaneScatter(
        r.wg, r.far_in, (r.near_in_a, r.near_in_b), r.far2_in, r.near2_in, (r.stage_a, r.stage_b), r.load_sem, r.sw, r.rw
    )
    lax.fori_loop(0, 4, backward_act, 0)
    lax.fori_loop(0, 4, backward_down, 0)
    scatter.far(4)
    scatter.far(5)
    lax.fori_loop(0, 4, backward_in, 0)
    pair_copies, x_copies = line_scatter(combine, r.mine, r.pair, r.sib, r.inbox, r.s3, r.r3)

    def gate_rows(s, _):
        for e in range(4):
            hit = r.pcat[s, e * 64 : (e + 1) * 64, :].astype(F32)
            r.dgsend[s, e : e + 1, :] = jnp.sum(hit * r.gslot[s, e * 64 : (e + 1) * 64, :], axis=0, keepdims=True)
        return 0

    lax.fori_loop(0, 8, gate_rows, 0)
    gate_copies = []
    for o in range(1, 8):
        to = lax.rem(me + o, 8)
        copy = remote(r.dgsend.at[to], r.dgates.at[me], r.s4.at[o], r.r4.at[o], (to, c, d))
        copy.start()
        gate_copies.append(copy)
    r.dgates[me] = r.dgsend[me]
    for e in range(4):
        rows = r.big1[:, 64 * e : 64 * e + 64, :].reshape(512, 1024)
        store_grad(e, mm_tn(rows, r.gbuf[e]))
        store_grad(6 + e, mm_tn(rows, r.ubuf[e]))
        scatter.far(e)
    wall_back = pltpu.make_async_copy(r.wall_keep, wall, r.keep_sem.at[1])
    wall_back.start()
    dmid = line_scatter_sum(r.mine, r.inbox, x_copies)
    for copy in gate_copies:
        copy.wait()

    probs = r.probs[...]
    dprobs = jnp.concatenate([r.dgates[i, 0:4, :] for i in range(8)], axis=0) * r.picks[...]
    dlogits = probs * (dprobs - jnp.sum(probs * dprobs, axis=0, keepdims=True))
    high = dlogits.astype(BF16)
    r.dlog[0:32, :] = high
    r.dlog[32:64, :] = (dlogits - high.astype(F32)).astype(BF16)

    def router_back(i, _):
        at = pl.ds(pl.multiple_of(128 * i, 128), 128)
        part = mm(r.dlog[...], r.midl[:, at])
        r.smsend[i, 16:48, :] = part[:32] + part[32:]
        router = r.small_all[i, 16:48, :]
        r.dnorm[i] = mm_tn(r.dlog[...], jnp.concatenate([router, router], axis=0))
        return 0

    lax.fori_loop(0, 8, router_back, 0)
    gains = r.small_all[...].astype(F32)
    dmid = dmid + jnp.concatenate([r.dnorm[i] for i in range(8)], axis=1)
    res = r.residual[...]
    res_inv = inverse_rms(res)
    dgain_mid = jnp.sum(dmid * (res * res_inv), axis=0, keepdims=True)
    dres = r.gtok[...] + rms_back(res, res_inv, dmid * gain_row(gains, 2))
    r.gtok[...] = dres
    r.low[...] = dres.astype(BF16)

    def attended_back(t, _):
        both = mm_nt(r.low[...], r.wo_all[pl.ds(2 * t, 2)].reshape(256, 1024)).astype(BF16)
        for h in range(2):
            r.osend[2 * t + h] = both[:, 128 * h : 128 * h + 128]
        return 0

    lax.fori_loop(0, 4, attended_back, 0)
    r.dattbuf[c] = r.osend[c]
    d_copies = []
    for o in range(1, 8):
        to = lax.rem(c + o, 8)
        copy = remote(r.osend.at[to], r.dattbuf.at[c], r.sd.at[o], r.rd.at[o], (e_at, to, d))
        copy.start()
        d_copies.append(copy)
    r.rows[me] = r.low[...]
    branch_gather = line_gather_start(r.low, lambda i: r.rows.at[i], r.sb, r.rb)
    scatter.near_out(4, 5)
    for copy in spread_copies:
        copy.wait()
    for copy in d_copies:
        copy.wait_recv()

    def prepare_back(b, _):
        tile = r.dattbuf[b].astype(F32)
        r.dop[b] = stack_heads(tile, True).astype(BF16)
        both = tile * r.oheads[b]
        first = jnp.sum(jnp.where(lo, both, 0.0), axis=1, keepdims=True)
        second = jnp.sum(jnp.where(lo, 0.0, both), axis=1, keepdims=True)
        delta = jnp.concatenate([first, second], axis=0)
        lane = lax.broadcasted_iota(jnp.int32, (256, 128), 1)
        r.lse[b] = jnp.where(lane < 64, r.lse[b], delta)
        r.gslot[b] = jnp.zeros((256, 128), F32)
        return 0

    lax.fori_loop(0, 8, prepare_back, 0)

    def key_block(k, _):
        block = key_rows(r.kvbuf, k)
        bias = key_bias(r.vbuf, k)

        def one(b, acc, scores):
            weights = jnp.exp(scores - r.lse[b][:, 0:1])
            dweights = mm_nt(r.dop[b], block)
            dscores = (weights * (dweights - r.lse[b][:, 64:65])).astype(BF16)
            r.gslot[b] = r.gslot[b] + mm(dscores, block)
            return acc + mm_tn(weights.astype(BF16), r.dop[b]) + mm_tn(dscores, r.qpad[b])

        def edge(b, acc):
            return one(b, acc, mask_last(mm_nt(r.qpad[b], block), bias, b, d))

        acc = lax.fori_loop(2 * k, 2 * k + 2, edge, jnp.zeros((512, 128), F32))
        acc = lax.fori_loop(2 * k + 2, 8, lambda b, acc: one(b, acc, mm_nt(r.qpad[b], block) + bias), acc)
        r.dkvsend[pl.ds(4 * k, 4)] = acc.astype(BF16).reshape(4, 128, 128)
        for h in range(2):
            b = 2 * k + h
            done = r.gslot[b] * SCALE
            r.sendq[b] = jnp.where(lo, done[:128], pltpu.roll(done[128:], 64, 1)).astype(BF16)

            @pl.when(b != c)
            def _():
                remote(r.sendq.at[b], r.qbuf.at[c], r.sdq.at[b], r.rdq.at[c], (e_at, b, d)).start()
                for g in range(2):
                    to = 2 * b + g
                    remote(r.dkvsend.at[to], r.dkvbuf.at[p], r.sdkv.at[to], r.rdkv.at[p], (e_at, b, g)).start()

            @pl.when(b == c)
            def _():
                r.qbuf[c] = r.sendq[c]
                r.dkvbuf[p] = r.dkvsend[p]
                to = c * 2 + 1 - d
                remote(r.dkvsend.at[to], r.dkvbuf.at[p], r.sdkv.at[to], r.rdkv.at[p], (e_at, c, 1 - d)).start()

        return 0

    lax.fori_loop(0, 1, key_block, 0)
    scatter.near_out(0)
    lax.fori_loop(1, 4, key_block, 0)
    line_gather_finish(branch_gather, lambda i: r.rows.at[i], r.sb, r.rb)

    def wait_dq(i, _):
        b = lax.rem(c + 1 + i, 8)
        copy = remote(r.sendq.at[b], r.qbuf.at[b], r.sdq.at[b], r.rdq.at[b], (e_at, b, d))
        copy.wait_send()
        copy.wait_recv()
        return 0

    def wait_dkv(i, _):
        q = lax.rem(p + 1 + i, 16)
        copy = remote(
            r.dkvsend.at[q], r.dkvbuf.at[q], r.sdkv.at[q], r.rdkv.at[q], (e_at, lax.div(q, 2), lax.rem(q, 2))
        )
        copy.wait_send()
        copy.wait_recv()
        return 0

    lax.fori_loop(0, 7, wait_dq, 0)
    lax.fori_loop(0, 15, wait_dkv, 0)
    cos, sin = r.cosine[...], -r.sine[...]
    dq_tiles = []
    for t in range(8):
        tile = r.qbuf[t].astype(F32)
        dq_tiles.append(tile * cos + swap_halves(tile) * sin)
    dq = jnp.concatenate(dq_tiles, axis=1)
    q_pre = r.qpre[...]
    q_inv = inverse_rms(q_pre)
    dgain_q = jnp.sum(dq * (q_pre * q_inv), axis=0, keepdims=True)
    r.dqkv[0:128, :] = rms_back(q_pre, q_inv, dq * gain_row(gains, 1)).astype(BF16)
    r.big3[me, 0:128, :] = r.dqkv[0:128, :]
    dq_gather = line_gather_start(r.dqkv.at[q_part], lambda i: r.big3.at[i, q_part], r.sn, r.rn)
    dk_tiles, dv_tiles = [], []
    for t in range(4):
        even = r.dkvbuf[4 * t].astype(F32) + r.dkvbuf[4 * t + 1].astype(F32)
        odd = r.dkvbuf[4 * t + 2].astype(F32) + r.dkvbuf[4 * t + 3].astype(F32)
        tile = jnp.where(lo, even, pltpu.roll(odd, 64, 1))
        dk_tiles.append(tile * cos + swap_halves(tile) * sin)
        dv_tiles.append(jnp.where(lo, pltpu.roll(even, 64, 1), odd))
    dk = jnp.concatenate(dk_tiles, axis=1)
    k_pre = r.kpre[...]
    k_inv = inverse_rms(k_pre)
    dgain_k = jnp.sum(dk * (k_pre * k_inv), axis=0, keepdims=True)
    r.dqkv[128:256, 0:512] = rms_back(k_pre, k_inv, dk * key_gain_row(gains)).astype(BF16)
    r.dqkv[128:256, 512:1024] = jnp.concatenate(dv_tiles, axis=1).astype(BF16)
    r.big3[me, 128:256, :] = r.dqkv[128:256, :]
    dkv_gather = line_gather_start(r.dqkv.at[kv_part], lambda i: r.big3.at[i, kv_part], r.sn2, r.rn2)
    scatter.near_out(1, 2, 3)

    def out_grad(t, _):
        at = pl.ds(pl.multiple_of(512 * t, 512), 512)
        tiles = mm_tn(r.attx[...].reshape(1024, 128), r.rows[:, :, at].reshape(1024, 512)).astype(BF16)
        for i in range(4):
            r.pieces_o[pl.ds(8 * t + 2 * i, 2)] = tiles[:, 128 * i : 128 * i + 128].reshape(2, 64, 128)
        return 0

    lax.fori_loop(0, 2, out_grad, 0)
    p_copies_o = plane_sum_send(r.pieces_o, 1, r.pin_o, r.sp1, r.rp1)
    wall_back.wait()

    def normed_back(t, _):
        for i in range(2):
            part = slice(128 * i, 128 * i + 128)
            both = mm_nt(r.dqkv[part, :], wall[pl.ds(2 * t, 2), part, :].reshape(256, 1024))
            for h in range(2):
                tile = both[:, 128 * h : 128 * h + 128]
                r.dnorm[2 * t + h] = tile if i == 0 else r.dnorm[2 * t + h] + tile
        return 0

    lax.fori_loop(0, 4, normed_back, 0)
    dnormed = jnp.concatenate([r.dnorm[t] for t in range(8)], axis=1)
    values = r.tokens[...].astype(F32)
    inv = inverse_rms(values)
    dgain_in = jnp.sum(dnormed * (values * inv), axis=0, keepdims=True)
    r.gtok[...] = r.gtok[...] + rms_back(values, inv, dnormed * gain_row(gains, 0))
    for i in range(8):
        at = slice(128 * i, 128 * i + 128)
        r.smsend[i, 0:1, :] = dgain_in[:, at]
        r.smsend[i, 1:2, :] = dgain_q[:, at]
        r.smsend[i, 2:3, :] = dgain_mid[:, at]
        half = dgain_k[:, 128 * (i // 2) : 128 * (i // 2) + 128]
        r.smsend[i, 3:4, :] = half if i % 2 == 0 else pltpu.roll(jnp.broadcast_to(half, (8, 128)), 64, 1)[0:1]
        r.smsend[i, 4:6, :] = r.stats[0:2, :]
        r.smsend[i, 6:16, :] = jnp.zeros((10, 128), F32)
    sm_copies = []
    for o in range(1, 8):
        to = lax.rem(me + o, 8)
        copy = remote(r.smsend.at[to], r.sminbox.at[o], r.sms.at[o], r.rms.at[o], (to, c, d))
        copy.start()
        sm_copies.append(copy)
    scatter.near_sum(4, 5, 0)
    shares_o = plane_sum_share(p_copies_o, r.pieces_o, 1, r.pin_o, r.res_o, r.sp2, r.rp2)

    total = r.smsend[me]
    for at, copy in enumerate(sm_copies):
        copy.wait_recv()
        total = total + r.sminbox[at + 1]
    r.smsum[...] = total
    small_copies = []
    for o in range(1, 16):
        _, device = plane_peer(o)
        copy = remote(r.smsum, r.smplane.at[o], r.sp5.at[o], r.rp5.at[o], device)
        copy.start()
        small_copies.append(copy)

    def qkv_grad(part, pieces):
        def one(t, _):
            at = pl.ds(pl.multiple_of(512 * t, 512), 512)
            tiles = mm_tn(r.nx[...].reshape(1024, 128), r.big3[:, part, at].reshape(1024, 512)).astype(BF16)
            for i in range(4):
                pieces[pl.ds(8 * t + 2 * i, 2)] = tiles[:, 128 * i : 128 * i + 128].reshape(2, 64, 128)
            return 0

        lax.fori_loop(0, 2, one, 0)

    line_gather_finish(dq_gather, lambda i: r.big3.at[i, q_part], r.sn, r.rn)
    qkv_grad(slice(0, 128), r.pieces_q)
    p_copies_q = plane_sum_send(r.pieces_q, 1, r.pin_q, r.sp3, r.rp3)
    scatter.near_sum(1, 2, 3)
    scatter.far2()
    line_gather_finish(dkv_gather, lambda i: r.big3.at[i, kv_part], r.sn2, r.rn2)
    qkv_grad(slice(128, 256), r.pieces_n)
    p_copies_n = plane_sum_send(r.pieces_n, 1, r.pin_n, r.sp6, r.rp6)
    scatter.near2()
    shares_q = plane_sum_share(p_copies_q, r.pieces_q, 1, r.pin_q, r.res_q, r.sp4, r.rp4)
    shares_n = plane_sum_share(p_copies_n, r.pieces_n, 1, r.pin_n, r.res_n, r.sp7, r.rp7)
    for at, copy in enumerate(small_copies):
        copy.wait_recv()
        total = total + r.smplane[at + 1]
    r.gsmall[...] = total
    scatter.finish(r.gw)
    for copy in shares_o + shares_q + shares_n:
        copy.wait_recv()
    scatter.drain()
    for copy in (
        pair_copies + x_copies + d_copies + sm_copies
        + small_copies + p_copies_o + p_copies_q + p_copies_n + shares_o + shares_q + shares_n
    ):
        copy.wait_send()


def layer(*args):
    vm = pl.BlockSpec(memory_space=pltpu.VMEM)
    hbm = pl.BlockSpec(memory_space=pl.ANY)
    in_hbm = ("wq", "wk", "wv", "wo", "teacher")
    return pl.pallas_call(
        layer_kernel,
        out_shape=tuple(jax.ShapeDtypeStruct(shape, dtype) for _, shape, dtype in OUTPUTS + SPILLS),
        in_specs=[hbm if name in in_hbm else vm for name in INPUTS],
        out_specs=(vm,) * len(OUTPUTS) + (hbm,) * len(SPILLS),
        scratch_shapes=[pltpu.VMEM(shape, dtype) for _, shape, dtype in SCRATCH]
        + [pltpu.SemaphoreType.DMA((count,)) for _, count in SEMAPHORES],
        compiler_params=pltpu.CompilerParams(
            collective_id=0, has_side_effects=True, vmem_limit_bytes=64 << 20
        ),
        cost_estimate=pl.CostEstimate(flops=32 * 10**9, bytes_accessed=60 << 20, transcendentals=8 << 20),
        name="layer",
    )(*args)[: len(OUTPUTS)]


def finish_kernel(
    mixed, gtok, res_o_in, res_q_in, res_n_in, small_in, gw_in,
    mixed_out, loss, gtok_out, gnorm_in, gq, gk, gv, gq_gain, gk_gain, gout, gnorm_mid, grouter, ggate, gup, gdown,
    res_o, res_q, res_n, small, gw, sems,
):
    pairs = (
        (small_in, small), (res_o_in, res_o), (res_q_in, res_q), (res_n_in, res_n), (gw_in, gw),
        (mixed, mixed_out), (gtok, gtok_out),
    )
    copies = [pltpu.make_async_copy(src, dst, sems.at[i]) for i, (src, dst) in enumerate(pairs)]
    for copy in copies:
        copy.start()
    copies[0].wait()
    loss[...] = small[4:5, 0:1] / (small[5:6, 0:1] * 1024.0)
    gnorm_in[...] = small[0:1, :]
    gq_gain[...] = small[1:2, :]
    gnorm_mid[...] = small[2:3, :]
    gk_gain[...] = small[3:4, 0:64]
    grouter[...] = small[16:48, :]

    def tiles(ref, out, first, count):
        for t in range(count):
            n = 2 * (first + t)
            out[:, 128 * t : 128 * t + 128] = jnp.concatenate([ref[n], ref[n + 1]], axis=0).astype(F32)

    copies[1].wait()
    tiles(res_o, gout, 0, 8)
    copies[2].wait()
    tiles(res_q, gq, 0, 8)
    copies[3].wait()
    tiles(res_n, gk, 0, 4)
    tiles(res_n, gv, 4, 4)
    copies[4].wait()
    for e in range(4):
        ggate[:, e, :] = gw[e]
        gup[:, e, :] = gw[6 + e]
        gdown[:, e, :] = gw[4 + e + 4 * (e // 2)]
    for copy in copies[5:]:
        copy.wait()


def finish(*args):
    vm = pl.BlockSpec(memory_space=pltpu.VMEM)
    hbm = pl.BlockSpec(memory_space=pl.ANY)
    shapes = (
        (128, 1024), (1, 1), (128, 1024), (1, 128), (128, 1024), (128, 512), (128, 512), (1, 128), (1, 64), (128, 1024),
        (1, 128), (32, 128), (64, 4, 512), (64, 4, 512), (64, 4, 512),
    )
    return pl.pallas_call(
        finish_kernel,
        out_shape=tuple(jax.ShapeDtypeStruct(v, BF16 if i == 0 else F32) for i, v in enumerate(shapes)),
        in_specs=[hbm] * 7,
        out_specs=(vm,) * len(shapes),
        scratch_shapes=[
            pltpu.VMEM((16, 64, 128), BF16),
            pltpu.VMEM((16, 64, 128), BF16),
            pltpu.VMEM((16, 64, 128), BF16),
            pltpu.VMEM((48, 128), F32),
            pltpu.VMEM((12, 64, 512), F32),
            pltpu.SemaphoreType.DMA((7,)),
        ],
        compiler_params=pltpu.CompilerParams(vmem_limit_bytes=62 << 20),
        name="finish",
    )(*args)


def per_device(
    tokens,
    norm_in,
    w_query,
    w_key,
    w_value,
    query_gain,
    key_gain,
    w_out,
    norm_mid,
    w_router,
    expert_gate,
    expert_up,
    expert_down,
    routes,
    valid,
    teacher,
):
    positions = (lax.axis_index("ctx") * 2 + lax.axis_index("dp")) * 128 + jnp.arange(128, dtype=jnp.int32)
    lane = jnp.arange(128, dtype=jnp.int32)
    frequency = THETA ** (-((lane % 32).astype(F32) * (2.0 / HEAD)))
    angles = positions.astype(F32)[:, None] * frequency[None, :]
    sign = jnp.where(lane % 64 < 32, -1.0, 1.0)
    parts = layer(
        tokens, w_query, w_key, w_value, w_out, norm_in, query_gain, norm_mid, key_gain, w_router.T,
        expert_gate, expert_up, expert_down, valid, jnp.cos(angles), jnp.sin(angles) * sign, routes.T, teacher,
    )
    (
        mixed, loss, gtok, gnorm_in, gq, gk, gv, gq_gain, gk_gain, gout, gnorm_mid, grouter, ggate, gup, gdown
    ) = finish(*parts)
    return (
        mixed, loss.reshape(()), gtok, gnorm_in.reshape(128), gq, gk, gv, gq_gain.reshape(128), gk_gain.reshape(64), gout,
        gnorm_mid.reshape(128), grouter.T, ggate, gup, gdown,
    )


def solution(mesh):
    placed = (
        P(("expert", "ctx", "dp"), None),
        P("expert"),
        P("expert", None),
        P("expert", None),
        P("expert", None),
        P("expert"),
        P("expert"),
        P("expert", None),
        P("expert"),
        P("expert", None),
        P(("ctx", "dp"), "expert", None),
        P(("ctx", "dp"), "expert", None),
        P(("ctx", "dp"), "expert", None),
        P(("expert", "ctx", "dp"), None),
        P(("expert", "ctx", "dp")),
        P(("expert", "ctx", "dp"), None),
    )
    return jax.shard_map(
        per_device,
        mesh=mesh,
        in_specs=placed,
        out_specs=(
            P(("expert", "ctx", "dp"), None),
            P(),
            P(("expert", "ctx", "dp"), None),
            P("expert"),
            P("expert", None),
            P("expert", None),
            P("expert", None),
            P("expert"),
            P("expert"),
            P("expert", None),
            P("expert"),
            P("expert", None),
            P(("ctx", "dp"), "expert", None),
            P(("ctx", "dp"), "expert", None),
            P(("ctx", "dp"), "expert", None),
        ),
        check_vma=False,
    )
```

```python
import jax
import jax.numpy as jnp
from jax import lax
from jax.experimental import pallas as pl
from jax.experimental.pallas import tpu as pltpu
from jax.sharding import PartitionSpec as P

MESH = pl.DeviceIdType.MESH
F32 = jnp.float32
BF16 = jnp.bfloat16

HEAD = 64
TOP = 8
EPS = 1e-06
THETA = 10000.0
NEG = -1e30
SCALE = HEAD**-0.5


def mm(a, b):
    return lax.dot_general(a, b, (((1,), (0,)), ((), ())), preferred_element_type=F32)


def mm_nt(a, b):
    return lax.dot_general(a, b, (((1,), (1,)), ((), ())), preferred_element_type=F32)


def mm_tn(a, b):
    return lax.dot_general(a, b, (((0,), (0,)), ((), ())), preferred_element_type=F32)


def places():
    e, c, d = lax.axis_index("expert"), lax.axis_index("ctx"), lax.axis_index("dp")
    return e // 2, e % 2, c, d


def yz():
    c, d = lax.axis_index("ctx"), lax.axis_index("dp")
    return lax.rem(c, 4), lax.div(c, 4) * 2 + d


def remote(src, dst, send, recv, device):
    return pltpu.make_async_remote_copy(
        src_ref=src, dst_ref=dst, send_sem=send, recv_sem=recv, device_id=device, device_id_type=MESH
    )


def line_device(x, core):
    return (lax.rem(x + 4, 4) * 2 + core, lax.axis_index("ctx"), lax.axis_index("dp"))


def plane_device(y, z):
    return (lax.axis_index("expert"), lax.div(z, 2) * 4 + y, lax.rem(z, 2))


def plane_peer(o):
    e, c, d = lax.axis_index("expert"), lax.axis_index("ctx"), lax.axis_index("dp")
    q = lax.rem(c * 2 + d + o, 16)
    return q, (e, lax.div(q, 2), lax.rem(q, 2))


def greet_all():
    barrier = pltpu.get_barrier_semaphore()
    e, c, d = lax.axis_index("expert"), lax.axis_index("ctx"), lax.axis_index("dp")
    for o in range(1, 8):
        pl.semaphore_signal(barrier, inc=1, device_id=(lax.rem(e + o, 8), c, d), device_id_type=MESH)
    for o in range(1, 16):
        _, device = plane_peer(o)
        pl.semaphore_signal(barrier, inc=1, device_id=device, device_id_type=MESH)
    pl.semaphore_wait(barrier, 22)


def line_gather_start(own, buf, send, recv):
    x, core, _, _ = places()
    me = x * 2 + core
    copies = [remote(own, buf(me), send.at[o], recv.at[o], line_device(x + o, core)) for o in (2, 1, 3)]
    copies.append(remote(own, buf(me), send.at[0], recv.at[0], line_device(x, 1 - core)))
    for copy in copies:
        copy.start()
    return copies


def line_gather_finish(copies, buf, send, recv, use=None):
    x, core, _, _ = places()

    def used(o, c):
        if use is not None:
            use(lax.rem(x - o + 4, 4) * 2 + c)

    used(0, core)
    copies[3].wait_recv()
    used(0, 1 - core)
    forwards = []
    for at, o in ((1, 1), (2, 3), (0, 2)):
        copies[at].wait_recv()
        block = buf(lax.rem(x - o + 4, 4) * 2 + core)
        copy = remote(block, block, send.at[4 + o], recv.at[4 + o], line_device(x, 1 - core))
        copy.start()
        forwards.append((copy, o))
        used(o, core)
    for copy, o in forwards:
        copy.wait_recv()
        used(o, 1 - core)
    for copy in copies + [copy for copy, _ in forwards]:
        copy.wait_send()


def line_scatter(part, mine, pair, sib, inbox, send, recv):
    x, core, _, _ = places()
    copies, order = [], (2, 1, 3, 0)
    for o in order:
        at = lax.rem(x + o, 4)
        pair[at] = part(at * 2 + 1 - core).astype(BF16)
        copy = remote(pair.at[at], sib.at[at], send.at[o], recv.at[o], line_device(x, 1 - core))
        copy.start()
        copies.append(copy)
    out = []
    for n, o in enumerate(order):
        at = lax.rem(x + o, 4)
        own = part(at * 2 + core)
        copies[n].wait_recv()
        mine[at] = (own + sib[at].astype(F32)).astype(BF16)
        if o > 0:
            copy = remote(mine.at[at], inbox.at[o - 1], send.at[4 + o], recv.at[4 + o], line_device(x + o, core))
            copy.start()
            out.append(copy)
    return copies, out


def line_scatter_sum(mine, inbox, copies):
    x, _, _, _ = places()
    total = mine[x].astype(F32)
    for at, o in ((1, 1), (2, 3), (0, 2)):
        copies[at].wait_recv()
        total = total + inbox[o - 1].astype(F32)
    return total


def plane_sum_send(pieces, n, inbox, send, recv):
    copies = []
    for o in range(1, 16):
        q, device = plane_peer(o)
        copy = remote(pieces.at[pl.ds(q * n, n)], inbox.at[o], send.at[o], recv.at[o], device)
        copy.start()
        copies.append(copy)
    return copies


def plane_sum_share(copies, pieces, n, inbox, result, send, recv):
    p = lax.axis_index("ctx") * 2 + lax.axis_index("dp")
    total = pieces[pl.ds(p * n, n)].astype(F32)
    for at, copy in enumerate(copies):
        copy.wait_recv()
        total = total + inbox[at + 1].astype(F32)
    result[pl.ds(p * n, n)] = total.astype(BF16)
    shares = []
    view = result.at[pl.ds(p * n, n)]
    for o in range(1, 16):
        _, device = plane_peer(o)
        copy = remote(view, view, send.at[o], recv.at[o], device)
        copy.start()
        shares.append(copy)
    return shares


class Copies:
    def __init__(self, send, recv):
        self.send, self.recv = send, recv
        self.y, self.z = yz()
        self.copies = {}

    def go(self, n, src, dst, device):
        copy = remote(src, dst, self.send.at[n], self.recv.at[n], device)
        copy.start()
        self.copies[n] = copy

    def drain(self):
        for copy in self.copies.values():
            copy.wait_send()


class PlaneGather(Copies):
    def __init__(self, wg, send, recv):
        super().__init__(send, recv)
        self.wg = wg

    def place(self, m, y, z):
        return self.wg.at[m, lax.div(z, 2), y, lax.rem(z, 2)]

    def shards(self):
        y, z = self.y, self.z
        a, b = pl.ds(0, 6), pl.ds(6, 6)
        for i, o in enumerate((1, 3)):
            view = self.place(a, y, z)
            self.go(i, view, view, plane_device(lax.rem(y + o, 4), z))
            view = self.place(b, y, z)
            self.go(2 + i, view, view, plane_device(y, lax.rem(z + o, 4)))

    def shards_on(self):
        y, z = self.y, self.z
        a, b = pl.ds(0, 6), pl.ds(6, 6)
        for i, o in enumerate((1, 3)):
            rows = pl.ds(32 * i, 32)
            self.copies[i].wait_recv()
            view = self.place(a, lax.rem(y - o + 4, 4), z).at[:, rows]
            self.go(4 + i, view, view, plane_device(lax.rem(y + o, 4), z))
            self.copies[2 + i].wait_recv()
            view = self.place(b, y, lax.rem(z - o + 4, 4)).at[:, rows]
            self.go(6 + i, view, view, plane_device(y, lax.rem(z + o, 4)))

    def shards_wait(self):
        for n in range(4, 8):
            self.copies[n].wait_recv()

    def lines(self, j):
        y, z = self.y, self.z
        for i, o in enumerate((1, 3)):
            view = self.wg.at[j, lax.div(z, 2), :, lax.rem(z, 2)]
            self.go(8 + 8 * j + i, view, view, plane_device(y, lax.rem(z + o, 4)))
            view = self.wg.at[6 + j, :, y]
            self.go(10 + 8 * j + i, view, view, plane_device(lax.rem(y + o, 4), z))

    def lines_on(self, j):
        y, z = self.y, self.z
        for i, o in enumerate((1, 3)):
            self.copies[8 + 8 * j + i].wait_recv()
            from_z = lax.rem(z - o + 4, 4)
            view = self.wg.at[j, lax.div(from_z, 2), pl.ds(2 * i, 2), lax.rem(from_z, 2)]
            self.go(12 + 8 * j + i, view, view, plane_device(y, lax.rem(z + o, 4)))
            self.copies[10 + 8 * j + i].wait_recv()
            view = self.wg.at[6 + j, i, lax.rem(y - o + 4, 4)]
            self.go(14 + 8 * j + i, view, view, plane_device(lax.rem(y + o, 4), z))

    def lines_wait(self, j):
        for n in range(12 + 8 * j, 16 + 8 * j):
            self.copies[n].wait_recv()


class PlaneScatter(Copies):
    def __init__(self, dw, far_in, near_in, far2_in, near2_in, stage, load, send, recv):
        super().__init__(send, recv)
        self.dw, self.far_in, self.near_in = dw, far_in, near_in
        self.far2_in, self.near2_in, self.stage, self.load = far2_in, near2_in, stage, load

    def block(self, half, m, at):
        if half == 0:
            return self.dw.at[m, lax.div(at, 2), :, lax.rem(at, 2)]
        return self.dw.at[6 + m, :, at]

    def due(self, half, m, at):
        if half == 0:
            return self.dw.at[m, lax.div(self.z, 2), at, lax.rem(self.z, 2)]
        return self.dw.at[m, lax.div(at, 2), self.y, lax.rem(at, 2)]

    def device(self, half, at):
        return plane_device(self.y, at) if half == 0 else plane_device(at, self.z)

    def place(self, half):
        return self.z if half == 0 else self.y

    def far(self, j):
        for half in range(2):
            me = self.place(half)
            for i, o in enumerate((1, 3)):
                view = self.block(half, j, lax.rem(me + 2, 4))
                view = view.at[pl.ds(2 * i, 2)] if half == 0 else view.at[i]
                self.go(8 * j + 2 * half + i, view, self.far_in.at[half, i, j], self.device(half, lax.rem(me + o, 4)))

    def far_load(self, j, slot):
        loads = []
        for half in range(2):
            for i in range(2):
                self.copies[8 * j + 2 * half + i].wait_recv()
                spot = self.stage[0].at[i, pl.ds(2 * slot, 2)] if half == 0 else self.stage[1].at[i, slot]
                load = pltpu.make_async_copy(self.far_in.at[half, i, j], spot, self.load.at[4 * slot + 2 * half + i])
                load.start()
                loads.append((load, spot))
        return loads

    def near_out(self, *steps):
        loads = self.far_load(steps[0], 0)
        for n, j in enumerate(steps):
            now = loads
            if n + 1 < len(steps):
                loads = self.far_load(steps[n + 1], (n + 1) % 2)
            for half in range(2):
                me = self.place(half)
                for i, o in enumerate((1, 3)):
                    load, spot = now[2 * half + i]
                    load.wait()
                    to = lax.rem(me + o, 4)
                    whole = self.block(half, j, to)
                    part = whole.at[pl.ds(2 * i, 2)] if half == 0 else whole.at[i]
                    part[...] = part[...] + spot[...]
                    self.go(8 * j + 4 + 2 * half + i, whole, self.near_in[half].at[i, j], self.device(half, to))

    def near_load(self, j, half):
        loads = []
        for i in range(2):
            self.copies[8 * j + 4 + 2 * half + i].wait_recv()
            load = pltpu.make_async_copy(
                self.near_in[half].at[i, j], self.stage[half].at[i], self.load.at[2 * half + i]
            )
            load.start()
            loads.append(load)
        return loads

    def near_sum(self, *steps):
        loads = [self.near_load(steps[0], half) for half in range(2)]
        for n, j in enumerate(steps):
            for half in range(2):
                own, stage = self.block(half, j, self.place(half)), self.stage[half]
                for load in loads[half]:
                    load.wait()
                own[...] = own[...] + (stage[0] + stage[1])
                if n + 1 < len(steps):
                    loads[half] = self.near_load(steps[n + 1], half)

    def place2(self, half):
        return self.y if half == 0 else self.z

    def device2(self, half, at):
        return plane_device(at, self.z) if half == 0 else plane_device(self.y, at)

    def far2(self):
        for half in range(2):
            me = self.place2(half)
            for i, o in enumerate((1, 3)):
                view = self.due(half, pl.ds(6 * half, 6), lax.rem(me + 2, 4)).at[:, pl.ds(32 * i, 32)]
                self.go(48 + 2 * half + i, view, self.far2_in.at[half, i], self.device2(half, lax.rem(me + o, 4)))

    def near2(self):
        for half in range(2):
            me = self.place2(half)
            for i, o in enumerate((1, 3)):
                self.copies[48 + 2 * half + i].wait_recv()
                to = lax.rem(me + o, 4)

                def add(m, _):
                    part = self.due(half, 6 * half + m, to).at[pl.ds(32 * i, 32)]
                    part[...] = part[...] + self.far2_in[half, i, m]
                    return 0

                lax.fori_loop(0, 6, add, 0)
                view = self.due(half, pl.ds(6 * half, 6), to)
                self.go(52 + 2 * half + i, view, self.near2_in.at[half, i], self.device2(half, to))

    def finish(self, result):
        for half in range(2):
            me = self.place2(half)
            for i in range(2):
                self.copies[52 + 2 * half + i].wait_recv()

            def add(m, _):
                result[6 * half + m] = (
                    self.due(half, 6 * half + m, me)[...].astype(F32)
                    + self.near2_in[half, 0, m].astype(F32)
                    + self.near2_in[half, 1, m].astype(F32)
                )
                return 0

            lax.fori_loop(0, 6, add, 0)


def low_lanes():
    return lax.broadcasted_iota(jnp.int32, (128, 128), 1) < 64


def swap_halves(tile):
    lane = lax.rem(lax.broadcasted_iota(jnp.int32, (128, 128), 1), 64)
    return jnp.where(lane < 32, pltpu.roll(tile, 96, 1), pltpu.roll(tile, 32, 1))


def gain_row(small, row):
    return jnp.concatenate([small[i, row : row + 1, :] for i in range(8)], axis=1)


def key_gain_row(small):
    lane = lax.broadcasted_iota(jnp.int32, (1, 128), 1)
    return jnp.concatenate(
        [jnp.where(lane < 64, small[2 * t, 3:4, :], small[2 * t + 1, 3:4, :]) for t in range(4)], axis=1
    )


def router_rows(small):
    return jnp.concatenate([small[i, 16:48, :] for i in range(8)], axis=1)


def inverse_rms(values):
    return lax.rsqrt(jnp.mean(values * values, axis=1, keepdims=True) + EPS)


def rms_back(values, inverse, grad):
    hat = values * inverse
    return inverse * (grad - hat * jnp.mean(grad * hat, axis=1, keepdims=True))


def stack_heads(tile, upper):
    lo = low_lanes()
    turned = pltpu.roll(tile, 64, 1)
    first, second = (turned, tile) if upper else (tile, turned)
    keep = jnp.logical_not(lo) if upper else lo
    return jnp.concatenate([jnp.where(keep, first, 0.0), jnp.where(keep, second, 0.0)], axis=0)


def key_rows(kvbuf, k):
    return kvbuf[pl.ds(4 * k, 4)].reshape(512, 128)


def key_bias(vbuf, k):
    row = jnp.concatenate([vbuf[4 * k + i, 0:1, :] for i in range(4)], axis=1)
    return (row - 1.0) * 1e30


def mask_last(scores, bias, b, d):
    half = lax.rem(b, 2) * 256
    column = lax.broadcasted_iota(jnp.int32, (256, 512), 1)
    row = lax.rem(lax.broadcasted_iota(jnp.int32, (256, 512), 0), 128)
    masked = jnp.where(column < half + 256, scores + bias, NEG)
    return jnp.where(column == row + (half + 128 * d), scores, masked)


def down(e):
    return 4 + e + 4 * lax.div(e, 2)


class Refs:
    def __init__(self, names, refs):
        for name, ref in zip(names, refs, strict=True):
            setattr(self, name, ref)


INPUTS = (
    "tokens", "wq", "wk", "wv", "wo", "norm_in", "query_gain", "norm_mid", "key_gain", "w_router",
    "expert_gate", "expert_up", "expert_down", "valid", "cosine", "sine", "routes", "teacher",
)
OUTPUTS = (
    ("mixed", (128, 1024), BF16),
    ("gtok", (128, 1024), F32),
    ("res_o", (16, 64, 128), BF16),
    ("res_q", (16, 64, 128), BF16),
    ("res_n", (16, 64, 128), BF16),
    ("gsmall", (48, 128), F32),
    ("gw", (12, 64, 512), F32),
)
SPILLS = (
    ("wall_keep", (8, 256, 1024), BF16),
    ("far_in", (2, 2, 6, 2, 64, 512), BF16),
    ("near_in_a", (2, 6, 4, 64, 512), BF16),
    ("near_in_b", (2, 6, 2, 2, 64, 512), BF16),
)
SCRATCH = (
    ("big1", (8, 256, 1024), BF16),
    ("big2", (8, 256, 1024), BF16),
    ("big3", (8, 256, 1024), BF16),
    ("rows", (8, 128, 1024), BF16),
    ("wo_all", (8, 128, 1024), BF16),
    ("wg", (12, 2, 4, 2, 64, 512), BF16),
    ("shard_gate", (64, 4, 512), BF16),
    ("shard_up", (64, 4, 512), BF16),
    ("shard_down", (64, 4, 512), BF16),
    ("gbuf", (4, 512, 512), BF16),
    ("ubuf", (4, 512, 512), BF16),
    ("mine", (4, 128, 1024), BF16),
    ("pair", (4, 128, 1024), BF16),
    ("sib", (4, 128, 1024), BF16),
    ("inbox", (3, 128, 1024), BF16),
    ("stage_a", (2, 4, 64, 512), BF16),
    ("stage_b", (2, 2, 2, 64, 512), BF16),
    ("far2_in", (2, 2, 6, 32, 512), BF16),
    ("near2_in", (2, 2, 6, 64, 512), BF16),
    ("small_all", (8, 48, 128), BF16),
    ("vbuf", (16, 8, 128), F32),
    ("kvbuf", (16, 128, 128), BF16),
    ("qbuf", (8, 128, 128), BF16),
    ("oheads", (8, 128, 128), F32),
    ("lse", (8, 256, 128), F32),
    ("att", (8, 128, 128), BF16),
    ("attx", (8, 128, 128), BF16),
    ("normed_t", (8, 128, 128), BF16),
    ("nx", (8, 128, 128), BF16),
    ("sendq", (8, 128, 128), BF16),
    ("osend", (8, 128, 128), BF16),
    ("residual", (128, 1024), F32),
    ("qpre", (128, 1024), F32),
    ("kpre", (128, 512), F32),
    ("midl", (128, 1024), BF16),
    ("low", (128, 1024), BF16),
    ("meta", (8, 8, 128), F32),
    ("metasend", (8, 8, 128), F32),
    ("probs", (32, 128), F32),
    ("picks", (32, 128), F32),
    ("stats", (8, 128), F32),
    ("pcat", (8, 256, 128), BF16),
    ("gslot", (8, 256, 128), F32),
    ("dgates", (8, 8, 128), F32),
    ("dgsend", (8, 8, 128), F32),
    ("dattbuf", (8, 128, 128), BF16),
    ("qpad", (8, 256, 128), BF16),
    ("dop", (8, 256, 128), BF16),
    ("dkvsend", (16, 128, 128), BF16),
    ("dkvbuf", (16, 128, 128), BF16),
    ("dqkv", (256, 1024), BF16),
    ("dnorm", (8, 128, 128), F32),
    ("dlog", (64, 128), BF16),
    ("smsend", (8, 48, 128), F32),
    ("sminbox", (8, 48, 128), F32),
    ("smsum", (48, 128), F32),
    ("smplane", (16, 48, 128), F32),
    ("pieces_o", (16, 64, 128), BF16),
    ("pin_o", (16, 1, 64, 128), BF16),
    ("pieces_q", (16, 64, 128), BF16),
    ("pin_q", (16, 1, 64, 128), BF16),
    ("pieces_n", (16, 64, 128), BF16),
    ("pin_n", (16, 1, 64, 128), BF16),
)
SEMAPHORES = (
    ("own_sem", 8), ("keep_sem", 2), ("teacher_sem", 1), ("load_sem", 8),
    ("ssm", 8), ("rsm", 8), ("skvw", 8), ("rkvw", 8), ("sqw", 8), ("rqw", 8), ("swo", 8), ("rwo", 8), ("sv", 16), ("rv", 16),
    ("sew", 56), ("rew", 56), ("snx", 8), ("rnx", 8), ("sax", 8), ("rax", 8),
    ("skv", 16), ("rkv", 16), ("sq", 8), ("rq", 8), ("so", 8), ("ro", 8), ("sx", 8), ("rx", 8), ("sm", 8), ("rm", 8),
    ("s1", 8), ("r1", 8), ("s2", 8), ("r2", 8), ("s3", 8), ("r3", 8), ("s4", 8), ("r4", 8),
    ("sw", 56), ("rw", 56), ("sd", 8), ("rd", 8), ("sdq", 8), ("rdq", 8), ("sdkv", 16), ("rdkv", 16),
    ("sb", 8), ("rb", 8), ("sn", 8), ("rn", 8), ("sn2", 8), ("rn2", 8), ("sms", 8), ("rms", 8),
    ("sp1", 16), ("rp1", 16), ("sp2", 16), ("rp2", 16), ("sp3", 16), ("rp3", 16), ("sp4", 16), ("rp4", 16),
    ("sp5", 16), ("rp5", 16), ("sp6", 16), ("rp6", 16), ("sp7", 16), ("rp7", 16),
)
NAMES = INPUTS + tuple(n for part in (OUTPUTS, SPILLS, SCRATCH, SEMAPHORES) for n, *_ in part)


def layer_kernel(*refs):
    r = Refs(NAMES, refs)
    x, core, c, d = places()
    me = x * 2 + core
    p = c * 2 + d
    y, z = yz()
    e_at = lax.axis_index("expert")
    lo = low_lanes()

    wall = r.big1
    own = [
        pltpu.make_async_copy(r.wq, wall.at[me, pl.ds(0, 128)], r.own_sem.at[0]),
        pltpu.make_async_copy(r.wk, wall.at[me, pl.ds(128, 128), pl.ds(0, 512)], r.own_sem.at[1]),
        pltpu.make_async_copy(r.wv, wall.at[me, pl.ds(128, 128), pl.ds(512, 512)], r.own_sem.at[2]),
        pltpu.make_async_copy(r.wo, r.wo_all.at[me], r.own_sem.at[3]),
        pltpu.make_async_copy(r.expert_gate, r.shard_gate, r.own_sem.at[4]),
        pltpu.make_async_copy(r.expert_up, r.shard_up, r.own_sem.at[5]),
        pltpu.make_async_copy(r.expert_down, r.shard_down, r.own_sem.at[6]),
    ]
    for copy in own:
        copy.start()
    teacher_load = pltpu.make_async_copy(r.teacher, r.gtok, r.teacher_sem.at[0])
    teacher_load.start()
    eye = lax.broadcasted_iota(jnp.int32, (128, 128), 0) == lax.broadcasted_iota(jnp.int32, (128, 128), 1)
    rows = [ref[...].astype(F32).reshape(1, 128) for ref in (r.norm_in, r.query_gain, r.norm_mid)]
    key_row = r.key_gain[...].astype(F32).reshape(1, 64)
    rows += [jnp.concatenate([key_row, key_row], axis=1), jnp.zeros((12, 128), F32), r.w_router[...].astype(F32)]
    r.small_all[me] = jnp.concatenate(rows, axis=0).astype(BF16)
    valid_row = r.valid[...].astype(F32).reshape(1, 128)
    r.vbuf[p] = jnp.broadcast_to(valid_row, (8, 128))
    greet_all()

    gather = PlaneGather(r.wg, r.sew, r.rew)
    small_gather = line_gather_start(r.small_all.at[me], lambda i: r.small_all.at[i], r.ssm, r.rsm)
    for copy in own[:3]:
        copy.wait()
    kv_part, q_part = pl.ds(128, 128), pl.ds(0, 128)
    kv_gather = line_gather_start(wall.at[me, kv_part], lambda i: wall.at[i, kv_part], r.skvw, r.rkvw)
    q_gather = line_gather_start(wall.at[me, q_part], lambda i: wall.at[i, q_part], r.sqw, r.rqw)
    for copy in own[4:]:
        copy.wait()
    for ref, first in ((r.shard_gate, (0, 1, 2, 3)), (r.shard_up, (6, 7, 8, 9)), (r.shard_down, (4, 5, 10, 11))):
        whole = ref[...].astype(F32)
        for e, m in enumerate(first):
            r.wg[m, lax.div(z, 2), y, lax.rem(z, 2)] = whole[:, e, :].astype(BF16)
    gather.shards()
    own[3].wait()
    out_gather = line_gather_start(r.wo_all.at[me], lambda i: r.wo_all.at[i], r.swo, r.rwo)
    valid_copies = []
    for o in range(1, 16):
        _, device = plane_peer(o)
        copy = remote(r.vbuf.at[p], r.vbuf.at[p], r.sv.at[o], r.rv.at[o], device)
        copy.start()
        valid_copies.append(copy)

    line_gather_finish(small_gather, lambda i: r.small_all.at[i], r.ssm, r.rsm)
    gains = r.small_all[...].astype(F32)
    values = r.tokens[...].astype(F32)
    normed = (values * inverse_rms(values) * gain_row(gains, 0)).astype(BF16)
    for t in range(8):
        r.normed_t[t] = normed[:, 128 * t : 128 * t + 128]
    r.nx[me] = r.normed_t[me]
    spread_copies = []
    for o in range(1, 8):
        to = lax.rem(me + o, 8)
        copy = remote(r.normed_t.at[to], r.nx.at[me], r.snx.at[o], r.rnx.at[o], (to, c, d))
        copy.start()
        spread_copies.append(copy)
    gather.shards_on()
    gather.shards_wait()

    line_gather_finish(kv_gather, lambda i: wall.at[i, kv_part], r.skvw, r.rkvw)
    kv_pre = mm(normed, wall[:, 128:256, :].reshape(1024, 1024))
    k_pre = kv_pre[:, 0:512]
    v_low = kv_pre[:, 512:1024].astype(BF16).astype(F32)
    r.kpre[...] = k_pre
    cos, sin = r.cosine[...], r.sine[...]
    kn = k_pre * inverse_rms(k_pre) * key_gain_row(gains)
    for t in range(4):
        tile = kn[:, 128 * t : 128 * t + 128]
        k_rot = tile * cos + swap_halves(tile) * sin
        v_tile = v_low[:, 128 * t : 128 * t + 128]
        r.dkvsend[2 * t] = jnp.where(lo, k_rot, pltpu.roll(v_tile, 64, 1)).astype(BF16)
        r.dkvsend[2 * t + 1] = jnp.where(lo, pltpu.roll(k_rot, 64, 1), v_tile).astype(BF16)
    r.kvbuf[p] = r.dkvsend[c]
    kv_copies = []
    for o in range(1, 16):
        q, device = plane_peer(o)
        copy = remote(r.dkvsend.at[lax.div(q, 2)], r.kvbuf.at[p], r.skv.at[o], r.rkv.at[o], device)
        copy.start()
        kv_copies.append(copy)
    for j in range(2):
        gather.lines(j)
    line_gather_finish(q_gather, lambda i: wall.at[i, q_part], r.sqw, r.rqw)
    q_pre = mm(normed, wall[:, 0:128, :].reshape(1024, 1024))
    r.qpre[...] = q_pre
    qn = q_pre * inverse_rms(q_pre) * gain_row(gains, 1)
    for t in range(8):
        tile = qn[:, 128 * t : 128 * t + 128]
        r.sendq[t] = (tile * cos + swap_halves(tile) * sin).astype(BF16)
    r.qbuf[c] = r.sendq[c]
    q_copies = []
    for o in range(1, 8):
        to = lax.rem(c + o, 8)
        copy = remote(r.sendq.at[to], r.qbuf.at[c], r.sq.at[o], r.rq.at[o], (e_at, to, d))
        copy.start()
        q_copies.append(copy)
    keep = pltpu.make_async_copy(wall, r.wall_keep, r.keep_sem.at[0])
    keep.start()
    for j in range(2):
        gather.lines_on(j)
    gather.lines(2)
    for copy in valid_copies + kv_copies + q_copies:
        copy.wait()

    def prepare(b, _):
        r.qpad[b] = (stack_heads(r.qbuf[b].astype(F32), False) * SCALE).astype(BF16)
        return 0

    lax.fori_loop(0, 8, prepare, 0)

    def chunk(i, _):
        b = lax.rem(c + 1 + i, 8)
        queries = r.qpad[b]
        last = lax.div(b, 2)

        def update(carry, block, scores):
            top, total, acc = carry
            new_top = jnp.maximum(top, jnp.max(scores, axis=1, keepdims=True))
            weights = jnp.exp(scores - new_top)
            shrink = jnp.exp(top - new_top)
            total = total * shrink + jnp.sum(weights, axis=1, keepdims=True)
            acc = acc * shrink + mm(weights.astype(BF16), block)
            return (new_top, total, acc)

        def keys(k, carry):
            block = key_rows(r.kvbuf, k)
            return update(carry, block, mm_nt(queries, block) + key_bias(r.vbuf, k))

        zero = jnp.zeros((256, 1), F32)
        carry = lax.fori_loop(0, last, keys, (zero + NEG, zero, jnp.zeros((256, 128), F32)))
        block = key_rows(r.kvbuf, last)
        scores = mask_last(mm_nt(queries, block), key_bias(r.vbuf, last), b, d)
        top, total, acc = update(carry, block, scores)
        acc = acc / total
        r.lse[b] = jnp.broadcast_to(top + jnp.log(total), (256, 128))
        merged = jnp.where(lo, pltpu.roll(acc[:128], 64, 1), acc[128:])
        r.oheads[b] = merged
        r.osend[b] = merged.astype(BF16)

        @pl.when(b != c)
        def _():
            remote(r.osend.at[b], r.att.at[c], r.so.at[b], r.ro.at[c], (e_at, b, d)).start()

        @pl.when(b == c)
        def _():
            r.att[c] = r.osend[c]

        return 0

    lax.fori_loop(0, 4, chunk, 0)
    gather.lines_on(2)
    lax.fori_loop(4, 8, chunk, 0)
    line_gather_finish(out_gather, lambda i: r.wo_all.at[i], r.swo, r.rwo)

    def wait_rest(i, _):
        b = lax.rem(c + 1 + i, 8)
        copy = remote(r.osend.at[b], r.att.at[b], r.so.at[b], r.ro.at[b], (e_at, b, d))
        copy.wait_send()
        copy.wait_recv()
        return 0

    lax.fori_loop(0, 7, wait_rest, 0)
    gather.lines(3)
    gather.lines(4)
    r.attx[me] = r.att[me]
    for o in range(1, 8):
        to = lax.rem(me + o, 8)
        copy = remote(r.att.at[to], r.attx.at[me], r.sax.at[o], r.rax.at[o], (to, c, d))
        copy.start()
        spread_copies.append(copy)
    attended = jnp.concatenate([r.att[t] for t in range(8)], axis=1)
    res = r.tokens[...].astype(F32) + mm(attended, r.wo_all[...].reshape(1024, 1024))
    r.residual[...] = res
    mid = (res * inverse_rms(res) * gain_row(gains, 2)).astype(BF16)
    r.midl[...] = mid
    r.rows[me] = mid
    mid_gather = line_gather_start(r.midl, lambda i: r.rows.at[i], r.sx, r.rx)

    logits = mm_nt(router_rows(r.small_all[...]), mid)
    terms = jnp.exp(logits - jnp.max(logits, axis=0, keepdims=True))
    probs = terms / jnp.sum(terms, axis=0, keepdims=True)
    ids = lax.broadcasted_iota(jnp.int32, (32, 128), 0).astype(F32)
    routes = r.routes[...].astype(F32)
    picks = jnp.zeros((32, 128), F32)
    for k in range(TOP):
        picks = picks + (ids == routes[k : k + 1, :]).astype(F32)
    before = lax.broadcasted_iota(jnp.int32, (128, 128), 0) < lax.broadcasted_iota(jnp.int32, (128, 128), 1)
    slots = mm(picks.astype(BF16), before.astype(F32).astype(BF16))
    slots = jnp.where(picks > 0.0, slots, -1.0)
    r.probs[...] = probs
    r.picks[...] = picks
    gates = probs * picks
    for i in range(8):
        r.metasend[i, 0:4, :] = gates[4 * i : 4 * i + 4, :]
        r.metasend[i, 4:8, :] = slots[4 * i : 4 * i + 4, :]
    r.meta[me] = r.metasend[me]
    meta_copies = []
    for o in range(1, 8):
        to = lax.rem(me + o, 8)
        copy = remote(r.metasend.at[to], r.meta.at[me], r.sm.at[o], r.rm.at[o], (to, c, d))
        copy.start()
        meta_copies.append(copy)
    gather.lines_on(3)
    gather.lines(5)
    for copy in meta_copies:
        copy.wait()
    keep.wait()

    slot_ids = lax.broadcasted_iota(jnp.int32, (64, 128), 0).astype(F32)

    def compact(s):
        for e in range(4):
            hit = slot_ids == r.meta[s, 4 + e : 5 + e, :]
            at = slice(e * 64, (e + 1) * 64)
            r.pcat[s, at, :] = hit.astype(F32).astype(BF16)
            gate = jnp.sum(jnp.where(hit, r.meta[s, e : e + 1, :], 0.0), axis=1, keepdims=True)
            r.gslot[s, at, :] = jnp.broadcast_to(gate, (64, 128))
        r.big1[s] = mm(r.pcat[s], r.rows[s]).astype(BF16)

    line_gather_finish(mid_gather, lambda i: r.rows.at[i], r.sx, r.rx, compact)
    gather.lines_on(4)

    def slots_of(e):
        return pl.ds(pl.multiple_of(e * 64, 64), 64)

    def expert_rows(ref, e):
        return ref[:, slots_of(e), :].reshape(512, ref.shape[2])

    def weight(m):
        return r.wg[m].reshape(1024, 512)

    def forward_in(e, _):
        rows = expert_rows(r.big1, e)
        g = mm(rows, weight(e))
        u = mm(rows, weight(6 + e))
        r.gbuf[e] = g.astype(BF16)
        r.ubuf[e] = u.astype(BF16)
        r.big3[:, slots_of(e), 0:512] = (g * jax.nn.sigmoid(g) * u).astype(BF16).reshape(8, 64, 512)
        return 0

    def forward_out(e, _):
        act = r.big3[:, slots_of(e), 0:512].reshape(512, 512)
        gate = expert_rows(r.gslot, e)[:, 0:1]
        r.big3[:, slots_of(e), :] = (mm_nt(act, weight(down(e))) * gate).astype(BF16).reshape(8, 64, 1024)
        return 0

    for e in range(4):
        if e == 1:
            gather.lines_on(5)
        gather.lines_wait(e)
        forward_in(e, 0)
    for e in range(4):
        if e % 2 == 0:
            gather.lines_wait(4 + e // 2)
        forward_out(2 * (e % 2) + e // 2, 0)

    def combine(s):
        return mm_tn(r.pcat[s], r.big3[s])

    pair_copies, x_copies = line_scatter(combine, r.mine, r.pair, r.sib, r.inbox, r.s1, r.r1)
    teacher_load.wait()
    out = r.residual[...] + line_scatter_sum(r.mine, r.inbox, x_copies)
    r.mixed[...] = out.astype(BF16)
    valid_row = r.vbuf[p, 0:1, :]
    valid_col = jnp.sum(jnp.where(eye, valid_row, 0.0), axis=1, keepdims=True)
    err = (out - r.gtok[...]) * valid_col
    r.gtok[...] = err
    r.low[...] = err.astype(BF16)
    r.rows[me] = r.low[...]
    err_gather = line_gather_start(r.low, lambda i: r.rows.at[i], r.s2, r.r2)
    square = jnp.sum(jnp.sum(err * err, axis=1, keepdims=True), axis=0, keepdims=True)
    count = jnp.sum(valid_row, axis=1, keepdims=True)
    r.stats[0:1, :] = jnp.broadcast_to(square, (1, 128))
    r.stats[1:2, :] = jnp.broadcast_to(count, (1, 128))
    for copy in pair_copies + x_copies:
        copy.wait_send()

    def spread(s):
        r.big2[s] = mm(r.pcat[s], r.rows[s]).astype(BF16)

    line_gather_finish(err_gather, lambda i: r.rows.at[i], r.s2, r.r2, spread)
    gather.drain()

    def store_grad(m, value):
        r.wg[m] = value.astype(BF16).reshape(2, 4, 2, 64, 512)

    def backward_act(e, _):
        g = r.gbuf[e].astype(F32)
        u = r.ubuf[e].astype(F32)
        sigma = jax.nn.sigmoid(g)
        silu = g * sigma
        gate = expert_rows(r.gslot, e)[:, 0:1]
        raw = mm(expert_rows(r.big2, e), weight(down(e)))
        act = silu * u
        dgate = jnp.sum(raw * act, axis=1, keepdims=True)
        r.gslot[:, slots_of(e), :] = jnp.broadcast_to(dgate, (512, 128)).reshape(8, 64, 128)
        r.big3[:, slots_of(e), 0:512] = (act * gate).astype(BF16).reshape(8, 64, 512)
        da = raw * gate
        r.gbuf[e] = (da * u * (sigma * (1.0 + g * (1.0 - sigma)))).astype(BF16)
        r.ubuf[e] = (da * silu).astype(BF16)
        return 0

    def backward_down(e, _):
        gated = r.big3[:, slots_of(e), 0:512].reshape(512, 512)
        store_grad(down(e), mm_tn(expert_rows(r.big2, e), gated))
        return 0

    def backward_in(e, _):
        dx = mm_nt(r.gbuf[e], weight(e)) + mm_nt(r.ubuf[e], weight(6 + e))
        r.big3[:, slots_of(e), :] = dx.astype(BF16).reshape(8, 64, 1024)
        return 0

    scatter = PlaneScatter(
        r.wg, r.far_in, (r.near_in_a, r.near_in_b), r.far2_in, r.near2_in, (r.stage_a, r.stage_b), r.load_sem, r.sw, r.rw
    )
    lax.fori_loop(0, 4, backward_act, 0)
    lax.fori_loop(0, 4, backward_down, 0)
    scatter.far(4)
    scatter.far(5)
    lax.fori_loop(0, 4, backward_in, 0)
    pair_copies, x_copies = line_scatter(combine, r.mine, r.pair, r.sib, r.inbox, r.s3, r.r3)

    def gate_rows(s, _):
        for e in range(4):
            hit = r.pcat[s, e * 64 : (e + 1) * 64, :].astype(F32)
            r.dgsend[s, e : e + 1, :] = jnp.sum(hit * r.gslot[s, e * 64 : (e + 1) * 64, :], axis=0, keepdims=True)
        return 0

    lax.fori_loop(0, 8, gate_rows, 0)
    gate_copies = []
    for o in range(1, 8):
        to = lax.rem(me + o, 8)
        copy = remote(r.dgsend.at[to], r.dgates.at[me], r.s4.at[o], r.r4.at[o], (to, c, d))
        copy.start()
        gate_copies.append(copy)
    r.dgates[me] = r.dgsend[me]
    for e in range(4):
        rows = r.big1[:, 64 * e : 64 * e + 64, :].reshape(512, 1024)
        store_grad(e, mm_tn(rows, r.gbuf[e]))
        store_grad(6 + e, mm_tn(rows, r.ubuf[e]))
        scatter.far(e)
    wall_back = pltpu.make_async_copy(r.wall_keep, wall, r.keep_sem.at[1])
    wall_back.start()
    dmid = line_scatter_sum(r.mine, r.inbox, x_copies)
    for copy in gate_copies:
        copy.wait()

    probs = r.probs[...]
    dprobs = jnp.concatenate([r.dgates[i, 0:4, :] for i in range(8)], axis=0) * r.picks[...]
    dlogits = probs * (dprobs - jnp.sum(probs * dprobs, axis=0, keepdims=True))
    high = dlogits.astype(BF16)
    r.dlog[0:32, :] = high
    r.dlog[32:64, :] = (dlogits - high.astype(F32)).astype(BF16)

    def router_back(i, _):
        at = pl.ds(pl.multiple_of(128 * i, 128), 128)
        part = mm(r.dlog[...], r.midl[:, at])
        r.smsend[i, 16:48, :] = part[:32] + part[32:]
        router = r.small_all[i, 16:48, :]
        r.dnorm[i] = mm_tn(r.dlog[...], jnp.concatenate([router, router], axis=0))
        return 0

    lax.fori_loop(0, 8, router_back, 0)
    gains = r.small_all[...].astype(F32)
    dmid = dmid + jnp.concatenate([r.dnorm[i] for i in range(8)], axis=1)
    res = r.residual[...]
    res_inv = inverse_rms(res)
    dgain_mid = jnp.sum(dmid * (res * res_inv), axis=0, keepdims=True)
    dres = r.gtok[...] + rms_back(res, res_inv, dmid * gain_row(gains, 2))
    r.gtok[...] = dres
    r.low[...] = dres.astype(BF16)

    def attended_back(t, _):
        both = mm_nt(r.low[...], r.wo_all[pl.ds(2 * t, 2)].reshape(256, 1024)).astype(BF16)
        for h in range(2):
            r.osend[2 * t + h] = both[:, 128 * h : 128 * h + 128]
        return 0

    lax.fori_loop(0, 4, attended_back, 0)
    r.dattbuf[c] = r.osend[c]
    d_copies = []
    for o in range(1, 8):
        to = lax.rem(c + o, 8)
        copy = remote(r.osend.at[to], r.dattbuf.at[c], r.sd.at[o], r.rd.at[o], (e_at, to, d))
        copy.start()
        d_copies.append(copy)
    r.rows[me] = r.low[...]
    branch_gather = line_gather_start(r.low, lambda i: r.rows.at[i], r.sb, r.rb)
    scatter.near_out(4, 5)
    for copy in spread_copies:
        copy.wait()
    for copy in d_copies:
        copy.wait_recv()

    def prepare_back(b, _):
        tile = r.dattbuf[b].astype(F32)
        r.dop[b] = stack_heads(tile, True).astype(BF16)
        both = tile * r.oheads[b]
        first = jnp.sum(jnp.where(lo, both, 0.0), axis=1, keepdims=True)
        second = jnp.sum(jnp.where(lo, 0.0, both), axis=1, keepdims=True)
        delta = jnp.concatenate([first, second], axis=0)
        lane = lax.broadcasted_iota(jnp.int32, (256, 128), 1)
        r.lse[b] = jnp.where(lane < 64, r.lse[b], delta)
        r.gslot[b] = jnp.zeros((256, 128), F32)
        return 0

    lax.fori_loop(0, 8, prepare_back, 0)

    def key_block(k, _):
        block = key_rows(r.kvbuf, k)
        bias = key_bias(r.vbuf, k)

        def one(b, acc, scores):
            weights = jnp.exp(scores - r.lse[b][:, 0:1])
            dweights = mm_nt(r.dop[b], block)
            dscores = (weights * (dweights - r.lse[b][:, 64:65])).astype(BF16)
            r.gslot[b] = r.gslot[b] + mm(dscores, block)
            return acc + mm_tn(weights.astype(BF16), r.dop[b]) + mm_tn(dscores, r.qpad[b])

        def edge(b, acc):
            return one(b, acc, mask_last(mm_nt(r.qpad[b], block), bias, b, d))

        acc = lax.fori_loop(2 * k, 2 * k + 2, edge, jnp.zeros((512, 128), F32))
        acc = lax.fori_loop(2 * k + 2, 8, lambda b, acc: one(b, acc, mm_nt(r.qpad[b], block) + bias), acc)
        r.dkvsend[pl.ds(4 * k, 4)] = acc.astype(BF16).reshape(4, 128, 128)
        for h in range(2):
            b = 2 * k + h
            done = r.gslot[b] * SCALE
            r.sendq[b] = jnp.where(lo, done[:128], pltpu.roll(done[128:], 64, 1)).astype(BF16)

            @pl.when(b != c)
            def _():
                remote(r.sendq.at[b], r.qbuf.at[c], r.sdq.at[b], r.rdq.at[c], (e_at, b, d)).start()
                for g in range(2):
                    to = 2 * b + g
                    remote(r.dkvsend.at[to], r.dkvbuf.at[p], r.sdkv.at[to], r.rdkv.at[p], (e_at, b, g)).start()

            @pl.when(b == c)
            def _():
                r.qbuf[c] = r.sendq[c]
                r.dkvbuf[p] = r.dkvsend[p]
                to = c * 2 + 1 - d
                remote(r.dkvsend.at[to], r.dkvbuf.at[p], r.sdkv.at[to], r.rdkv.at[p], (e_at, c, 1 - d)).start()

        return 0

    lax.fori_loop(0, 1, key_block, 0)
    scatter.near_out(0)
    lax.fori_loop(1, 4, key_block, 0)
    line_gather_finish(branch_gather, lambda i: r.rows.at[i], r.sb, r.rb)

    def wait_dq(i, _):
        b = lax.rem(c + 1 + i, 8)
        copy = remote(r.sendq.at[b], r.qbuf.at[b], r.sdq.at[b], r.rdq.at[b], (e_at, b, d))
        copy.wait_send()
        copy.wait_recv()
        return 0

    def wait_dkv(i, _):
        q = lax.rem(p + 1 + i, 16)
        copy = remote(
            r.dkvsend.at[q], r.dkvbuf.at[q], r.sdkv.at[q], r.rdkv.at[q], (e_at, lax.div(q, 2), lax.rem(q, 2))
        )
        copy.wait_send()
        copy.wait_recv()
        return 0

    lax.fori_loop(0, 7, wait_dq, 0)
    lax.fori_loop(0, 15, wait_dkv, 0)
    cos, sin = r.cosine[...], -r.sine[...]
    dq_tiles = []
    for t in range(8):
        tile = r.qbuf[t].astype(F32)
        dq_tiles.append(tile * cos + swap_halves(tile) * sin)
    dq = jnp.concatenate(dq_tiles, axis=1)
    q_pre = r.qpre[...]
    q_inv = inverse_rms(q_pre)
    dgain_q = jnp.sum(dq * (q_pre * q_inv), axis=0, keepdims=True)
    r.dqkv[0:128, :] = rms_back(q_pre, q_inv, dq * gain_row(gains, 1)).astype(BF16)
    r.big3[me, 0:128, :] = r.dqkv[0:128, :]
    dq_gather = line_gather_start(r.dqkv.at[q_part], lambda i: r.big3.at[i, q_part], r.sn, r.rn)
    dk_tiles, dv_tiles = [], []
    for t in range(4):
        even = r.dkvbuf[4 * t].astype(F32) + r.dkvbuf[4 * t + 1].astype(F32)
        odd = r.dkvbuf[4 * t + 2].astype(F32) + r.dkvbuf[4 * t + 3].astype(F32)
        tile = jnp.where(lo, even, pltpu.roll(odd, 64, 1))
        dk_tiles.append(tile * cos + swap_halves(tile) * sin)
        dv_tiles.append(jnp.where(lo, pltpu.roll(even, 64, 1), odd))
    dk = jnp.concatenate(dk_tiles, axis=1)
    k_pre = r.kpre[...]
    k_inv = inverse_rms(k_pre)
    dgain_k = jnp.sum(dk * (k_pre * k_inv), axis=0, keepdims=True)
    r.dqkv[128:256, 0:512] = rms_back(k_pre, k_inv, dk * key_gain_row(gains)).astype(BF16)
    r.dqkv[128:256, 512:1024] = jnp.concatenate(dv_tiles, axis=1).astype(BF16)
    r.big3[me, 128:256, :] = r.dqkv[128:256, :]
    dkv_gather = line_gather_start(r.dqkv.at[kv_part], lambda i: r.big3.at[i, kv_part], r.sn2, r.rn2)
    scatter.near_out(1, 2, 3)

    def out_grad(t, _):
        at = pl.ds(pl.multiple_of(512 * t, 512), 512)
        tiles = mm_tn(r.attx[...].reshape(1024, 128), r.rows[:, :, at].reshape(1024, 512)).astype(BF16)
        for i in range(4):
            r.pieces_o[pl.ds(8 * t + 2 * i, 2)] = tiles[:, 128 * i : 128 * i + 128].reshape(2, 64, 128)
        return 0

    lax.fori_loop(0, 2, out_grad, 0)
    p_copies_o = plane_sum_send(r.pieces_o, 1, r.pin_o, r.sp1, r.rp1)
    wall_back.wait()

    def normed_back(t, _):
        for i in range(2):
            part = slice(128 * i, 128 * i + 128)
            both = mm_nt(r.dqkv[part, :], wall[pl.ds(2 * t, 2), part, :].reshape(256, 1024))
            for h in range(2):
                tile = both[:, 128 * h : 128 * h + 128]
                r.dnorm[2 * t + h] = tile if i == 0 else r.dnorm[2 * t + h] + tile
        return 0

    lax.fori_loop(0, 4, normed_back, 0)
    dnormed = jnp.concatenate([r.dnorm[t] for t in range(8)], axis=1)
    values = r.tokens[...].astype(F32)
    inv = inverse_rms(values)
    dgain_in = jnp.sum(dnormed * (values * inv), axis=0, keepdims=True)
    r.gtok[...] = r.gtok[...] + rms_back(values, inv, dnormed * gain_row(gains, 0))
    for i in range(8):
        at = slice(128 * i, 128 * i + 128)
        r.smsend[i, 0:1, :] = dgain_in[:, at]
        r.smsend[i, 1:2, :] = dgain_q[:, at]
        r.smsend[i, 2:3, :] = dgain_mid[:, at]
        half = dgain_k[:, 128 * (i // 2) : 128 * (i // 2) + 128]
        r.smsend[i, 3:4, :] = half if i % 2 == 0 else pltpu.roll(jnp.broadcast_to(half, (8, 128)), 64, 1)[0:1]
        r.smsend[i, 4:6, :] = r.stats[0:2, :]
        r.smsend[i, 6:16, :] = jnp.zeros((10, 128), F32)
    sm_copies = []
    for o in range(1, 8):
        to = lax.rem(me + o, 8)
        copy = remote(r.smsend.at[to], r.sminbox.at[o], r.sms.at[o], r.rms.at[o], (to, c, d))
        copy.start()
        sm_copies.append(copy)
    scatter.near_sum(4, 5, 0)
    shares_o = plane_sum_share(p_copies_o, r.pieces_o, 1, r.pin_o, r.res_o, r.sp2, r.rp2)

    total = r.smsend[me]
    for at, copy in enumerate(sm_copies):
        copy.wait_recv()
        total = total + r.sminbox[at + 1]
    r.smsum[...] = total
    small_copies = []
    for o in range(1, 16):
        _, device = plane_peer(o)
        copy = remote(r.smsum, r.smplane.at[o], r.sp5.at[o], r.rp5.at[o], device)
        copy.start()
        small_copies.append(copy)

    def qkv_grad(part, pieces):
        def one(t, _):
            at = pl.ds(pl.multiple_of(512 * t, 512), 512)
            tiles = mm_tn(r.nx[...].reshape(1024, 128), r.big3[:, part, at].reshape(1024, 512)).astype(BF16)
            for i in range(4):
                pieces[pl.ds(8 * t + 2 * i, 2)] = tiles[:, 128 * i : 128 * i + 128].reshape(2, 64, 128)
            return 0

        lax.fori_loop(0, 2, one, 0)

    line_gather_finish(dq_gather, lambda i: r.big3.at[i, q_part], r.sn, r.rn)
    qkv_grad(slice(0, 128), r.pieces_q)
    p_copies_q = plane_sum_send(r.pieces_q, 1, r.pin_q, r.sp3, r.rp3)
    scatter.near_sum(1, 2, 3)
    scatter.far2()
    line_gather_finish(dkv_gather, lambda i: r.big3.at[i, kv_part], r.sn2, r.rn2)
    qkv_grad(slice(128, 256), r.pieces_n)
    p_copies_n = plane_sum_send(r.pieces_n, 1, r.pin_n, r.sp6, r.rp6)
    scatter.near2()
    shares_q = plane_sum_share(p_copies_q, r.pieces_q, 1, r.pin_q, r.res_q, r.sp4, r.rp4)
    shares_n = plane_sum_share(p_copies_n, r.pieces_n, 1, r.pin_n, r.res_n, r.sp7, r.rp7)
    for at, copy in enumerate(small_copies):
        copy.wait_recv()
        total = total + r.smplane[at + 1]
    r.gsmall[...] = total
    scatter.finish(r.gw)
    for copy in shares_o + shares_q + shares_n:
        copy.wait_recv()
    scatter.drain()
    for copy in (
        pair_copies + x_copies + d_copies + sm_copies
        + small_copies + p_copies_o + p_copies_q + p_copies_n + shares_o + shares_q + shares_n
    ):
        copy.wait_send()


def layer(*args):
    vm = pl.BlockSpec(memory_space=pltpu.VMEM)
    hbm = pl.BlockSpec(memory_space=pl.ANY)
    in_hbm = ("wq", "wk", "wv", "wo", "expert_gate", "expert_up", "expert_down", "teacher")
    return pl.pallas_call(
        layer_kernel,
        out_shape=tuple(jax.ShapeDtypeStruct(shape, dtype) for _, shape, dtype in OUTPUTS + SPILLS),
        in_specs=[hbm if name in in_hbm else vm for name in INPUTS],
        out_specs=(vm,) * len(OUTPUTS) + (hbm,) * len(SPILLS),
        scratch_shapes=[pltpu.VMEM(shape, dtype) for _, shape, dtype in SCRATCH]
        + [pltpu.SemaphoreType.DMA((count,)) for _, count in SEMAPHORES],
        compiler_params=pltpu.CompilerParams(
            collective_id=0, has_side_effects=True, vmem_limit_bytes=64 << 20
        ),
        cost_estimate=pl.CostEstimate(flops=32 * 10**9, bytes_accessed=60 << 20, transcendentals=8 << 20),
        name="layer",
    )(*args)[: len(OUTPUTS)]


def finish_kernel(
    mixed, gtok, res_o_in, res_q_in, res_n_in, small_in, gw_in,
    mixed_out, loss, gtok_out, gnorm_in, gq, gk, gv, gq_gain, gk_gain, gout, gnorm_mid, grouter, ggate, gup, gdown,
    res_o, res_q, res_n, small, gw, sems,
):
    pairs = (
        (small_in, small), (res_o_in, res_o), (res_q_in, res_q), (res_n_in, res_n), (gw_in, gw),
        (mixed, mixed_out), (gtok, gtok_out),
    )
    copies = [pltpu.make_async_copy(src, dst, sems.at[i]) for i, (src, dst) in enumerate(pairs)]
    for copy in copies:
        copy.start()
    copies[0].wait()
    loss[...] = small[4:5, 0:1] / (small[5:6, 0:1] * 1024.0)
    gnorm_in[...] = small[0:1, :]
    gq_gain[...] = small[1:2, :]
    gnorm_mid[...] = small[2:3, :]
    gk_gain[...] = small[3:4, 0:64]
    grouter[...] = small[16:48, :]

    def tiles(ref, out, first, count):
        for t in range(count):
            n = 2 * (first + t)
            out[:, 128 * t : 128 * t + 128] = jnp.concatenate([ref[n], ref[n + 1]], axis=0).astype(F32)

    copies[1].wait()
    tiles(res_o, gout, 0, 8)
    copies[2].wait()
    tiles(res_q, gq, 0, 8)
    copies[3].wait()
    tiles(res_n, gk, 0, 4)
    tiles(res_n, gv, 4, 4)
    copies[4].wait()
    for e in range(4):
        ggate[:, e, :] = gw[e]
        gup[:, e, :] = gw[6 + e]
        gdown[:, e, :] = gw[4 + e + 4 * (e // 2)]
    for copy in copies[5:]:
        copy.wait()


def finish(*args):
    vm = pl.BlockSpec(memory_space=pltpu.VMEM)
    hbm = pl.BlockSpec(memory_space=pl.ANY)
    shapes = (
        (128, 1024), (1, 1), (128, 1024), (1, 128), (128, 1024), (128, 512), (128, 512), (1, 128), (1, 64), (128, 1024),
        (1, 128), (32, 128), (64, 4, 512), (64, 4, 512), (64, 4, 512),
    )
    return pl.pallas_call(
        finish_kernel,
        out_shape=tuple(jax.ShapeDtypeStruct(v, BF16 if i == 0 else F32) for i, v in enumerate(shapes)),
        in_specs=[hbm] * 7,
        out_specs=(vm,) * len(shapes),
        scratch_shapes=[
            pltpu.VMEM((16, 64, 128), BF16),
            pltpu.VMEM((16, 64, 128), BF16),
            pltpu.VMEM((16, 64, 128), BF16),
            pltpu.VMEM((48, 128), F32),
            pltpu.VMEM((12, 64, 512), F32),
            pltpu.SemaphoreType.DMA((7,)),
        ],
        compiler_params=pltpu.CompilerParams(vmem_limit_bytes=62 << 20),
        name="finish",
    )(*args)


def per_device(
    tokens,
    norm_in,
    w_query,
    w_key,
    w_value,
    query_gain,
    key_gain,
    w_out,
    norm_mid,
    w_router,
    expert_gate,
    expert_up,
    expert_down,
    routes,
    valid,
    teacher,
):
    positions = (lax.axis_index("ctx") * 2 + lax.axis_index("dp")) * 128 + jnp.arange(128, dtype=jnp.int32)
    lane = jnp.arange(128, dtype=jnp.int32)
    frequency = THETA ** (-((lane % 32).astype(F32) * (2.0 / HEAD)))
    angles = positions.astype(F32)[:, None] * frequency[None, :]
    sign = jnp.where(lane % 64 < 32, -1.0, 1.0)
    parts = layer(
        tokens, w_query, w_key, w_value, w_out, norm_in, query_gain, norm_mid, key_gain, w_router.T,
        expert_gate, expert_up, expert_down, valid, jnp.cos(angles), jnp.sin(angles) * sign, routes.T, teacher,
    )
    (
        mixed, loss, gtok, gnorm_in, gq, gk, gv, gq_gain, gk_gain, gout, gnorm_mid, grouter, ggate, gup, gdown
    ) = finish(*parts)
    return (
        mixed, loss.reshape(()), gtok, gnorm_in.reshape(128), gq, gk, gv, gq_gain.reshape(128), gk_gain.reshape(64), gout,
        gnorm_mid.reshape(128), grouter.T, ggate, gup, gdown,
    )


def solution(mesh):
    placed = (
        P(("expert", "ctx", "dp"), None),
        P("expert"),
        P("expert", None),
        P("expert", None),
        P("expert", None),
        P("expert"),
        P("expert"),
        P("expert", None),
        P("expert"),
        P("expert", None),
        P(("ctx", "dp"), "expert", None),
        P(("ctx", "dp"), "expert", None),
        P(("ctx", "dp"), "expert", None),
        P(("expert", "ctx", "dp"), None),
        P(("expert", "ctx", "dp")),
        P(("expert", "ctx", "dp"), None),
    )
    return jax.shard_map(
        per_device,
        mesh=mesh,
        in_specs=placed,
        out_specs=(
            P(("expert", "ctx", "dp"), None),
            P(),
            P(("expert", "ctx", "dp"), None),
            P("expert"),
            P("expert", None),
            P("expert", None),
            P("expert", None),
            P("expert"),
            P("expert"),
            P("expert", None),
            P("expert"),
            P("expert", None),
            P(("ctx", "dp"), "expert", None),
            P(("ctx", "dp"), "expert", None),
            P(("ctx", "dp"), "expert", None),
        ),
        check_vma=False,
    )
```
